256 devices in a mesh: seq: 32 (over y_lo, z, core), head: 8 (over y_hi, x).
Axes of the slice: x: 4, y: 4 (y_hi: 2, y_lo: 2; y = y_hi * 2 + y_lo), z: 8, core: 2. Of those that a mesh axis runs over, the one named last changes fastest.
Arguments:
- cotangent: bfloat16 [4096, 6144], P('seq', 'head'), may hold values from -0.1875 to 0.1875
- queries: bfloat16 [4096, 8192], P('seq', 'head'), may hold values from -0.5 to 0.5
- key_proj: bfloat16 [4096, 8192], P('seq', 'head'), may hold values from -0.5 to 0.5
- value_proj: bfloat16 [4096, 8192], P('seq', 'head'), may hold values from -1.5 to 1.5
- log_decay: float32 [4096, 64], P('seq', 'head'), may hold values from -0.8 to 0
- out_weight: bfloat16 [6144, 8192], P('seq', 'head'), may hold values from -0.0625 to 0.0625
Outputs:
- grad_queries: bfloat16 [4096, 8192], P('seq', 'head')
- grad_keys: bfloat16 [4096, 8192], P('seq', 'head')
- grad_values: bfloat16 [4096, 8192], P('seq', 'head')
- grad_weight: bfloat16 [6144, 8192], P('seq', 'head')
The draws below stay inside these ranges and needn't reach their ends.
All inputs are finite; a program needn't handle non-finite values.
Results may differ from the reference program's by a relative error of at most 0.03.
Values may be sent and summed in bfloat16 or wider, within the bound.
No kernel may reach another device: no remote copies, remote signals or barrier semaphores. Data moves between devices by JAX's collectives and lax.ppermute only.
A program may use at most 128 MiB of HBM per device.

```python
import math
import jax
import jax.numpy as jnp
from jax import lax

D = 6144
HEADS = 64
HEAD_DIM = 128
TOK_DEV = 128
BLOCK = 128
TOKENS = 4096
N_SEQ = 32


def draw_log_decay(key, part):
    keys_all = jax.random.split(key, 6)
    fast_share = 0.5
    chooser = jax.random.uniform(keys_all[0], (HEADS,), jnp.float32)
    is_fast = chooser < fast_share
    fast_rate = jnp.exp(jax.random.uniform(keys_all[1], (HEADS,), jnp.float32, math.log(1.0 / 50.0), math.log(1.0 / 25.0)))
    slow_rate = jnp.exp(jax.random.uniform(keys_all[2], (HEADS,), jnp.float32, math.log(0.05), math.log(0.5))) * (math.log(2.0) / TOKENS)
    base_rate = jnp.where(is_fast, fast_rate, slow_rate)
    jitter = jax.random.uniform(keys_all[3], (TOKENS, HEADS), jnp.float32, 0.5, 1.5)
    places = jax.random.randint(keys_all[4], (2, HEADS), 0, TOKENS)
    position = jnp.arange(TOKENS)[:, None]
    struck = jnp.logical_or(position == places[0][None, :], position == places[1][None, :])
    struck = jnp.logical_and(struck, jnp.logical_not(is_fast)[None, :])
    losses = jnp.log(jax.random.uniform(keys_all[5], (TOKENS, HEADS), jnp.float32, 0.5, 0.8))
    return -base_rate[None, :] * jitter + jnp.where(struck, losses, 0.0)


def raised(entries, key, source, target, shards_of, factor):
    def block_of(dim):
        return (jnp.arange(entries.shape[dim]) // (entries.shape[dim] // shards_of)).reshape((-1,) + (1,) * (entries.ndim - 1 - dim))

    one_side = jax.random.permutation(key, shards_of)[block_of(target)]
    other_side = (block_of(target) + shards_of // 2) % shards_of
    return jnp.where((block_of(source) == one_side) | (block_of(source) == other_side), factor * entries, entries)


def steps_of(rng, shape, shards, low, high):
    gain = 1.0
    for axis_at, shards_of in shards:
        draws = jax.random.uniform(jax.random.fold_in(jax.random.fold_in(rng, 6), axis_at), (shards_of,), jnp.float32, low / len(shards), high / len(shards))
        gain = gain * jnp.repeat(jnp.exp(draws), shape[axis_at] // shards_of).reshape((-1,) + (1,) * (len(shape) - 1 - axis_at))
    return gain


def normal_values(stream_key, shape, width, bound, cuts=(), kind=jnp.bfloat16):
    result = width * jax.random.normal(stream_key, shape, jnp.float32)
    if cuts:
        result = result * steps_of(stream_key, shape, cuts, -0.22, 0.18)
    return jnp.clip(result, -bound, bound).astype(kind)


def bell_draw_with(rng, extent, width, most, pieces, heavy, dtype=jnp.bfloat16):
    drawn = width * jax.random.normal(rng, extent, jnp.float32)
    if pieces:
        drawn = drawn * steps_of(rng, extent, pieces, -0.22, 0.18)
    return jnp.clip(raised(drawn, jax.random.fold_in(rng, 3), *heavy), -most, most).astype(dtype)


def setup_inputs(seed: int = 0) -> dict:
    arg_keys = jax.random.split(jax.random.key(seed), 7)
    return {
        "cotangent": bell_draw_with(arg_keys[0], (TOKENS, D), (TOKENS ** -0.5), 0.1875, ((0, 32), (1, 8)), (0, 1, 32, 2.75)),
        "queries": normal_values(arg_keys[1], (TOKENS, HEADS * HEAD_DIM), (HEAD_DIM ** -0.5), 0.5, ((0, 32), (1, 8))),
        "key_proj": normal_values(arg_keys[2], (TOKENS, HEADS * HEAD_DIM), (HEAD_DIM ** -0.5), 0.5, ((0, 32), (1, 8))),
        "value_proj": normal_values(arg_keys[3], (TOKENS, HEADS * HEAD_DIM), 0.25, 1.5, ((0, 32), (1, 8))),
        "log_decay": draw_log_decay(jax.random.fold_in(arg_keys[6], 71), 0),
        "out_weight": normal_values(arg_keys[5], (D, HEADS * HEAD_DIM), (HEADS * HEAD_DIM) ** -0.5, 0.0625, ((0, 32), (1, 8))),
    }


def advance(running, element):
    factor, addend = element
    return jnp.exp(factor)[:, None, None] * running + addend, running


def reference(cotangent, queries, key_proj, value_proj, log_decay, out_weight):
    grad_attn = jnp.dot(cotangent, out_weight, preferred_element_type=jnp.float32).astype(jnp.bfloat16)
    block_count = TOKENS // BLOCK
    block_shape = (block_count, BLOCK, HEADS, HEAD_DIM)
    query_blk = queries.reshape(block_shape).astype(jnp.float32)
    key_blk = key_proj.reshape(block_shape).astype(jnp.float32)
    value_blk = value_proj.reshape(block_shape).astype(jnp.float32)
    grad_blk = grad_attn.reshape(block_shape).astype(jnp.float32)
    decays = log_decay.reshape(block_count, BLOCK, HEADS)
    within = jnp.cumsum(decays, axis=1)
    block_decay = within[:, -1, :]
    key_weight = jnp.exp(block_decay[:, None, :] - within)
    query_weight = jnp.exp(within)
    key_scaled = (key_weight[..., None] * key_blk).astype(jnp.bfloat16).astype(jnp.float32)
    key_terms = jnp.einsum('nbhe,nbhf->nhef', key_scaled, value_blk)
    zero_state = jnp.zeros((HEADS, HEAD_DIM, HEAD_DIM), jnp.float32)
    _, states_before = lax.scan(advance, zero_state, (block_decay, key_terms))
    query_scaled = (query_weight[..., None] * query_blk).astype(jnp.bfloat16).astype(jnp.float32)
    query_terms = jnp.einsum('nbhe,nbhf->nhef', query_scaled, grad_blk)
    _, states_after = lax.scan(advance, zero_state, (block_decay, query_terms), reverse=True)
    states_low = states_before.astype(jnp.bfloat16).astype(jnp.float32)
    after_low = states_after.astype(jnp.bfloat16).astype(jnp.float32)
    within_heads = jnp.transpose(within, (0, 2, 1))
    gaps = within_heads[:, :, :, None] - within_heads[:, :, None, :]
    causal = jnp.arange(BLOCK)[:, None] >= jnp.arange(BLOCK)[None, :]
    mask = jnp.exp(jnp.where(causal[None, None], gaps, -jnp.inf))
    scores = (jnp.einsum('nthe,nshe->nhts', query_blk, key_blk) * mask).astype(jnp.bfloat16).astype(jnp.float32)
    attended = query_weight[..., None] * jnp.einsum('nthe,nhef->nthf', query_blk, states_low)
    attended = attended + jnp.einsum('nhts,nshf->nthf', scores, value_blk)
    attended = attended.astype(jnp.bfloat16)
    grad_scores = (jnp.einsum('nthf,nshf->nhts', grad_blk, value_blk) * mask).astype(jnp.bfloat16).astype(jnp.float32)
    grad_queries = query_weight[..., None] * jnp.einsum('nthf,nhef->nthe', grad_blk, states_low)
    grad_queries = grad_queries + jnp.einsum('nhts,nshe->nthe', grad_scores, key_blk)
    grad_keys = key_weight[..., None] * jnp.einsum('nshf,nhef->nshe', value_blk, after_low)
    grad_keys = grad_keys + jnp.einsum('nhts,nthe->nshe', grad_scores, query_blk)
    grad_values = key_weight[..., None] * jnp.einsum('nshe,nhef->nshf', key_blk, after_low)
    grad_values = grad_values + jnp.einsum('nhts,nthf->nshf', scores, grad_blk)
    col_count = HEADS * HEAD_DIM
    attended_rows = attended.reshape(N_SEQ, TOK_DEV, col_count)
    cot_rows = cotangent.reshape(N_SEQ, TOK_DEV, D)

    def add_group(running, element):
        cot_group, att_group = element
        partial_value = jnp.dot(cot_group.T, att_group, preferred_element_type=jnp.float32)
        rounded = lax.optimization_barrier(partial_value.astype(jnp.bfloat16))
        return running + rounded.astype(jnp.float32), None

    summed, _ = lax.scan(add_group, jnp.zeros((D, col_count), jnp.float32), (cot_rows, attended_rows))
    return (grad_queries.reshape(TOKENS, col_count).astype(jnp.bfloat16),
            grad_keys.reshape(TOKENS, col_count).astype(jnp.bfloat16),
            grad_values.reshape(TOKENS, col_count).astype(jnp.bfloat16),
            summed.astype(jnp.bfloat16))
```

```python
import functools

import jax
import jax.numpy as jnp
from jax import lax
from jax.experimental import pallas as pl
from jax.experimental.pallas import tpu as pltpu
from jax.sharding import PartitionSpec as P

HEAD_DIM = 128
BLOCK = 128
HEADS_LOCAL = 8
N_SEQ = 32
ROWS = 32
NZ = 8
BF = jnp.bfloat16
F32 = jnp.float32
AXES = ("seq", "head")
PARAMS = pltpu.CompilerParams(vmem_limit_bytes=48 * 1024 * 1024)


def pairs(move):
    out = []
    for yl in range(2):
        for z in range(8):
            for c in range(2):
                for yh in range(2):
                    for x in range(4):
                        a, b, d, e, f = move(yl, z, c, yh, x)
                        out.append(
                            (
                                (yl * 16 + z * 2 + c) * 8 + yh * 4 + x,
                                (a * 16 + (b % 8) * 2 + d) * 8 + e * 4 + f % 4,
                            )
                        )
    return out


Z_UP = pairs(lambda yl, z, c, yh, x: (yl, z + 1, c, yh, x))
Z_DOWN = pairs(lambda yl, z, c, yh, x: (yl, z + 7, c, yh, x))
X_UP = pairs(lambda yl, z, c, yh, x: (yl, z, c, yh, x + 1))
X_DOWN = pairs(lambda yl, z, c, yh, x: (yl, z, c, yh, x + 3))
CORE = pairs(lambda yl, z, c, yh, x: (yl, z, 1 - c, yh, x))
Y_LO = pairs(lambda yl, z, c, yh, x: (1 - yl, z, c, yh, x))


def send(array, table):
    return lax.ppermute(array, AXES, table)


def mm(a, b, ca, cb):
    return lax.dot_general(a, b, (((ca,), (cb,)), ((), ())), preferred_element_type=F32)


def within_columns(decay):
    at = lax.broadcasted_iota(jnp.int32, (BLOCK, BLOCK), 0)
    of = lax.broadcasted_iota(jnp.int32, (BLOCK, BLOCK), 1)
    lower = (of <= at).astype(F32)
    return lax.dot_general(
        lower, decay, (((1,), (0,)), ((), ())),
        precision=lax.Precision.HIGHEST, preferred_element_type=F32,
    )


def causal_mask(within_col):
    gaps = within_col - jnp.transpose(within_col)
    at = lax.broadcasted_iota(jnp.int32, (BLOCK, BLOCK), 0)
    of = lax.broadcasted_iota(jnp.int32, (BLOCK, BLOCK), 1)
    return jnp.exp(jnp.where(at >= of, gaps, -jnp.inf))


def head_cols(h):
    return pl.ds(h * HEAD_DIM, HEAD_DIM)


def key_terms_kernel(decay_ref, key_ref, value_ref, out_ref):
    within = within_columns(decay_ref[...])
    row = lax.broadcasted_iota(jnp.int32, (16, HEAD_DIM), 0)
    for h in range(HEADS_LOCAL):
        col = within[:, h : h + 1]
        last = within[BLOCK - 1 : BLOCK, h : h + 1]
        scaled = (jnp.exp(last - col) * key_ref[:, head_cols(h)].astype(F32)).astype(BF)
        terms = mm(scaled, value_ref[:, head_cols(h)], 0, 0).astype(BF)
        high = last.astype(BF).astype(F32)
        middle = (last - high).astype(BF).astype(F32)
        low = last - high - middle
        parts = jnp.where(row == 0, high, jnp.where(row == 1, middle, jnp.where(row == 2, low, 0.0)))
        parts = parts.astype(BF)
        for i in range(4):
            out_ref[4 * h + i, 0:ROWS, :] = terms[i * ROWS : (i + 1) * ROWS]
            out_ref[4 * h + i, ROWS : ROWS + 16, :] = parts


def recurrence_kernel(reverse, decay_ref, terms_ref, out_ref):
    state = jnp.zeros((ROWS, HEAD_DIM), F32)
    for k in reversed(range(N_SEQ)) if reverse else range(N_SEQ):
        out_ref[k] = state.astype(BF)
        parts = decay_ref[k, ROWS : ROWS + 16, :].astype(F32)
        factor = jnp.exp(parts[0:1] + (parts[1:2] + parts[2:3]))
        state = factor * state + terms_ref[k, 0:ROWS, :].astype(F32)


def attended_kernel(decay_ref, query_ref, key_ref, value_ref, state_ref, att_ref, score_ref):
    within = within_columns(decay_ref[...])
    for h in range(HEADS_LOCAL):
        cols = head_cols(h)
        col = within[:, h : h + 1]
        query = query_ref[:, cols]
        scores = (mm(query, key_ref[:, cols], 1, 1) * causal_mask(col)).astype(BF)
        score_ref[:, cols] = scores
        att = jnp.exp(col) * mm(query, state_ref[pl.ds(h * HEAD_DIM, HEAD_DIM), :], 1, 0)
        att_ref[:, cols] = (att + mm(scores, value_ref[:, cols], 1, 0)).astype(BF)


def query_terms_kernel(decay_ref, query_ref, own_ref, other_ref, grad_ref, out_ref):
    within = within_columns(decay_ref[...])
    for h in range(HEADS_LOCAL):
        cols = head_cols(h)
        grad = (own_ref[:, cols] + other_ref[:, cols].astype(F32)).astype(BF)
        grad_ref[:, cols] = grad
        scaled = (jnp.exp(within[:, h : h + 1]) * query_ref[:, cols].astype(F32)).astype(BF)
        terms = mm(scaled, grad, 0, 0).astype(BF)
        for i in range(4):
            out_ref[4 * h + i] = terms[i * ROWS : (i + 1) * ROWS]


def grads_kernel(
    decay_ref, query_ref, key_ref, value_ref, grad_ref, score_ref, state_ref, after_ref,
    gq_ref, gk_ref, gv_ref,
):
    within = within_columns(decay_ref[...])
    for h in range(HEADS_LOCAL):
        cols = head_cols(h)
        rows = pl.ds(h * HEAD_DIM, HEAD_DIM)
        col = within[:, h : h + 1]
        last = within[BLOCK - 1 : BLOCK, h : h + 1]
        key_weight = jnp.exp(last - col)
        grad, key, value = grad_ref[:, cols], key_ref[:, cols], value_ref[:, cols]
        after = after_ref[rows, :]
        grad_scores = (mm(grad, value, 1, 1) * causal_mask(col)).astype(BF)
        gq = jnp.exp(col) * mm(grad, state_ref[rows, :], 1, 1) + mm(grad_scores, key, 1, 0)
        gq_ref[:, cols] = gq.astype(BF)
        gk = key_weight * mm(value, after, 1, 1) + mm(grad_scores, query_ref[:, cols], 0, 0)
        gk_ref[:, cols] = gk.astype(BF)
        gv = key_weight * mm(key, after, 1, 0) + mm(score_ref[:, cols], grad, 0, 0)
        gv_ref[:, cols] = gv.astype(BF)


def kernel_call(body, outs, name, flops, moved):
    return pl.pallas_call(
        body,
        out_shape=outs,
        compiler_params=PARAMS,
        name=name,
        cost_estimate=pl.CostEstimate(flops=flops, bytes_accessed=moved, transcendentals=0),
    )


def shape(dims, dtype=BF):
    return jax.ShapeDtypeStruct(dims, dtype)


def exchange(array):
    return lax.all_to_all(array, "seq", 0, 0, tiled=True)


def body(cotangent, queries, key_proj, value_proj, log_decay, out_weight):
    tokens, cols = queries.shape
    seq, head = lax.axis_index("seq"), lax.axis_index("head")
    core, z = seq % 2, (seq // 2) % 8
    y_lo, y_hi, x = seq // 16, head // 4, head % 4
    flip = y_lo ^ y_hi
    share = out_weight.shape[0]

    up, down = send(out_weight, Z_UP), send(out_weight, Z_DOWN)
    below, above = [up], [down]
    for _ in range(2):
        below.append(send(below[-1], Z_UP))
        above.append(send(above[-1], Z_DOWN))
    half = share // 2
    far_low = send(below[-1][:half], Z_UP)
    far_high = send(above[-1][half:], Z_DOWN)
    weights = jnp.concatenate(
        [out_weight] + above + [far_low, far_high] + below[::-1], axis=0
    )

    cot = jnp.transpose(cotangent).reshape(2, 2, share, tokens)
    pieces = []
    for a in range(2):
        part = lax.dynamic_index_in_dim(cot, core ^ a, 1, keepdims=False).reshape(2 * share, tokens)
        for b in range(2):
            table = pairs(lambda yl, z, c, yh, x, a=a, b=b: (yh, z, c ^ a, yl ^ b, x))
            pieces.append(send(part, table))
    own = jnp.concatenate(pieces, axis=1)
    left, right = send(own, X_UP), send(own, X_DOWN)
    opposite = jnp.concatenate([send(left[:share], X_UP), send(right[share:], X_DOWN)], axis=0)
    around = [own, right, opposite, left]
    block = jnp.concatenate(around + around, axis=0)
    start = ((z - 2 * x) % NZ) * share
    block = lax.dynamic_slice_in_dim(block, start, NZ * share, axis=0)

    terms = kernel_call(
        key_terms_kernel, shape((N_SEQ, ROWS + 16, HEAD_DIM)), "key_terms", 40_000_000, 1_000_000
    )(log_decay, key_proj, value_proj)
    gathered = exchange(terms)
    befores = kernel_call(
        functools.partial(recurrence_kernel, False),
        shape((N_SEQ, ROWS, HEAD_DIM)), "states_before", 1_000_000, 1_000_000,
    )(gathered, gathered)
    states = exchange(befores).reshape(cols, HEAD_DIM)
    attended, scores = kernel_call(
        attended_kernel, (shape((tokens, cols)), shape((tokens, cols))), "attended",
        110_000_000, 2_000_000,
    )(log_decay, queries, key_proj, value_proj, states)

    def project(part):
        return lax.dot_general(part, weights, (((0,), (0,)), ((), ())), preferred_element_type=F32)

    crossing = send(project(block[:, 2 * tokens :]).astype(BF), CORE)
    summed = project(block[:, : 2 * tokens]) + crossing.astype(F32)
    mine = lax.dynamic_slice_in_dim(summed, flip * tokens, tokens, axis=0)
    theirs = lax.dynamic_slice_in_dim(summed, (1 - flip) * tokens, tokens, axis=0)
    arrived = send(theirs.astype(BF), Y_LO)
    grad_attn, query_terms = kernel_call(
        query_terms_kernel, (shape((tokens, cols)), shape((N_SEQ, ROWS, HEAD_DIM))), "query_terms",
        40_000_000, 1_000_000,
    )(log_decay, queries, mine, arrived)

    neighbour = send(attended, Y_LO)
    pair = jnp.where(
        flip == 0,
        jnp.concatenate([attended, neighbour], axis=0),
        jnp.concatenate([neighbour, attended], axis=0),
    )
    all_attended = jnp.concatenate([pair, send(pair, CORE)], axis=0)
    partial = lax.dot_general(
        block, all_attended, (((1,), (0,)), ((), ())), preferred_element_type=F32
    ).astype(BF)
    part = partial.reshape(NZ, share, cols)
    going_up = send(part[4, :half], Z_UP)
    going_down = send(part[4, half:], Z_DOWN)
    going_up = jnp.concatenate(
        [(part[3, :half].astype(F32) + going_up.astype(F32)).astype(BF), part[3, half:]], axis=0
    )
    going_down = jnp.concatenate(
        [part[5, :half], (part[5, half:].astype(F32) + going_down.astype(F32)).astype(BF)], axis=0
    )
    for k in (2, 1):
        going_up = (part[k].astype(F32) + send(going_up, Z_UP).astype(F32)).astype(BF)
        going_down = (part[8 - k].astype(F32) + send(going_down, Z_DOWN).astype(F32)).astype(BF)
    grad_weight = (
        part[0].astype(F32)
        + send(going_up, Z_UP).astype(F32)
        + send(going_down, Z_DOWN).astype(F32)
    ).astype(BF)

    afters = kernel_call(
        functools.partial(recurrence_kernel, True),
        shape((N_SEQ, ROWS, HEAD_DIM)), "states_after", 1_000_000, 1_000_000,
    )(gathered, exchange(query_terms))
    after = exchange(afters).reshape(cols, HEAD_DIM)
    grad_queries, grad_keys, grad_values = kernel_call(
        grads_kernel, (shape((tokens, cols)),) * 3, "grads", 270_000_000, 3_000_000
    )(log_decay, queries, key_proj, value_proj, grad_attn, scores, states, after)
    return grad_queries, grad_keys, grad_values, grad_weight


def solution(mesh):
    placed = P("seq", "head")
    return jax.shard_map(
        body,
        mesh=mesh,
        in_specs=(placed,) * 6,
        out_specs=(placed,) * 4,
        check_vma=False,
    )
```

```python
import functools

import jax
import jax.numpy as jnp
from jax import lax
from jax.experimental import pallas as pl
from jax.experimental.pallas import tpu as pltpu
from jax.sharding import PartitionSpec as P

HEAD_DIM = 128
BLOCK = 128
HEADS_LOCAL = 8
N_SEQ = 32
ROWS = 32
NZ = 8
BF = jnp.bfloat16
F32 = jnp.float32
AXES = ("seq", "head")
PARAMS = pltpu.CompilerParams(vmem_limit_bytes=48 * 1024 * 1024)


def pairs(move):
    out = []
    for yl in range(2):
        for z in range(8):
            for c in range(2):
                for yh in range(2):
                    for x in range(4):
                        a, b, d, e, f = move(yl, z, c, yh, x)
                        out.append(
                            (
                                (yl * 16 + z * 2 + c) * 8 + yh * 4 + x,
                                (a * 16 + (b % 8) * 2 + d) * 8 + e * 4 + f % 4,
                            )
                        )
    return out


Z_GROUPS = [[yl * 16 + z * 2 + c for z in range(NZ)] for yl in range(2) for c in range(2)]
X_UP = pairs(lambda yl, z, c, yh, x: (yl, z, c, yh, x + 1))
X_DOWN = pairs(lambda yl, z, c, yh, x: (yl, z, c, yh, x + 3))
CORE = pairs(lambda yl, z, c, yh, x: (yl, z, 1 - c, yh, x))
Y_LO = pairs(lambda yl, z, c, yh, x: (1 - yl, z, c, yh, x))


def send(array, table):
    return lax.ppermute(array, AXES, table)


def mm(a, b, ca, cb):
    return lax.dot_general(a, b, (((ca,), (cb,)), ((), ())), preferred_element_type=F32)


def within_columns(decay):
    at = lax.broadcasted_iota(jnp.int32, (BLOCK, BLOCK), 0)
    of = lax.broadcasted_iota(jnp.int32, (BLOCK, BLOCK), 1)
    lower = (of <= at).astype(F32)
    return lax.dot_general(
        lower, decay, (((1,), (0,)), ((), ())),
        precision=lax.Precision.HIGHEST, preferred_element_type=F32,
    )


def causal_mask(within_col):
    gaps = within_col - jnp.transpose(within_col)
    at = lax.broadcasted_iota(jnp.int32, (BLOCK, BLOCK), 0)
    of = lax.broadcasted_iota(jnp.int32, (BLOCK, BLOCK), 1)
    return jnp.exp(jnp.where(at >= of, gaps, -jnp.inf))


def head_cols(h):
    return pl.ds(h * HEAD_DIM, HEAD_DIM)


def key_terms_kernel(decay_ref, key_ref, value_ref, out_ref):
    within = within_columns(decay_ref[...])
    row = lax.broadcasted_iota(jnp.int32, (16, HEAD_DIM), 0)
    for h in range(HEADS_LOCAL):
        col = within[:, h : h + 1]
        last = within[BLOCK - 1 : BLOCK, h : h + 1]
        scaled = (jnp.exp(last - col) * key_ref[:, head_cols(h)].astype(F32)).astype(BF)
        terms = mm(scaled, value_ref[:, head_cols(h)], 0, 0).astype(BF)
        high = last.astype(BF).astype(F32)
        middle = (last - high).astype(BF).astype(F32)
        low = last - high - middle
        parts = jnp.where(row == 0, high, jnp.where(row == 1, middle, jnp.where(row == 2, low, 0.0)))
        parts = parts.astype(BF)
        for i in range(4):
            out_ref[4 * h + i, 0:ROWS, :] = terms[i * ROWS : (i + 1) * ROWS]
            out_ref[4 * h + i, ROWS : ROWS + 16, :] = parts


def recurrence_kernel(reverse, decay_ref, terms_ref, out_ref):
    state = jnp.zeros((ROWS, HEAD_DIM), F32)
    for k in reversed(range(N_SEQ)) if reverse else range(N_SEQ):
        out_ref[k] = state.astype(BF)
        parts = decay_ref[k, ROWS : ROWS + 16, :].astype(F32)
        factor = jnp.exp(parts[0:1] + (parts[1:2] + parts[2:3]))
        state = factor * state + terms_ref[k, 0:ROWS, :].astype(F32)


def attended_kernel(decay_ref, query_ref, key_ref, value_ref, state_ref, att_ref, score_ref):
    within = within_columns(decay_ref[...])
    for h in range(HEADS_LOCAL):
        cols = head_cols(h)
        col = within[:, h : h + 1]
        query = query_ref[:, cols]
        scores = (mm(query, key_ref[:, cols], 1, 1) * causal_mask(col)).astype(BF)
        score_ref[:, cols] = scores
        att = jnp.exp(col) * mm(query, state_ref[pl.ds(h * HEAD_DIM, HEAD_DIM), :], 1, 0)
        att_ref[:, cols] = (att + mm(scores, value_ref[:, cols], 1, 0)).astype(BF)


def query_terms_kernel(decay_ref, query_ref, own_ref, other_ref, grad_ref, out_ref):
    within = within_columns(decay_ref[...])
    for h in range(HEADS_LOCAL):
        cols = head_cols(h)
        grad = (own_ref[:, cols] + other_ref[:, cols].astype(F32)).astype(BF)
        grad_ref[:, cols] = grad
        scaled = (jnp.exp(within[:, h : h + 1]) * query_ref[:, cols].astype(F32)).astype(BF)
        terms = mm(scaled, grad, 0, 0).astype(BF)
        for i in range(4):
            out_ref[4 * h + i] = terms[i * ROWS : (i + 1) * ROWS]


def grads_kernel(
    decay_ref, query_ref, key_ref, value_ref, grad_ref, score_ref, state_ref, after_ref,
    gq_ref, gk_ref, gv_ref,
):
    within = within_columns(decay_ref[...])
    for h in range(HEADS_LOCAL):
        cols = head_cols(h)
        rows = pl.ds(h * HEAD_DIM, HEAD_DIM)
        col = within[:, h : h + 1]
        last = within[BLOCK - 1 : BLOCK, h : h + 1]
        key_weight = jnp.exp(last - col)
        grad, key, value = grad_ref[:, cols], key_ref[:, cols], value_ref[:, cols]
        after = after_ref[rows, :]
        grad_scores = (mm(grad, value, 1, 1) * causal_mask(col)).astype(BF)
        gq = jnp.exp(col) * mm(grad, state_ref[rows, :], 1, 1) + mm(grad_scores, key, 1, 0)
        gq_ref[:, cols] = gq.astype(BF)
        gk = key_weight * mm(value, after, 1, 1) + mm(grad_scores, query_ref[:, cols], 0, 0)
        gk_ref[:, cols] = gk.astype(BF)
        gv = key_weight * mm(key, after, 1, 0) + mm(score_ref[:, cols], grad, 0, 0)
        gv_ref[:, cols] = gv.astype(BF)


def flip_bit():
    return (lax.axis_index("seq") // 16) ^ (lax.axis_index("head") // 4)


def assemble_kernel(share, own_ref, left_ref, right_ref, low_ref, high_ref, out_ref, out_t_ref):
    x = lax.axis_index("head") % 4
    features = NZ * share
    for off, ref, start, count in (
        (0, own_ref, 0, 2 * share),
        (1, right_ref, 0, 2 * share),
        (2, low_ref, 0, share),
        (2, high_ref, share, share),
        (3, left_ref, 0, 2 * share),
    ):
        at = pl.multiple_of(((x + off) % 4) * (2 * share) + start, 64)
        out_ref[pl.ds(at, count), :] = ref[...]
    for i in range(features // 256):
        rows = pl.ds(i * 256, 256)
        out_t_ref[:, rows] = jnp.transpose(out_ref[rows, :])


def project_kernel(block_ref, weight_ref, kept_ref, crossing_ref):
    half = kept_ref.shape[0]
    crossing_ref[...] = mm(block_ref[half:, :], weight_ref[...], 1, 0).astype(BF)
    kept_ref[...] = mm(block_ref[:half, :], weight_ref[...], 1, 0)


def weight_kernel(block_ref, own_ref, neighbour_ref, across_ref, diagonal_ref, out_ref, tokens_ref):
    flip = flip_bit()
    for i, ref in ((flip, own_ref), (1 - flip, neighbour_ref), (2 + flip, across_ref), (3 - flip, diagonal_ref)):
        tokens_ref[pl.ds(pl.multiple_of(i * BLOCK, BLOCK), BLOCK), :] = ref[...]
    out_ref[...] = mm(block_ref[...], tokens_ref[...], 1, 0).astype(BF)


def kernel_call(body, outs, name, flops, moved):
    return pl.pallas_call(
        body,
        out_shape=outs,
        compiler_params=PARAMS,
        name=name,
        cost_estimate=pl.CostEstimate(flops=flops, bytes_accessed=moved, transcendentals=0),
    )


def shape(dims, dtype=BF):
    return jax.ShapeDtypeStruct(dims, dtype)


def exchange(array):
    return lax.all_to_all(array, "seq", 0, 0, tiled=True)


def body(cotangent, queries, key_proj, value_proj, log_decay, out_weight):
    tokens, cols = queries.shape
    core = lax.axis_index("seq") % 2
    flip = flip_bit()
    share = out_weight.shape[0]

    weights = lax.all_gather(
        out_weight, "seq", axis=0, tiled=True, axis_index_groups=Z_GROUPS
    )

    cot = jnp.transpose(cotangent).reshape(2, 2, share, tokens)
    pieces = []
    for a in range(2):
        part = lax.dynamic_index_in_dim(cot, core ^ a, 1, keepdims=False).reshape(2 * share, tokens)
        for b in range(2):
            table = pairs(lambda yl, z, c, yh, x, a=a, b=b: (yh, z, c ^ a, yl ^ b, x))
            pieces.append(send(part, table))
    own = jnp.concatenate(pieces, axis=1)
    left, right = send(own, X_UP), send(own, X_DOWN)
    opposite_low = send(left[:share], X_UP)
    opposite_high = send(right[share:], X_DOWN)
    features = NZ * share
    block, block_t = kernel_call(
        functools.partial(assemble_kernel, share),
        (shape((features, 4 * tokens)), shape((4 * tokens, features))), "assemble",
        1_000_000, 5_000_000,
    )(own, left, right, opposite_low, opposite_high)

    terms = kernel_call(
        key_terms_kernel, shape((N_SEQ, ROWS + 16, HEAD_DIM)), "key_terms", 40_000_000, 1_000_000
    )(log_decay, key_proj, value_proj)
    gathered = exchange(terms)
    befores = kernel_call(
        functools.partial(recurrence_kernel, False),
        shape((N_SEQ, ROWS, HEAD_DIM)), "states_before", 1_000_000, 1_000_000,
    )(gathered, gathered)
    states = exchange(befores).reshape(cols, HEAD_DIM)
    attended, scores = kernel_call(
        attended_kernel, (shape((tokens, cols)), shape((tokens, cols))), "attended",
        110_000_000, 2_000_000,
    )(log_decay, queries, key_proj, value_proj, states)

    kept, crossing = pl.pallas_call(
        project_kernel,
        grid=(4,),
        in_specs=[
            pl.BlockSpec((4 * tokens, features), lambda i: (0, 0)),
            pl.BlockSpec((features, cols // 4), lambda i: (0, i)),
        ],
        out_specs=(pl.BlockSpec((2 * tokens, cols // 4), lambda i: (0, i)),) * 2,
        out_shape=(shape((2 * tokens, cols), F32), shape((2 * tokens, cols))),
        compiler_params=PARAMS,
        name="project",
        cost_estimate=pl.CostEstimate(
            flops=1_600_000_000, bytes_accessed=6_000_000, transcendentals=0
        ),
    )(block_t, weights)
    summed = kept + send(crossing, CORE).astype(F32)
    mine = lax.dynamic_slice_in_dim(summed, flip * tokens, tokens, axis=0)
    theirs = lax.dynamic_slice_in_dim(summed, (1 - flip) * tokens, tokens, axis=0)
    arrived = send(theirs.astype(BF), Y_LO)
    grad_attn, query_terms = kernel_call(
        query_terms_kernel, (shape((tokens, cols)), shape((N_SEQ, ROWS, HEAD_DIM))), "query_terms",
        40_000_000, 1_000_000,
    )(log_decay, queries, mine, arrived)

    across = send(attended, CORE)
    neighbour = send(attended, Y_LO)
    diagonal = send(neighbour, CORE)
    column_spec = pl.BlockSpec((tokens, cols // 4), lambda i: (0, i))
    partial = pl.pallas_call(
        weight_kernel,
        grid=(4,),
        in_specs=[pl.BlockSpec((features, 4 * tokens), lambda i: (0, 0))] + [column_spec] * 4,
        out_specs=pl.BlockSpec((features, cols // 4), lambda i: (0, i)),
        out_shape=shape((features, cols)),
        scratch_shapes=[pltpu.VMEM((4 * tokens, cols // 4), BF)],
        compiler_params=PARAMS,
        name="weight_partial",
        cost_estimate=pl.CostEstimate(
            flops=1_600_000_000, bytes_accessed=6_000_000, transcendentals=0
        ),
    )(block, attended, neighbour, across, diagonal)
    grad_weight = lax.psum_scatter(
        partial, "seq", scatter_dimension=0, tiled=True, axis_index_groups=Z_GROUPS
    )

    afters = kernel_call(
        functools.partial(recurrence_kernel, True),
        shape((N_SEQ, ROWS, HEAD_DIM)), "states_after", 1_000_000, 1_000_000,
    )(gathered, exchange(query_terms))
    after = exchange(afters).reshape(cols, HEAD_DIM)
    grad_queries, grad_keys, grad_values = kernel_call(
        grads_kernel, (shape((tokens, cols)),) * 3, "grads", 270_000_000, 3_000_000
    )(log_decay, queries, key_proj, value_proj, grad_attn, scores, states, after)
    return grad_queries, grad_keys, grad_values, grad_weight


def solution(mesh):
    placed = P("seq", "head")
    return jax.shard_map(
        body,
        mesh=mesh,
        in_specs=(placed,) * 6,
        out_specs=(placed,) * 4,
        check_vma=False,
    )
```

```python
import functools

import jax
import jax.numpy as jnp
from jax import lax
from jax.experimental import pallas as pl
from jax.experimental.pallas import tpu as pltpu
from jax.sharding import PartitionSpec as P

HEAD_DIM = 128
BLOCK = 128
HEADS_LOCAL = 8
N_SEQ = 32
ROWS = 32
NZ = 8
TILES = 4
BF = jnp.bfloat16
F32 = jnp.float32
AXES = ("seq", "head")
PARAMS = pltpu.CompilerParams(vmem_limit_bytes=48 * 1024 * 1024)


def pairs(move):
    out = []
    for yl in range(2):
        for z in range(8):
            for c in range(2):
                for yh in range(2):
                    for x in range(4):
                        a, b, d, e, f = move(yl, z, c, yh, x)
                        out.append(
                            (
                                (yl * 16 + z * 2 + c) * 8 + yh * 4 + x,
                                (a * 16 + (b % 8) * 2 + d) * 8 + e * 4 + f % 4,
                            )
                        )
    return out


Z_UP = pairs(lambda yl, z, c, yh, x: (yl, z + 1, c, yh, x))
Z_DOWN = pairs(lambda yl, z, c, yh, x: (yl, z + 7, c, yh, x))
X_UP = pairs(lambda yl, z, c, yh, x: (yl, z, c, yh, x + 1))
X_DOWN = pairs(lambda yl, z, c, yh, x: (yl, z, c, yh, x + 3))
CORE = pairs(lambda yl, z, c, yh, x: (yl, z, 1 - c, yh, x))
Y_LO = pairs(lambda yl, z, c, yh, x: (1 - yl, z, c, yh, x))


def send(array, table):
    return lax.ppermute(array, AXES, table)


def mm(a, b, ca, cb):
    return lax.dot_general(a, b, (((ca,), (cb,)), ((), ())), preferred_element_type=F32)


def coordinates():
    seq, head = lax.axis_index("seq"), lax.axis_index("head")
    y_lo = seq // 16
    rest = seq - 16 * y_lo
    z = rest // 2
    core = rest - 2 * z
    y_hi = head // 4
    return y_lo, z, core, y_hi, head - 4 * y_hi


def flip_bit():
    y_lo, _, _, y_hi, _ = coordinates()
    return y_lo + y_hi - 2 * y_lo * y_hi


def within_columns(decay):
    at = lax.broadcasted_iota(jnp.int32, (BLOCK, BLOCK), 0)
    of = lax.broadcasted_iota(jnp.int32, (BLOCK, BLOCK), 1)
    lower = (of <= at).astype(F32)
    return lax.dot_general(
        lower, decay, (((1,), (0,)), ((), ())),
        precision=lax.Precision.HIGHEST, preferred_element_type=F32,
    )


def causal_mask(within_col):
    gaps = within_col - jnp.transpose(within_col)
    at = lax.broadcasted_iota(jnp.int32, (BLOCK, BLOCK), 0)
    of = lax.broadcasted_iota(jnp.int32, (BLOCK, BLOCK), 1)
    return jnp.exp(jnp.where(at >= of, gaps, -jnp.inf))


def head_cols(h):
    return pl.ds(h * HEAD_DIM, HEAD_DIM)


def cotangent_kernel(cot_ref, same_ref, swap_ref):
    _, _, core, _, _ = coordinates()
    turned = jnp.transpose(cot_ref[...])
    share = turned.shape[0] // 4
    for i in range(2):
        first = turned[(2 * i) * share : (2 * i + 1) * share]
        second = turned[(2 * i + 1) * share : (2 * i + 2) * share]
        rows = pl.ds(i * share, share)

        @pl.when(core == 0)
        def _():
            same_ref[rows, :] = first
            swap_ref[rows, :] = second

        @pl.when(core == 1)
        def _():
            same_ref[rows, :] = second
            swap_ref[rows, :] = first


def key_terms_kernel(decay_ref, key_ref, value_ref, out_ref):
    within = within_columns(decay_ref[...])
    row = lax.broadcasted_iota(jnp.int32, (16, HEAD_DIM), 0)
    for h in range(HEADS_LOCAL):
        col = within[:, h : h + 1]
        last = within[BLOCK - 1 : BLOCK, h : h + 1]
        scaled = (jnp.exp(last - col) * key_ref[:, head_cols(h)].astype(F32)).astype(BF)
        terms = mm(scaled, value_ref[:, head_cols(h)], 0, 0).astype(BF)
        high = last.astype(BF).astype(F32)
        middle = (last - high).astype(BF).astype(F32)
        low = last - high - middle
        parts = jnp.where(row == 0, high, jnp.where(row == 1, middle, jnp.where(row == 2, low, 0.0)))
        parts = parts.astype(BF)
        for i in range(4):
            out_ref[4 * h + i, 0:ROWS, :] = terms[i * ROWS : (i + 1) * ROWS]
            out_ref[4 * h + i, ROWS : ROWS + 16, :] = parts


def recurrence_kernel(reverse, decay_ref, terms_ref, *rest):
    out_ref = rest[-1]
    state = jnp.zeros((ROWS, HEAD_DIM), F32)
    for k in reversed(range(N_SEQ)) if reverse else range(N_SEQ):
        out_ref[k] = state.astype(BF)
        parts = decay_ref[k, ROWS : ROWS + 16, :].astype(F32)
        factor = jnp.exp(parts[0:1] + (parts[1:2] + parts[2:3]))
        state = factor * state + terms_ref[k, 0:ROWS, :].astype(F32)


def attended_kernel(decay_ref, query_ref, key_ref, value_ref, state_ref, *rest):
    att_ref, score_ref = rest[-2:]
    within = within_columns(decay_ref[...])
    for h in range(HEADS_LOCAL):
        cols = head_cols(h)
        col = within[:, h : h + 1]
        query = query_ref[:, cols]
        scores = (mm(query, key_ref[:, cols], 1, 1) * causal_mask(col)).astype(BF)
        score_ref[:, cols] = scores
        att = jnp.exp(col) * mm(query, state_ref[pl.ds(h * HEAD_DIM, HEAD_DIM), :], 1, 0)
        att_ref[:, cols] = (att + mm(scores, value_ref[:, cols], 1, 0)).astype(BF)


def query_terms_kernel(decay_ref, query_ref, own_ref, core_ref, other_ref, *rest):
    grad_ref, out_ref = rest[-2:]
    within = within_columns(decay_ref[...])
    for h in range(HEADS_LOCAL):
        cols = head_cols(h)
        grad = own_ref[:, cols] + core_ref[:, cols].astype(F32) + other_ref[:, cols].astype(F32)
        grad = grad.astype(BF)
        grad_ref[:, cols] = grad
        scaled = (jnp.exp(within[:, h : h + 1]) * query_ref[:, cols].astype(F32)).astype(BF)
        terms = mm(scaled, grad, 0, 0).astype(BF)
        for i in range(4):
            out_ref[4 * h + i] = terms[i * ROWS : (i + 1) * ROWS]


def inner_grads_kernel(
    decay_ref, query_ref, key_ref, value_ref, grad_ref, score_ref, state_ref,
    gq_ref, gk_ref, gv_ref,
):
    within = within_columns(decay_ref[...])
    for h in range(HEADS_LOCAL):
        cols = head_cols(h)
        col = within[:, h : h + 1]
        grad, key = grad_ref[:, cols], key_ref[:, cols]
        grad_scores = (mm(grad, value_ref[:, cols], 1, 1) * causal_mask(col)).astype(BF)
        state = state_ref[pl.ds(h * HEAD_DIM, HEAD_DIM), :]
        gq = jnp.exp(col) * mm(grad, state, 1, 1) + mm(grad_scores, key, 1, 0)
        gq_ref[:, cols] = gq.astype(BF)
        gk_ref[:, cols] = mm(grad_scores, query_ref[:, cols], 0, 0)
        gv_ref[:, cols] = mm(score_ref[:, cols], grad, 0, 0)


def outer_grads_kernel(
    decay_ref, key_ref, value_ref, inner_k_ref, inner_v_ref, after_ref, gk_ref, gv_ref
):
    within = within_columns(decay_ref[...])
    for h in range(HEADS_LOCAL):
        cols = head_cols(h)
        key_weight = jnp.exp(within[BLOCK - 1 : BLOCK, h : h + 1] - within[:, h : h + 1])
        after = after_ref[pl.ds(h * HEAD_DIM, HEAD_DIM), :]
        gk = key_weight * mm(value_ref[:, cols], after, 1, 1) + inner_k_ref[:, cols]
        gk_ref[:, cols] = gk.astype(BF)
        gv = key_weight * mm(key_ref[:, cols], after, 1, 0) + inner_v_ref[:, cols]
        gv_ref[:, cols] = gv.astype(BF)


def collect_kernel(a_ref, b_ref, c_ref, d_ref, out_ref):
    flip = flip_bit()
    for i, ref in ((flip, a_ref), (1 - flip, b_ref), (2 + flip, c_ref), (3 - flip, d_ref)):
        out_ref[:, pl.ds(pl.multiple_of(i * BLOCK, BLOCK), BLOCK)] = ref[...]


def assemble_kernel(share, own_ref, left_ref, right_ref, low_ref, high_ref, out_ref, out_t_ref):
    _, z, _, _, x = coordinates()
    for off, ref, start, part in (
        (0, own_ref, 0, 0), (0, own_ref, share, 1),
        (1, right_ref, 0, 0), (1, right_ref, share, 1),
        (2, low_ref, 0, 0), (2, high_ref, 0, 1),
        (3, left_ref, 0, 0), (3, left_ref, share, 1),
    ):
        k = (2 * ((x + off) % 4) + part - z + NZ) % NZ
        at = pl.multiple_of(k * share, 64)
        out_ref[pl.ds(at, share), :] = ref[start : start + share, :]
    for i in range(NZ * share // 256):
        rows = pl.ds(i * 256, 256)
        out_t_ref[:, rows] = jnp.transpose(out_ref[rows, :])


def project_kernel(block_ref, *refs):
    pieces, (kept_ref, theirs_ref, cross_ref, cross_theirs_ref), weight_ref = refs[:9], refs[-5:-1], refs[-1]
    at = 0
    for ref in pieces:
        weight_ref[at : at + ref.shape[0], :] = ref[...]
        at += ref.shape[0]
    out = mm(block_ref[...], weight_ref[...], 1, 0)
    kept_ref[...] = out[0:BLOCK]
    theirs_ref[...] = out[BLOCK : 2 * BLOCK]
    cross_ref[...] = out[2 * BLOCK : 3 * BLOCK].astype(BF)
    cross_theirs_ref[...] = out[3 * BLOCK : 4 * BLOCK].astype(BF)


def weight_kernel(block_ref, own_ref, neighbour_ref, across_ref, diagonal_ref, *rest):
    outs, tokens_ref = rest[-10:-1], rest[-1]
    for i, ref in enumerate((own_ref, neighbour_ref, across_ref, diagonal_ref)):
        tokens_ref[i * BLOCK : (i + 1) * BLOCK, :] = ref[...]
    out = mm(block_ref[...], tokens_ref[...], 1, 0).astype(BF)
    at = 0
    for ref in outs:
        ref[...] = out[at : at + ref.shape[0]]
        at += ref.shape[0]


def add_kernel(a_ref, b_ref, out_ref):
    out_ref[...] = (a_ref[...].astype(F32) + b_ref[...].astype(F32)).astype(BF)


def first_adds_kernel(up_part_ref, up_ref, down_part_ref, down_ref, up_out_ref, down_out_ref):
    half = up_ref.shape[0]
    up_out_ref[:half] = (up_part_ref[:half].astype(F32) + up_ref[...].astype(F32)).astype(BF)
    up_out_ref[half:] = up_part_ref[half:]
    down_out_ref[:half] = down_part_ref[:half]
    down_out_ref[half:] = (down_part_ref[half:].astype(F32) + down_ref[...].astype(F32)).astype(BF)


def adds_kernel(up_part_ref, up_ref, down_part_ref, down_ref, up_out_ref, down_out_ref):
    up_out_ref[...] = (up_part_ref[...].astype(F32) + up_ref[...].astype(F32)).astype(BF)
    down_out_ref[...] = (down_part_ref[...].astype(F32) + down_ref[...].astype(F32)).astype(BF)


def last_add_kernel(part_ref, up_ref, down_ref, out_ref):
    out_ref[...] = (
        part_ref[...].astype(F32) + (up_ref[...].astype(F32) + down_ref[...].astype(F32))
    ).astype(BF)


def shape(dims, dtype=BF):
    return jax.ShapeDtypeStruct(dims, dtype)


def call(body, outs, name, flops, moved, args, after=()):
    return pl.pallas_call(
        body,
        in_specs=[pl.BlockSpec(a.shape, lambda n=a.ndim: (0,) * n) for a in args]
        + [pl.BlockSpec(memory_space=pl.ANY)] * len(after),
        out_shape=outs,
        compiler_params=PARAMS,
        name=name,
        cost_estimate=pl.CostEstimate(flops=flops, bytes_accessed=moved, transcendentals=0),
    )(*args, *after)


def exchange(array):
    return lax.all_to_all(array, "seq", 0, 0, tiled=True)


def body(cotangent, queries, key_proj, value_proj, log_decay, out_weight):
    tokens, cols = queries.shape
    share = out_weight.shape[0]
    half = share // 2
    features = NZ * share
    row = shape((tokens, cols))
    row32 = shape((tokens, cols), F32)
    piece = shape((share, cols))
    state = shape((N_SEQ, ROWS, HEAD_DIM))

    below, above = [send(out_weight, Z_UP)], [send(out_weight, Z_DOWN)]

    terms = call(
        key_terms_kernel, shape((N_SEQ, ROWS + 16, HEAD_DIM)), "key_terms", 40_000_000, 1_000_000,
        (log_decay, key_proj, value_proj),
    )
    parts = call(
        cotangent_kernel, (shape((2 * share, tokens)),) * 2, "cotangent_parts", 0, 400_000, (cotangent,)
    )
    pieces = []
    for a in range(2):
        for b in range(2):
            table = pairs(lambda yl, z, c, yh, x, a=a, b=b: (yh, z, c ^ a, yl ^ b, x))
            pieces.append(send(parts[a], table))
    gathered = exchange(terms)
    own = call(collect_kernel, shape((2 * share, 4 * tokens)), "collect", 0, 800_000, pieces)
    left, right = send(own, X_UP), send(own, X_DOWN)

    befores = call(
        functools.partial(recurrence_kernel, False), state, "states_before", 1_000_000, 1_000_000,
        (gathered, gathered), (below[0], above[0], own),
    )
    below.append(send(below[-1], Z_UP))
    above.append(send(above[-1], Z_DOWN))
    states = exchange(befores).reshape(cols, HEAD_DIM)
    attended, scores = call(
        attended_kernel, (row, row), "attended", 110_000_000, 2_000_000,
        (log_decay, queries, key_proj, value_proj, states), (below[1], above[1], left, right),
    )
    below.append(send(below[-1], Z_UP))
    above.append(send(above[-1], Z_DOWN))
    across = send(attended, CORE)
    neighbour = send(attended, Y_LO)
    opposite_low = send(left[:share], X_UP)
    opposite_high = send(right[share:], X_DOWN)
    block, block_t = call(
        functools.partial(assemble_kernel, share),
        (shape((features, 4 * tokens)), shape((4 * tokens, features))), "assemble",
        1_000_000, 5_000_000, (own, left, right, opposite_low, opposite_high),
    )
    diagonal = send(neighbour, CORE)
    far_low = send(below[2][:half], Z_UP)
    far_high = send(above[2][half:], Z_DOWN)

    width = cols // TILES
    column_spec = pl.BlockSpec((tokens, width), lambda i: (0, i))
    piece_spec = pl.BlockSpec((share, width), lambda i: (0, i))
    half_spec = pl.BlockSpec((half, width), lambda i: (0, i))
    ring_specs = [piece_spec] * 4 + [half_spec] * 2 + [piece_spec] * 3
    cost = pl.CostEstimate(flops=1_600_000_000, bytes_accessed=6_000_000, transcendentals=0)
    part = pl.pallas_call(
        weight_kernel,
        grid=(TILES,),
        in_specs=[pl.BlockSpec((features, 4 * tokens), lambda i: (0, 0))]
        + [column_spec] * 4
        + [pl.BlockSpec(memory_space=pl.ANY)] * 2,
        out_specs=ring_specs,
        out_shape=[piece] * 4 + [shape((half, cols))] * 2 + [piece] * 3,
        scratch_shapes=[pltpu.VMEM((4 * tokens, width), BF)],
        compiler_params=PARAMS,
        name="weight_partial",
        cost_estimate=cost,
    )(block, attended, neighbour, across, diagonal, below[2], above[2])
    up, down = send(part[4], Z_UP), send(part[5], Z_DOWN)

    weights = [out_weight] + above + [far_low, far_high] + below[::-1]
    kept, theirs, cross, cross_theirs = pl.pallas_call(
        project_kernel,
        grid=(TILES,),
        in_specs=[pl.BlockSpec((4 * tokens, features), lambda i: (0, 0))] + ring_specs,
        out_specs=[column_spec] * 4,
        out_shape=[row32, row32, row, row],
        scratch_shapes=[pltpu.VMEM((features, width), BF)],
        compiler_params=PARAMS,
        name="project",
        cost_estimate=cost,
    )(block_t, *weights)
    from_core_theirs = send(cross_theirs, CORE)
    from_core = send(cross, CORE)
    passed = call(add_kernel, row, "sum_theirs", 100_000, 1_000_000, (theirs, from_core_theirs))
    arrived = send(passed, Y_LO)
    up, down = call(
        first_adds_kernel, (piece, piece), "ring_sum_3", 400_000, 2_000_000,
        (part[3], up, part[6], down),
    )
    up, down = send(up, Z_UP), send(down, Z_DOWN)
    grad_attn, query_terms = call(
        query_terms_kernel, (row, state), "query_terms", 40_000_000, 1_000_000,
        (log_decay, queries, kept, from_core, arrived),
    )
    returned = exchange(query_terms)
    up, down = call(
        adds_kernel, (piece, piece), "ring_sum_2", 400_000, 2_000_000, (part[2], up, part[7], down)
    )
    afters = call(
        functools.partial(recurrence_kernel, True), state, "states_after", 1_000_000, 1_000_000,
        (gathered, returned), (up, down),
    )
    up, down = send(up, Z_UP), send(down, Z_DOWN)
    after = exchange(afters).reshape(cols, HEAD_DIM)
    grad_queries, inner_k, inner_v = call(
        inner_grads_kernel, (row, row32, row32), "inner_grads", 200_000_000, 3_000_000,
        (log_decay, queries, key_proj, value_proj, grad_attn, scores, states),
    )
    up, down = call(
        adds_kernel, (piece, piece), "ring_sum_1", 400_000, 2_000_000, (part[1], up, part[8], down)
    )
    up, down = send(up, Z_UP), send(down, Z_DOWN)
    grad_keys, grad_values = call(
        outer_grads_kernel, (row, row), "outer_grads", 70_000_000, 3_000_000,
        (log_decay, key_proj, value_proj, inner_k, inner_v, after),
    )
    grad_weight = call(last_add_kernel, piece, "ring_sum_0", 400_000, 2_000_000, (part[0], up, down))
    return grad_queries, grad_keys, grad_values, grad_weight


def solution(mesh):
    placed = P("seq", "head")
    return jax.shard_map(
        body,
        mesh=mesh,
        in_specs=(placed,) * 6,
        out_specs=(placed,) * 4,
        check_vma=False,
    )
```

```python
import functools

import jax
import jax.numpy as jnp
from jax import lax
from jax.experimental import pallas as pl
from jax.experimental.pallas import tpu as pltpu
from jax.sharding import PartitionSpec as P

HEAD_DIM = 128
BLOCK = 128
HEADS_LOCAL = 8
N_SEQ = 32
ROWS = 32
NZ = 8
TILES = 4
BF = jnp.bfloat16
F32 = jnp.float32
AXES = ("seq", "head")
PARAMS = pltpu.CompilerParams(vmem_limit_bytes=16 * 1024 * 1024)


def pairs(move):
    out = []
    for yl in range(2):
        for z in range(8):
            for c in range(2):
                for yh in range(2):
                    for x in range(4):
                        a, b, d, e, f = move(yl, z, c, yh, x)
                        out.append(
                            (
                                (yl * 16 + z * 2 + c) * 8 + yh * 4 + x,
                                (a * 16 + (b % 8) * 2 + d) * 8 + e * 4 + f % 4,
                            )
                        )
    return out


Z_UP = pairs(lambda yl, z, c, yh, x: (yl, z + 1, c, yh, x))
Z_DOWN = pairs(lambda yl, z, c, yh, x: (yl, z + 7, c, yh, x))
X_UP = pairs(lambda yl, z, c, yh, x: (yl, z, c, yh, x + 1))
X_DOWN = pairs(lambda yl, z, c, yh, x: (yl, z, c, yh, x + 3))
CORE = pairs(lambda yl, z, c, yh, x: (yl, z, 1 - c, yh, x))
Y_LO = pairs(lambda yl, z, c, yh, x: (1 - yl, z, c, yh, x))


def send(array, table):
    return lax.ppermute(array, AXES, table)


def mm(a, b, ca, cb):
    return lax.dot_general(a, b, (((ca,), (cb,)), ((), ())), preferred_element_type=F32)


def coordinates():
    seq, head = lax.axis_index("seq"), lax.axis_index("head")
    y_lo = seq // 16
    rest = seq - 16 * y_lo
    z = rest // 2
    core = rest - 2 * z
    y_hi = head // 4
    return y_lo, z, core, y_hi, head - 4 * y_hi


def flip_bit():
    y_lo, _, _, y_hi, _ = coordinates()
    return y_lo + y_hi - 2 * y_lo * y_hi


def within_columns(decay):
    at = lax.broadcasted_iota(jnp.int32, (BLOCK, BLOCK), 0)
    of = lax.broadcasted_iota(jnp.int32, (BLOCK, BLOCK), 1)
    lower = (of <= at).astype(F32)
    return lax.dot_general(
        lower, decay, (((1,), (1,)), ((), ())),
        precision=lax.Precision.HIGHEST, preferred_element_type=F32,
    )


def causal_mask(within_col):
    gaps = within_col - jnp.transpose(within_col)
    at = lax.broadcasted_iota(jnp.int32, (BLOCK, BLOCK), 0)
    of = lax.broadcasted_iota(jnp.int32, (BLOCK, BLOCK), 1)
    return jnp.exp(jnp.where(at >= of, gaps, -jnp.inf))


def head_cols(h):
    return pl.ds(h * HEAD_DIM, HEAD_DIM)


def cotangent_kernel(cot_ref, same_ref, swap_ref):
    _, _, core, _, _ = coordinates()
    turned = jnp.transpose(cot_ref[...])
    share = turned.shape[0] // 4
    for i in range(2):
        first = turned[(2 * i) * share : (2 * i + 1) * share]
        second = turned[(2 * i + 1) * share : (2 * i + 2) * share]
        rows = pl.ds(i * share, share)

        @pl.when(core == 0)
        def _():
            same_ref[rows, :] = first
            swap_ref[rows, :] = second

        @pl.when(core == 1)
        def _():
            same_ref[rows, :] = second
            swap_ref[rows, :] = first


def key_terms_kernel(decay_ref, key_hbm, value_hbm, out_ref, key_ref, value_ref, sems):
    copies = (
        pltpu.make_async_copy(key_hbm, key_ref, sems.at[0]),
        pltpu.make_async_copy(value_hbm, value_ref, sems.at[1]),
    )
    for copy in copies:
        copy.start()
    within = within_columns(decay_ref[...])
    row = lax.broadcasted_iota(jnp.int32, (16, HEAD_DIM), 0)
    for copy in copies:
        copy.wait()
    for h in range(HEADS_LOCAL):
        col = within[:, h : h + 1]
        last = col[BLOCK - 1 : BLOCK]
        scaled = (jnp.exp(last - col) * key_ref[:, head_cols(h)].astype(F32)).astype(BF)
        terms = mm(scaled, value_ref[:, head_cols(h)], 0, 0).astype(BF)
        high = last.astype(BF).astype(F32)
        middle = (last - high).astype(BF).astype(F32)
        low = last - high - middle
        parts = jnp.where(row == 0, high, jnp.where(row == 1, middle, jnp.where(row == 2, low, 0.0)))
        parts = parts.astype(BF)
        for i in range(4):
            out_ref[4 * h + i, 0:ROWS, :] = terms[i * ROWS : (i + 1) * ROWS]
            out_ref[4 * h + i, ROWS : ROWS + 16, :] = parts


def recurrence_kernel(reverse, decay_ref, terms_ref, *rest):
    out_ref = rest[-1]
    state = jnp.zeros((ROWS, HEAD_DIM), F32)
    for k in reversed(range(N_SEQ)) if reverse else range(N_SEQ):
        out_ref[k] = state.astype(BF)
        parts = decay_ref[k, ROWS : ROWS + 16, :].astype(F32)
        factor = jnp.exp(parts[0:1] + (parts[1:2] + parts[2:3]))
        state = factor * state + terms_ref[k, 0:ROWS, :].astype(F32)


def attended_kernel(decay_ref, query_ref, key_ref, value_ref, state_ref, *rest):
    att_ref, score_ref = rest[-2:]
    within = within_columns(decay_ref[...])
    for h in range(HEADS_LOCAL):
        cols = head_cols(h)
        col = within[:, h : h + 1]
        query = query_ref[:, cols]
        scores = (mm(query, key_ref[:, cols], 1, 1) * causal_mask(col)).astype(BF)
        score_ref[:, cols] = scores
        att = jnp.exp(col) * mm(query, state_ref[pl.ds(h * HEAD_DIM, HEAD_DIM), :], 1, 0)
        att_ref[:, cols] = (att + mm(scores, value_ref[:, cols], 1, 0)).astype(BF)


def query_terms_kernel(decay_ref, query_ref, own_ref, core_ref, other_ref, *rest):
    grad_ref, out_ref = rest[-2:]
    within = within_columns(decay_ref[...])
    for h in range(HEADS_LOCAL):
        cols = head_cols(h)
        grad = own_ref[:, cols] + core_ref[:, cols].astype(F32) + other_ref[:, cols].astype(F32)
        grad = grad.astype(BF)
        grad_ref[:, cols] = grad
        scaled = (jnp.exp(within[:, h : h + 1]) * query_ref[:, cols].astype(F32)).astype(BF)
        terms = mm(scaled, grad, 0, 0).astype(BF)
        for i in range(4):
            out_ref[4 * h + i] = terms[i * ROWS : (i + 1) * ROWS]


def inner_grads_kernel(
    decay_ref, query_ref, key_ref, value_ref, grad_ref, score_ref, state_ref,
    gq_ref, gk_ref, gv_ref,
):
    within = within_columns(decay_ref[...])
    for h in range(HEADS_LOCAL):
        cols = head_cols(h)
        col = within[:, h : h + 1]
        grad, key = grad_ref[:, cols], key_ref[:, cols]
        grad_scores = (mm(grad, value_ref[:, cols], 1, 1) * causal_mask(col)).astype(BF)
        state = state_ref[pl.ds(h * HEAD_DIM, HEAD_DIM), :]
        gq = jnp.exp(col) * mm(grad, state, 1, 1) + mm(grad_scores, key, 1, 0)
        gq_ref[:, cols] = gq.astype(BF)
        gk_ref[:, cols] = mm(grad_scores, query_ref[:, cols], 0, 0)
        gv_ref[:, cols] = mm(score_ref[:, cols], grad, 0, 0)


def outer_grads_kernel(
    decay_ref, key_ref, value_ref, inner_k_ref, inner_v_ref, after_ref, gk_ref, gv_ref
):
    within = within_columns(decay_ref[...])
    for h in range(HEADS_LOCAL):
        cols = head_cols(h)
        key_weight = jnp.exp(within[BLOCK - 1 : BLOCK, h : h + 1] - within[:, h : h + 1])
        after = after_ref[pl.ds(h * HEAD_DIM, HEAD_DIM), :]
        gk = key_weight * mm(value_ref[:, cols], after, 1, 1) + inner_k_ref[:, cols]
        gk_ref[:, cols] = gk.astype(BF)
        gv = key_weight * mm(key_ref[:, cols], after, 1, 0) + inner_v_ref[:, cols]
        gv_ref[:, cols] = gv.astype(BF)


def collect_kernel(a_ref, b_ref, c_ref, d_ref, out_ref):
    flip = flip_bit()
    for i, ref in ((flip, a_ref), (1 - flip, b_ref), (2 + flip, c_ref), (3 - flip, d_ref)):
        out_ref[:, pl.ds(pl.multiple_of(i * BLOCK, BLOCK), BLOCK)] = ref[...]


def assemble_kernel(share, own_ref, left_ref, right_ref, low_ref, high_ref, out_ref, out_t_ref):
    _, z, _, _, x = coordinates()
    for off, ref, start, part in (
        (0, own_ref, 0, 0), (0, own_ref, share, 1),
        (1, right_ref, 0, 0), (1, right_ref, share, 1),
        (2, low_ref, 0, 0), (2, high_ref, 0, 1),
        (3, left_ref, 0, 0), (3, left_ref, share, 1),
    ):
        k = (2 * ((x + off) % 4) + part - z + NZ) % NZ
        at = pl.multiple_of(k * share, 64)
        out_ref[pl.ds(at, share), :] = ref[start : start + share, :]
    for i in range(NZ * share // 256):
        rows = pl.ds(i * 256, 256)
        out_t_ref[:, rows] = jnp.transpose(out_ref[rows, :])


def project_kernel(block_ref, *refs):
    pieces, (kept_ref, theirs_ref, cross_ref, cross_theirs_ref), weight_ref = refs[:9], refs[-5:-1], refs[-1]
    width = weight_ref.shape[1]
    for tile in range(kept_ref.shape[1] // width):
        cols = slice(tile * width, (tile + 1) * width)
        at = 0
        for ref in pieces:
            weight_ref[at : at + ref.shape[0], :] = ref[:, cols]
            at += ref.shape[0]
        out = mm(block_ref[...], weight_ref[...], 1, 0)
        kept_ref[:, cols] = out[0:BLOCK]
        theirs_ref[:, cols] = out[BLOCK : 2 * BLOCK]
        cross_ref[:, cols] = out[2 * BLOCK : 3 * BLOCK].astype(BF)
        cross_theirs_ref[:, cols] = out[3 * BLOCK : 4 * BLOCK].astype(BF)


def weight_kernel(block_ref, own_ref, neighbour_ref, across_ref, diagonal_ref, *rest):
    outs, tokens_ref = rest[-10:-1], rest[-1]
    width = tokens_ref.shape[1]
    for tile in range(own_ref.shape[1] // width):
        cols = slice(tile * width, (tile + 1) * width)
        for i, ref in enumerate((own_ref, neighbour_ref, across_ref, diagonal_ref)):
            tokens_ref[i * BLOCK : (i + 1) * BLOCK, :] = ref[:, cols]
        at = 0
        for ref in outs:
            rows = slice(at, at + ref.shape[0])
            ref[:, cols] = mm(block_ref[rows, :], tokens_ref[...], 1, 0).astype(BF)
            at += ref.shape[0]


def pass_kernel(a_ref, b_ref, after_ref, a_out_ref, b_out_ref):
    del after_ref
    a_out_ref[...] = a_ref[...]
    b_out_ref[...] = b_ref[...]


def add_kernel(a_ref, b_ref, out_ref):
    out_ref[...] = (a_ref[...].astype(F32) + b_ref[...].astype(F32)).astype(BF)


def first_adds_kernel(up_part_ref, up_ref, down_part_ref, down_ref, up_out_ref, down_out_ref):
    half = up_ref.shape[0]
    up_out_ref[:half] = (up_part_ref[:half].astype(F32) + up_ref[...].astype(F32)).astype(BF)
    up_out_ref[half:] = up_part_ref[half:]
    down_out_ref[:half] = down_part_ref[:half]
    down_out_ref[half:] = (down_part_ref[half:].astype(F32) + down_ref[...].astype(F32)).astype(BF)


def adds_kernel(up_part_ref, up_ref, down_part_ref, down_ref, up_out_ref, down_out_ref):
    up_out_ref[...] = (up_part_ref[...].astype(F32) + up_ref[...].astype(F32)).astype(BF)
    down_out_ref[...] = (down_part_ref[...].astype(F32) + down_ref[...].astype(F32)).astype(BF)


def last_add_kernel(part_ref, up_ref, down_ref, out_ref):
    out_ref[...] = (
        part_ref[...].astype(F32) + (up_ref[...].astype(F32) + down_ref[...].astype(F32))
    ).astype(BF)


def shape(dims, dtype=BF):
    return jax.ShapeDtypeStruct(dims, dtype)


def call(body, outs, name, flops, moved, args, after=()):
    return pl.pallas_call(
        body,
        in_specs=[pl.BlockSpec(a.shape, lambda n=a.ndim: (0,) * n) for a in args]
        + [pl.BlockSpec(memory_space=pltpu.VMEM)] * len(after),
        out_shape=outs,
        compiler_params=PARAMS,
        name=name,
        cost_estimate=pl.CostEstimate(flops=flops, bytes_accessed=moved, transcendentals=0),
    )(*args, *after)


def exchange(array):
    return lax.all_to_all(array, "seq", 0, 0, tiled=True)


def body(cotangent, queries, key_proj, value_proj, log_decay, out_weight):
    tokens, cols = queries.shape
    share = out_weight.shape[0]
    half = share // 2
    features = NZ * share
    row = shape((tokens, cols))
    row32 = shape((tokens, cols), F32)
    piece = shape((share, cols))
    state = shape((N_SEQ, ROWS, HEAD_DIM))

    below, above = [send(out_weight, Z_UP)], [send(out_weight, Z_DOWN)]

    log_decay = jnp.transpose(log_decay)
    terms = pl.pallas_call(
        key_terms_kernel,
        in_specs=[pl.BlockSpec(memory_space=pltpu.VMEM)] + [pl.BlockSpec(memory_space=pltpu.HBM)] * 2,
        out_shape=shape((N_SEQ, ROWS + 16, HEAD_DIM)),
        scratch_shapes=[pltpu.VMEM((tokens, cols), BF)] * 2 + [pltpu.SemaphoreType.DMA((2,))],
        compiler_params=PARAMS,
        name="key_terms",
        cost_estimate=pl.CostEstimate(flops=40_000_000, bytes_accessed=1_000_000, transcendentals=0),
    )(log_decay, key_proj, value_proj)
    parts = call(
        cotangent_kernel, (shape((2 * share, tokens)),) * 2, "cotangent_parts", 0, 400_000, (cotangent,)
    )
    pieces = []
    for a in range(2):
        for b in range(2):
            table = pairs(lambda yl, z, c, yh, x, a=a, b=b: (yh, z, c ^ a, yl ^ b, x))
            pieces.append(send(parts[a], table))
    gathered = exchange(terms)
    own = call(collect_kernel, shape((2 * share, 4 * tokens)), "collect", 0, 800_000, pieces)
    left, right = send(own, X_UP), send(own, X_DOWN)

    befores = call(
        functools.partial(recurrence_kernel, False), state, "states_before", 1_000_000, 1_000_000,
        (gathered, gathered),
    )
    below[0], above[0] = call(
        pass_kernel, (piece, piece), "pass_on", 0, 1_600_000, (below[0], above[0]), (own,)
    )
    below.append(send(below[-1], Z_UP))
    above.append(send(above[-1], Z_DOWN))
    states = exchange(befores).reshape(cols, HEAD_DIM)
    attended, scores = call(
        attended_kernel, (row, row), "attended", 110_000_000, 2_000_000,
        (log_decay, queries, key_proj, value_proj, states), (below[1], above[1], left, right),
    )
    below.append(send(below[-1], Z_UP))
    above.append(send(above[-1], Z_DOWN))
    across = send(attended, CORE)
    neighbour = send(attended, Y_LO)
    opposite_low = send(left[:share], X_UP)
    opposite_high = send(right[share:], X_DOWN)
    block, block_t = call(
        functools.partial(assemble_kernel, share),
        (shape((features, 4 * tokens)), shape((4 * tokens, features))), "assemble",
        1_000_000, 5_000_000, (own, left, right, opposite_low, opposite_high),
    )
    diagonal = send(neighbour, CORE)
    far_low = send(below[2][:half], Z_UP)
    far_high = send(above[2][half:], Z_DOWN)

    part = pl.pallas_call(
        weight_kernel,
        in_specs=[pl.BlockSpec(memory_space=pltpu.VMEM)] * 7,
        out_shape=[piece] * 4 + [shape((half, cols))] * 2 + [piece] * 3,
        scratch_shapes=[pltpu.VMEM((4 * tokens, cols // TILES), BF)],
        compiler_params=PARAMS,
        name="weight_partial",
        cost_estimate=pl.CostEstimate(
            flops=1_600_000_000, bytes_accessed=6_000_000, transcendentals=0
        ),
    )(block, attended, neighbour, across, diagonal, below[2], above[2])
    up, down = send(part[4], Z_UP), send(part[5], Z_DOWN)

    weights = [out_weight] + above + [far_low, far_high] + below[::-1]
    kept, theirs, cross, cross_theirs = pl.pallas_call(
        project_kernel,
        out_shape=[row32, row32, row, row],
        scratch_shapes=[pltpu.VMEM((features, cols // TILES), BF)],
        compiler_params=PARAMS,
        name="project",
        cost_estimate=pl.CostEstimate(
            flops=1_600_000_000, bytes_accessed=6_000_000, transcendentals=0
        ),
    )(block_t, *weights)
    from_core_theirs = send(cross_theirs, CORE)
    from_core = send(cross, CORE)
    passed = call(add_kernel, row, "sum_theirs", 100_000, 1_000_000, (theirs, from_core_theirs))
    arrived = send(passed, Y_LO)
    up, down = call(
        first_adds_kernel, (piece, piece), "ring_sum_3", 400_000, 2_000_000,
        (part[3], up, part[6], down),
    )
    up, down = send(up, Z_UP), send(down, Z_DOWN)
    grad_attn, query_terms = call(
        query_terms_kernel, (row, state), "query_terms", 40_000_000, 1_000_000,
        (log_decay, queries, kept, from_core, arrived),
    )
    returned = exchange(query_terms)
    up, down = call(
        adds_kernel, (piece, piece), "ring_sum_2", 400_000, 2_000_000, (part[2], up, part[7], down)
    )
    afters = call(
        functools.partial(recurrence_kernel, True), state, "states_after", 1_000_000, 1_000_000,
        (gathered, returned), (up, down),
    )
    up, down = send(up, Z_UP), send(down, Z_DOWN)
    after = exchange(afters).reshape(cols, HEAD_DIM)
    grad_queries, inner_k, inner_v = call(
        inner_grads_kernel, (row, row32, row32), "inner_grads", 200_000_000, 3_000_000,
        (log_decay, queries, key_proj, value_proj, grad_attn, scores, states),
    )
    up, down = call(
        adds_kernel, (piece, piece), "ring_sum_1", 400_000, 2_000_000, (part[1], up, part[8], down)
    )
    up, down = send(up, Z_UP), send(down, Z_DOWN)
    grad_keys, grad_values = call(
        outer_grads_kernel, (row, row), "outer_grads", 70_000_000, 3_000_000,
        (log_decay, key_proj, value_proj, inner_k, inner_v, after),
    )
    grad_weight = call(last_add_kernel, piece, "ring_sum_0", 400_000, 2_000_000, (part[0], up, down))
    return grad_queries, grad_keys, grad_values, grad_weight


def solution(mesh):
    placed = P("seq", "head")
    return jax.shard_map(
        body,
        mesh=mesh,
        in_specs=(placed,) * 6,
        out_specs=(placed,) * 4,
        check_vma=False,
    )
```

```python
import functools

import jax
import jax.numpy as jnp
from jax import lax
from jax.experimental import pallas as pl
from jax.experimental.pallas import tpu as pltpu
from jax.sharding import PartitionSpec as P

HEAD_DIM = 128
BLOCK = 128
HEADS_LOCAL = 8
N_SEQ = 32
ROWS = 32
NZ = 8
TILES = 4
BF = jnp.bfloat16
F32 = jnp.float32
AXES = ("seq", "head")
PARAMS = pltpu.CompilerParams(vmem_limit_bytes=16 * 1024 * 1024)


def pairs(move):
    out = []
    for yl in range(2):
        for z in range(8):
            for c in range(2):
                for yh in range(2):
                    for x in range(4):
                        a, b, d, e, f = move(yl, z, c, yh, x)
                        out.append(
                            (
                                (yl * 16 + z * 2 + c) * 8 + yh * 4 + x,
                                (a * 16 + (b % 8) * 2 + d) * 8 + e * 4 + f % 4,
                            )
                        )
    return out


Z_UP = pairs(lambda yl, z, c, yh, x: (yl, z + 1, c, yh, x))
Z_DOWN = pairs(lambda yl, z, c, yh, x: (yl, z + 7, c, yh, x))
X_UP = pairs(lambda yl, z, c, yh, x: (yl, z, c, yh, x + 1))
X_DOWN = pairs(lambda yl, z, c, yh, x: (yl, z, c, yh, x + 3))
CORE = pairs(lambda yl, z, c, yh, x: (yl, z, 1 - c, yh, x))
Y_LO = pairs(lambda yl, z, c, yh, x: (1 - yl, z, c, yh, x))


def send(array, table):
    return lax.ppermute(array, AXES, table)


def mm(a, b, ca, cb):
    return lax.dot_general(a, b, (((ca,), (cb,)), ((), ())), preferred_element_type=F32)


def coordinates():
    seq, head = lax.axis_index("seq"), lax.axis_index("head")
    y_lo = seq // 16
    rest = seq - 16 * y_lo
    z = rest // 2
    core = rest - 2 * z
    y_hi = head // 4
    return y_lo, z, core, y_hi, head - 4 * y_hi


def flip_bit():
    y_lo, _, _, y_hi, _ = coordinates()
    return y_lo + y_hi - 2 * y_lo * y_hi


def within_columns(decay):
    at = lax.broadcasted_iota(jnp.int32, (BLOCK, BLOCK), 0)
    of = lax.broadcasted_iota(jnp.int32, (BLOCK, BLOCK), 1)
    lower = (of <= at).astype(F32)
    return lax.dot_general(
        lower, decay, (((1,), (1,)), ((), ())),
        precision=lax.Precision.HIGHEST, preferred_element_type=F32,
    )


def causal_mask(within_col):
    gaps = within_col - jnp.transpose(within_col)
    at = lax.broadcasted_iota(jnp.int32, (BLOCK, BLOCK), 0)
    of = lax.broadcasted_iota(jnp.int32, (BLOCK, BLOCK), 1)
    return jnp.exp(jnp.where(at >= of, gaps, -jnp.inf))


def head_cols(h):
    return pl.ds(h * HEAD_DIM, HEAD_DIM)


def cotangent_kernel(cot_ref, *rest):
    same_ref, swap_ref = rest[-2:]
    _, _, core, _, _ = coordinates()
    turned = jnp.transpose(cot_ref[...])
    share = turned.shape[0] // 4
    for i in range(2):
        first = turned[(2 * i) * share : (2 * i + 1) * share]
        second = turned[(2 * i + 1) * share : (2 * i + 2) * share]
        rows = pl.ds(i * share, share)

        @pl.when(core == 0)
        def _():
            same_ref[rows, :] = first
            swap_ref[rows, :] = second

        @pl.when(core == 1)
        def _():
            same_ref[rows, :] = second
            swap_ref[rows, :] = first


def key_terms_kernel(decay_ref, key_hbm, value_hbm, out_ref, key_ref, value_ref, sems):
    copies = (
        pltpu.make_async_copy(key_hbm, key_ref, sems.at[0]),
        pltpu.make_async_copy(value_hbm, value_ref, sems.at[1]),
    )
    for copy in copies:
        copy.start()
    within = within_columns(decay_ref[...])
    row = lax.broadcasted_iota(jnp.int32, (16, HEAD_DIM), 0)
    for copy in copies:
        copy.wait()
    for h in range(HEADS_LOCAL):
        col = within[:, h : h + 1]
        last = col[BLOCK - 1 : BLOCK]
        scaled = (jnp.exp(last - col) * key_ref[:, head_cols(h)].astype(F32)).astype(BF)
        terms = mm(scaled, value_ref[:, head_cols(h)], 0, 0).astype(BF)
        high = last.astype(BF).astype(F32)
        middle = (last - high).astype(BF).astype(F32)
        low = last - high - middle
        parts = jnp.where(row == 0, high, jnp.where(row == 1, middle, jnp.where(row == 2, low, 0.0)))
        parts = parts.astype(BF)
        for i in range(4):
            out_ref[4 * h + i, 0:ROWS, :] = terms[i * ROWS : (i + 1) * ROWS]
            out_ref[4 * h + i, ROWS : ROWS + 16, :] = parts


def recurrence_kernel(reverse, decay_ref, terms_ref, *rest):
    out_ref = rest[-1]
    state = jnp.zeros((ROWS, HEAD_DIM), F32)
    for k in reversed(range(N_SEQ)) if reverse else range(N_SEQ):
        out_ref[k] = state.astype(BF)
        parts = decay_ref[k, ROWS : ROWS + 16, :].astype(F32)
        factor = jnp.exp(parts[0:1] + (parts[1:2] + parts[2:3]))
        state = factor * state + terms_ref[k, 0:ROWS, :].astype(F32)


def attended_kernel(decay_ref, query_ref, key_ref, value_ref, state_ref, *rest):
    att_ref, score_ref = rest[-2:]
    within = within_columns(decay_ref[...])
    for h in range(HEADS_LOCAL):
        cols = head_cols(h)
        col = within[:, h : h + 1]
        query = query_ref[:, cols]
        scores = (mm(query, key_ref[:, cols], 1, 1) * causal_mask(col)).astype(BF)
        score_ref[:, cols] = scores
        att = jnp.exp(col) * mm(query, state_ref[pl.ds(h * HEAD_DIM, HEAD_DIM), :], 1, 0)
        att_ref[:, cols] = (att + mm(scores, value_ref[:, cols], 1, 0)).astype(BF)


def query_terms_kernel(decay_ref, query_ref, own_ref, core_ref, other_ref, *rest):
    grad_ref, out_ref = rest[-2:]
    within = within_columns(decay_ref[...])
    for h in range(HEADS_LOCAL):
        cols = head_cols(h)
        grad = own_ref[:, cols] + core_ref[:, cols].astype(F32) + other_ref[:, cols].astype(F32)
        grad = grad.astype(BF)
        grad_ref[:, cols] = grad
        scaled = (jnp.exp(within[:, h : h + 1]) * query_ref[:, cols].astype(F32)).astype(BF)
        terms = mm(scaled, grad, 0, 0).astype(BF)
        for i in range(4):
            out_ref[4 * h + i] = terms[i * ROWS : (i + 1) * ROWS]


def inner_grads_kernel(
    decay_ref, query_ref, key_ref, value_ref, grad_ref, score_ref, state_ref,
    gq_ref, gk_ref, gv_ref,
):
    within = within_columns(decay_ref[...])
    for h in range(HEADS_LOCAL):
        cols = head_cols(h)
        col = within[:, h : h + 1]
        grad, key = grad_ref[:, cols], key_ref[:, cols]
        grad_scores = (mm(grad, value_ref[:, cols], 1, 1) * causal_mask(col)).astype(BF)
        state = state_ref[pl.ds(h * HEAD_DIM, HEAD_DIM), :]
        gq = jnp.exp(col) * mm(grad, state, 1, 1) + mm(grad_scores, key, 1, 0)
        gq_ref[:, cols] = gq.astype(BF)
        gk_ref[:, cols] = mm(grad_scores, query_ref[:, cols], 0, 0)
        gv_ref[:, cols] = mm(score_ref[:, cols], grad, 0, 0)


def outer_grads_kernel(
    decay_ref, key_ref, value_ref, inner_k_ref, inner_v_ref, after_ref, gk_ref, gv_ref
):
    within = within_columns(decay_ref[...])
    for h in range(HEADS_LOCAL):
        cols = head_cols(h)
        key_weight = jnp.exp(within[BLOCK - 1 : BLOCK, h : h + 1] - within[:, h : h + 1])
        after = after_ref[pl.ds(h * HEAD_DIM, HEAD_DIM), :]
        gk = key_weight * mm(value_ref[:, cols], after, 1, 1) + inner_k_ref[:, cols]
        gk_ref[:, cols] = gk.astype(BF)
        gv = key_weight * mm(key_ref[:, cols], after, 1, 0) + inner_v_ref[:, cols]
        gv_ref[:, cols] = gv.astype(BF)


def collect_kernel(a_ref, b_ref, c_ref, d_ref, out_ref):
    flip = flip_bit()
    for i, ref in ((flip, a_ref), (1 - flip, b_ref), (2 + flip, c_ref), (3 - flip, d_ref)):
        out_ref[:, pl.ds(pl.multiple_of(i * BLOCK, BLOCK), BLOCK)] = ref[...]


def assemble_kernel(share, own_ref, left_ref, right_ref, low_ref, high_ref, out_ref, out_t_ref):
    _, z, _, _, x = coordinates()
    for off, ref, start, part in (
        (0, own_ref, 0, 0), (0, own_ref, share, 1),
        (1, right_ref, 0, 0), (1, right_ref, share, 1),
        (2, low_ref, 0, 0), (2, high_ref, 0, 1),
        (3, left_ref, 0, 0), (3, left_ref, share, 1),
    ):
        k = (2 * ((x + off) % 4) + part - z + NZ) % NZ
        at = pl.multiple_of(k * share, 64)
        out_ref[pl.ds(at, share), :] = ref[start : start + share, :]
    for i in range(NZ * share // 256):
        rows = pl.ds(i * 256, 256)
        out_t_ref[:, rows] = jnp.transpose(out_ref[rows, :])


def project_kernel(block_ref, *refs):
    pieces, (kept_ref, theirs_ref, cross_ref, cross_theirs_ref), weight_ref = refs[:9], refs[-5:-1], refs[-1]
    width = weight_ref.shape[1]
    for tile in range(kept_ref.shape[1] // width):
        cols = slice(tile * width, (tile + 1) * width)
        at = 0
        for ref in pieces:
            weight_ref[at : at + ref.shape[0], :] = ref[:, cols]
            at += ref.shape[0]
        out = mm(block_ref[...], weight_ref[...], 1, 0)
        kept_ref[:, cols] = out[0:BLOCK]
        theirs_ref[:, cols] = out[BLOCK : 2 * BLOCK]
        cross_ref[:, cols] = out[2 * BLOCK : 3 * BLOCK].astype(BF)
        cross_theirs_ref[:, cols] = out[3 * BLOCK : 4 * BLOCK].astype(BF)


def weight_kernel(block_ref, own_ref, neighbour_ref, across_ref, diagonal_ref, *rest):
    outs, tokens_ref = rest[-10:-1], rest[-1]
    width = tokens_ref.shape[1]
    for tile in range(own_ref.shape[1] // width):
        cols = slice(tile * width, (tile + 1) * width)
        for i, ref in enumerate((own_ref, neighbour_ref, across_ref, diagonal_ref)):
            tokens_ref[i * BLOCK : (i + 1) * BLOCK, :] = ref[:, cols]
        at = 0
        for ref in outs:
            rows = slice(at, at + ref.shape[0])
            ref[:, cols] = mm(block_ref[rows, :], tokens_ref[...], 1, 0).astype(BF)
            at += ref.shape[0]


def add_kernel(a_ref, b_ref, out_ref):
    out_ref[...] = (a_ref[...].astype(F32) + b_ref[...].astype(F32)).astype(BF)


def first_adds_kernel(up_part_ref, up_ref, down_part_ref, down_ref, *rest):
    up_out_ref, down_out_ref = rest[-2:]
    half = up_ref.shape[0]
    up_out_ref[:half] = (up_part_ref[:half].astype(F32) + up_ref[...].astype(F32)).astype(BF)
    up_out_ref[half:] = up_part_ref[half:]
    down_out_ref[:half] = down_part_ref[:half]
    down_out_ref[half:] = (down_part_ref[half:].astype(F32) + down_ref[...].astype(F32)).astype(BF)


def adds_kernel(up_part_ref, up_ref, down_part_ref, down_ref, up_out_ref, down_out_ref):
    up_out_ref[...] = (up_part_ref[...].astype(F32) + up_ref[...].astype(F32)).astype(BF)
    down_out_ref[...] = (down_part_ref[...].astype(F32) + down_ref[...].astype(F32)).astype(BF)


def last_add_kernel(part_ref, up_ref, down_ref, out_ref):
    out_ref[...] = (
        part_ref[...].astype(F32) + (up_ref[...].astype(F32) + down_ref[...].astype(F32))
    ).astype(BF)


def shape(dims, dtype=BF):
    return jax.ShapeDtypeStruct(dims, dtype)


def call(body, outs, name, flops, moved, args, after=()):
    return pl.pallas_call(
        body,
        in_specs=[pl.BlockSpec(a.shape, lambda n=a.ndim: (0,) * n) for a in args]
        + [pl.BlockSpec(memory_space=pltpu.VMEM)] * len(after),
        out_shape=outs,
        compiler_params=PARAMS,
        name=name,
        cost_estimate=pl.CostEstimate(flops=flops, bytes_accessed=moved, transcendentals=0),
    )(*args, *after)


def exchange(array):
    return lax.all_to_all(array, "seq", 0, 0, tiled=True)


def body(cotangent, queries, key_proj, value_proj, log_decay, out_weight):
    tokens, cols = queries.shape
    share = out_weight.shape[0]
    half = share // 2
    features = NZ * share
    row = shape((tokens, cols))
    row32 = shape((tokens, cols), F32)
    piece = shape((share, cols))
    state = shape((N_SEQ, ROWS, HEAD_DIM))

    below, above = [send(out_weight, Z_UP)], [send(out_weight, Z_DOWN)]

    log_decay = jnp.transpose(log_decay)
    terms = pl.pallas_call(
        key_terms_kernel,
        in_specs=[pl.BlockSpec(memory_space=pltpu.VMEM)] + [pl.BlockSpec(memory_space=pltpu.HBM)] * 2,
        out_shape=shape((N_SEQ, ROWS + 16, HEAD_DIM)),
        scratch_shapes=[pltpu.VMEM((tokens, cols), BF)] * 2 + [pltpu.SemaphoreType.DMA((2,))],
        compiler_params=PARAMS,
        name="key_terms",
        cost_estimate=pl.CostEstimate(flops=40_000_000, bytes_accessed=1_000_000, transcendentals=0),
    )(log_decay, key_proj, value_proj)
    parts = call(
        cotangent_kernel, (shape((2 * share, tokens)),) * 2, "cotangent_parts", 40_000_000_000, 400_000,
        (cotangent,), (below[0], above[0]),
    )
    below.append(send(below[0], Z_UP))
    above.append(send(above[0], Z_DOWN))
    pieces = []
    for a in range(2):
        for b in range(2):
            table = pairs(lambda yl, z, c, yh, x, a=a, b=b: (yh, z, c ^ a, yl ^ b, x))
            pieces.append(send(parts[a], table))
    gathered = exchange(terms)
    own = call(collect_kernel, shape((2 * share, 4 * tokens)), "collect", 0, 800_000, pieces)
    left, right = send(own, X_UP), send(own, X_DOWN)

    befores = call(
        functools.partial(recurrence_kernel, False), state, "states_before", 1_000_000, 1_000_000,
        (gathered, gathered),
    )
    states = exchange(befores).reshape(cols, HEAD_DIM)
    attended, scores = call(
        attended_kernel, (row, row), "attended", 110_000_000, 2_000_000,
        (log_decay, queries, key_proj, value_proj, states), (below[1], above[1]),
    )
    below.append(send(below[-1], Z_UP))
    above.append(send(above[-1], Z_DOWN))
    across = send(attended, CORE)
    neighbour = send(attended, Y_LO)
    opposite_low = send(left[:share], X_UP)
    opposite_high = send(right[share:], X_DOWN)
    block, block_t = call(
        functools.partial(assemble_kernel, share),
        (shape((features, 4 * tokens)), shape((4 * tokens, features))), "assemble",
        1_000_000, 5_000_000, (own, left, right, opposite_low, opposite_high),
    )
    diagonal = send(neighbour, CORE)
    far_low = send(below[2][:half], Z_UP)
    far_high = send(above[2][half:], Z_DOWN)

    weights = [out_weight] + above + [far_low, far_high] + below[::-1]
    kept, theirs, cross, cross_theirs = pl.pallas_call(
        project_kernel,
        out_shape=[row32, row32, row, row],
        scratch_shapes=[pltpu.VMEM((features, cols // TILES), BF)],
        compiler_params=PARAMS,
        name="project",
        cost_estimate=pl.CostEstimate(
            flops=1_600_000_000, bytes_accessed=6_000_000, transcendentals=0
        ),
    )(block_t, *weights)
    from_core_theirs = send(cross_theirs, CORE)
    from_core = send(cross, CORE)
    passed = call(add_kernel, row, "sum_theirs", 100_000, 1_000_000, (theirs, from_core_theirs))
    arrived = send(passed, Y_LO)

    part = pl.pallas_call(
        weight_kernel,
        in_specs=[pl.BlockSpec(memory_space=pltpu.VMEM)] * 6,
        out_shape=[piece] * 4 + [shape((half, cols))] * 2 + [piece] * 3,
        scratch_shapes=[pltpu.VMEM((4 * tokens, cols // TILES), BF)],
        compiler_params=PARAMS,
        name="weight_partial",
        cost_estimate=pl.CostEstimate(
            flops=1_600_000_000, bytes_accessed=6_000_000, transcendentals=0
        ),
    )(block, attended, neighbour, across, diagonal, passed)
    up, down = send(part[4], Z_UP), send(part[5], Z_DOWN)

    up, down = call(
        first_adds_kernel, (piece, piece), "ring_sum_3", 400_000, 2_000_000,
        (part[3], up, part[6], down), (arrived,),
    )
    up, down = send(up, Z_UP), send(down, Z_DOWN)
    grad_attn, query_terms = call(
        query_terms_kernel, (row, state), "query_terms", 40_000_000, 1_000_000,
        (log_decay, queries, kept, from_core, arrived),
    )
    returned = exchange(query_terms)
    up, down = call(
        adds_kernel, (piece, piece), "ring_sum_2", 400_000, 2_000_000, (part[2], up, part[7], down)
    )
    afters = call(
        functools.partial(recurrence_kernel, True), state, "states_after", 1_000_000, 1_000_000,
        (gathered, returned), (up, down),
    )
    up, down = send(up, Z_UP), send(down, Z_DOWN)
    after = exchange(afters).reshape(cols, HEAD_DIM)
    grad_queries, inner_k, inner_v = call(
        inner_grads_kernel, (row, row32, row32), "inner_grads", 200_000_000, 3_000_000,
        (log_decay, queries, key_proj, value_proj, grad_attn, scores, states),
    )
    up, down = call(
        adds_kernel, (piece, piece), "ring_sum_1", 400_000, 2_000_000, (part[1], up, part[8], down)
    )
    up, down = send(up, Z_UP), send(down, Z_DOWN)
    grad_keys, grad_values = call(
        outer_grads_kernel, (row, row), "outer_grads", 70_000_000, 3_000_000,
        (log_decay, key_proj, value_proj, inner_k, inner_v, after),
    )
    grad_weight = call(last_add_kernel, piece, "ring_sum_0", 400_000, 2_000_000, (part[0], up, down))
    return grad_queries, grad_keys, grad_values, grad_weight


def solution(mesh):
    placed = P("seq", "head")
    return jax.shard_map(
        body,
        mesh=mesh,
        in_specs=(placed,) * 6,
        out_specs=(placed,) * 4,
        check_vma=False,
    )
```

```python
import functools

import jax
import jax.numpy as jnp
from jax import lax
from jax.experimental import pallas as pl
from jax.experimental.pallas import tpu as pltpu
from jax.sharding import PartitionSpec as P

HEAD_DIM = 128
BLOCK = 128
HEADS_LOCAL = 8
N_SEQ = 32
ROWS = 32
NZ = 8
TILES = 4
BF = jnp.bfloat16
F32 = jnp.float32
AXES = ("seq", "head")
PARAMS = pltpu.CompilerParams(vmem_limit_bytes=16 * 1024 * 1024)


def pairs(move):
    out = []
    for yl in range(2):
        for z in range(8):
            for c in range(2):
                for yh in range(2):
                    for x in range(4):
                        a, b, d, e, f = move(yl, z, c, yh, x)
                        out.append(
                            (
                                (yl * 16 + z * 2 + c) * 8 + yh * 4 + x,
                                (a * 16 + (b % 8) * 2 + d) * 8 + e * 4 + f % 4,
                            )
                        )
    return out


Z_UP = pairs(lambda yl, z, c, yh, x: (yl, z + 1, c, yh, x))
Z_DOWN = pairs(lambda yl, z, c, yh, x: (yl, z + 7, c, yh, x))
X_UP = pairs(lambda yl, z, c, yh, x: (yl, z, c, yh, x + 1))
X_DOWN = pairs(lambda yl, z, c, yh, x: (yl, z, c, yh, x + 3))
CORE = pairs(lambda yl, z, c, yh, x: (yl, z, 1 - c, yh, x))
Y_HI = pairs(lambda yl, z, c, yh, x: (yl, z, c, 1 - yh, x))
Y_LO = pairs(lambda yl, z, c, yh, x: (1 - yl, z, c, yh, x))


def send(array, table):
    return lax.ppermute(array, AXES, table)


def mm(a, b, ca, cb):
    return lax.dot_general(a, b, (((ca,), (cb,)), ((), ())), preferred_element_type=F32)


def coordinates():
    seq, head = lax.axis_index("seq"), lax.axis_index("head")
    y_lo = seq // 16
    rest = seq - 16 * y_lo
    z = rest // 2
    core = rest - 2 * z
    y_hi = head // 4
    return y_lo, z, core, y_hi, head - 4 * y_hi


def flip_bit():
    y_lo, _, _, y_hi, _ = coordinates()
    return y_lo + y_hi - 2 * y_lo * y_hi


def within_columns(decay):
    at = lax.broadcasted_iota(jnp.int32, (BLOCK, BLOCK), 0)
    of = lax.broadcasted_iota(jnp.int32, (BLOCK, BLOCK), 1)
    lower = (of <= at).astype(F32)
    return lax.dot_general(
        lower, decay, (((1,), (1,)), ((), ())),
        precision=lax.Precision.HIGHEST, preferred_element_type=F32,
    )


def causal_mask(within_col):
    gaps = within_col - jnp.transpose(within_col)
    at = lax.broadcasted_iota(jnp.int32, (BLOCK, BLOCK), 0)
    of = lax.broadcasted_iota(jnp.int32, (BLOCK, BLOCK), 1)
    return jnp.exp(jnp.where(at >= of, gaps, -jnp.inf))


def head_cols(h):
    return pl.ds(h * HEAD_DIM, HEAD_DIM)


def cotangent_kernel(cot_ref, *rest):
    same_ref, swap_ref = rest[-2:]
    _, _, core, _, _ = coordinates()
    turned = jnp.transpose(cot_ref[...])
    share = turned.shape[0] // 4
    for i in range(2):
        first = turned[(2 * i) * share : (2 * i + 1) * share]
        second = turned[(2 * i + 1) * share : (2 * i + 2) * share]
        rows = pl.ds(i * share, share)

        @pl.when(core == 0)
        def _():
            same_ref[rows, :] = first
            swap_ref[rows, :] = second

        @pl.when(core == 1)
        def _():
            same_ref[rows, :] = second
            swap_ref[rows, :] = first


def key_terms_kernel(decay_ref, key_hbm, value_hbm, out_ref, key_ref, value_ref, sems):
    copies = (
        pltpu.make_async_copy(key_hbm, key_ref, sems.at[0]),
        pltpu.make_async_copy(value_hbm, value_ref, sems.at[1]),
    )
    for copy in copies:
        copy.start()
    within = within_columns(decay_ref[...])
    row = lax.broadcasted_iota(jnp.int32, (16, HEAD_DIM), 0)
    for copy in copies:
        copy.wait()
    for h in range(HEADS_LOCAL):
        col = within[:, h : h + 1]
        last = col[BLOCK - 1 : BLOCK]
        scaled = (jnp.exp(last - col) * key_ref[:, head_cols(h)].astype(F32)).astype(BF)
        terms = mm(scaled, value_ref[:, head_cols(h)], 0, 0).astype(BF)
        high = last.astype(BF).astype(F32)
        middle = (last - high).astype(BF).astype(F32)
        low = last - high - middle
        parts = jnp.where(row == 0, high, jnp.where(row == 1, middle, jnp.where(row == 2, low, 0.0)))
        parts = parts.astype(BF)
        for i in range(4):
            out_ref[4 * h + i, 0:ROWS, :] = terms[i * ROWS : (i + 1) * ROWS]
            out_ref[4 * h + i, ROWS : ROWS + 16, :] = parts


def recurrence_kernel(reverse, decay_ref, terms_ref, *rest):
    out_ref = rest[-1]
    state = jnp.zeros((ROWS, HEAD_DIM), F32)
    for k in reversed(range(N_SEQ)) if reverse else range(N_SEQ):
        out_ref[k] = state.astype(BF)
        parts = decay_ref[k, ROWS : ROWS + 16, :].astype(F32)
        factor = jnp.exp(parts[0:1] + (parts[1:2] + parts[2:3]))
        state = factor * state + terms_ref[k, 0:ROWS, :].astype(F32)


def attended_kernel(decay_ref, query_ref, key_ref, value_ref, state_ref, *rest):
    att_ref, score_ref = rest[-2:]
    within = within_columns(decay_ref[...])
    for h in range(HEADS_LOCAL):
        cols = head_cols(h)
        col = within[:, h : h + 1]
        query = query_ref[:, cols]
        scores = (mm(query, key_ref[:, cols], 1, 1) * causal_mask(col)).astype(BF)
        score_ref[:, cols] = scores
        att = jnp.exp(col) * mm(query, state_ref[pl.ds(h * HEAD_DIM, HEAD_DIM), :], 1, 0)
        att_ref[:, cols] = (att + mm(scores, value_ref[:, cols], 1, 0)).astype(BF)


def query_terms_kernel(decay_ref, query_ref, own_ref, core_ref, other_ref, *rest):
    grad_ref, out_ref = rest[-2:]
    within = within_columns(decay_ref[...])
    for h in range(HEADS_LOCAL):
        cols = head_cols(h)
        grad = own_ref[:, cols] + core_ref[:, cols].astype(F32) + other_ref[:, cols].astype(F32)
        grad = grad.astype(BF)
        grad_ref[:, cols] = grad
        scaled = (jnp.exp(within[:, h : h + 1]) * query_ref[:, cols].astype(F32)).astype(BF)
        terms = mm(scaled, grad, 0, 0).astype(BF)
        for i in range(4):
            out_ref[4 * h + i] = terms[i * ROWS : (i + 1) * ROWS]


def inner_grads_kernel(
    decay_ref, query_ref, key_ref, value_ref, grad_ref, score_ref, state_ref,
    gq_ref, gk_ref, gv_ref,
):
    within = within_columns(decay_ref[...])
    for h in range(HEADS_LOCAL):
        cols = head_cols(h)
        col = within[:, h : h + 1]
        grad, key = grad_ref[:, cols], key_ref[:, cols]
        grad_scores = (mm(grad, value_ref[:, cols], 1, 1) * causal_mask(col)).astype(BF)
        state = state_ref[pl.ds(h * HEAD_DIM, HEAD_DIM), :]
        gq = jnp.exp(col) * mm(grad, state, 1, 1) + mm(grad_scores, key, 1, 0)
        gq_ref[:, cols] = gq.astype(BF)
        gk_ref[:, cols] = mm(grad_scores, query_ref[:, cols], 0, 0)
        gv_ref[:, cols] = mm(score_ref[:, cols], grad, 0, 0)


def outer_grads_kernel(
    decay_ref, key_ref, value_ref, inner_k_ref, inner_v_ref, after_ref, gk_ref, gv_ref
):
    within = within_columns(decay_ref[...])
    for h in range(HEADS_LOCAL):
        cols = head_cols(h)
        key_weight = jnp.exp(within[BLOCK - 1 : BLOCK, h : h + 1] - within[:, h : h + 1])
        after = after_ref[pl.ds(h * HEAD_DIM, HEAD_DIM), :]
        gk = key_weight * mm(value_ref[:, cols], after, 1, 1) + inner_k_ref[:, cols]
        gk_ref[:, cols] = gk.astype(BF)
        gv = key_weight * mm(key_ref[:, cols], after, 1, 0) + inner_v_ref[:, cols]
        gv_ref[:, cols] = gv.astype(BF)


def collect_kernel(a_ref, b_ref, c_ref, d_ref, out_ref):
    flip = flip_bit()
    for i, ref in ((flip, a_ref), (1 - flip, b_ref), (2 + flip, c_ref), (3 - flip, d_ref)):
        out_ref[:, pl.ds(pl.multiple_of(i * BLOCK, BLOCK), BLOCK)] = ref[...]


def assemble_kernel(share, own_ref, left_ref, right_ref, opposite_ref, out_ref, turned_ref):
    _, z, _, _, x = coordinates()
    for off, ref in ((0, own_ref), (1, right_ref), (2, opposite_ref), (3, left_ref)):
        for part in range(2):
            k = (2 * ((x + off) % 4) + part - z + NZ) % NZ
            at = pl.multiple_of(k * share, 64)
            turned_ref[pl.ds(at, share), :] = ref[part * share : (part + 1) * share, :]
    for i in range(NZ * share // 256):
        rows = slice(i * 256, (i + 1) * 256)
        out_ref[:, rows] = jnp.transpose(turned_ref[rows, :])


def halves_kernel(cot_ref, *rest):
    same_ref, swap_ref = rest[-2:]
    _, z, _, _, _ = coordinates()
    turned = jnp.transpose(cot_ref[...])
    half = turned.shape[0] // 2

    @pl.when(z % 2 == 0)
    def _():
        same_ref[...] = turned[:half]
        swap_ref[...] = turned[half:]

    @pl.when(z % 2 == 1)
    def _():
        same_ref[...] = turned[half:]
        swap_ref[...] = turned[:half]


def join_kernel(own_same_ref, own_swap_ref, other_ref, out_ref):
    half = other_ref.shape[0]
    out_ref[:half, :BLOCK] = own_same_ref[...]
    out_ref[:half, BLOCK:] = own_swap_ref[...]
    out_ref[half:, :] = other_ref[...]


def pair_kernel(a_ref, b_ref, out_ref):
    out_ref[:, :BLOCK] = a_ref[...]
    out_ref[:, BLOCK:] = b_ref[...]


def assemble_weight_kernel(share, own_ref, left_ref, right_ref, opposite_ref, out_ref):
    y_lo, z, core, y_hi, x = coordinates()
    parity = z % 2
    for off, ref in ((0, own_ref), (1, right_ref), (2, opposite_ref), (3, left_ref)):
        for r in range(2):
            bit = parity + r - 2 * parity * r
            k = (2 * ((x + off) % 4) + bit - z + NZ) % NZ
            lanes = pl.ds(pl.multiple_of(k * BLOCK, BLOCK), BLOCK)
            for group, (a, b) in enumerate(((0, 0), (0, 1), (1, 0), (1, 1))):
                of_core = core + a - 2 * core * a
                of_y = y_lo + b - 2 * y_lo * b
                far = of_y + y_hi - 2 * of_y * y_hi
                rows = pl.ds(pl.multiple_of((2 * far + of_core) * share, 64), share)
                out_ref[group * share : (group + 1) * share, lanes] = ref[
                    rows, r * BLOCK : (r + 1) * BLOCK
                ]


def project_kernel(block_ref, *refs):
    pieces, (kept_ref, theirs_ref, cross_ref, cross_theirs_ref), weight_ref = refs[:9], refs[-5:-1], refs[-1]
    width = weight_ref.shape[1]
    for tile in range(kept_ref.shape[1] // width):
        cols = slice(tile * width, (tile + 1) * width)
        at = 0
        for ref in pieces:
            weight_ref[at : at + ref.shape[0], :] = ref[:, cols]
            at += ref.shape[0]
        out = mm(block_ref[...], weight_ref[...], 1, 0)
        kept_ref[:, cols] = out[0:BLOCK]
        theirs_ref[:, cols] = out[BLOCK : 2 * BLOCK]
        cross_ref[:, cols] = out[2 * BLOCK : 3 * BLOCK].astype(BF)
        cross_theirs_ref[:, cols] = out[3 * BLOCK : 4 * BLOCK].astype(BF)


def weight_kernel(block_ref, *refs):
    pieces, (kept_ref, theirs_ref, cross_ref, cross_theirs_ref), tokens_ref = refs[:9], refs[-5:-1], refs[-1]
    share = kept_ref.shape[0]
    width = tokens_ref.shape[1]
    for tile in range(kept_ref.shape[1] // width):
        cols = slice(tile * width, (tile + 1) * width)
        at = 0
        for ref in pieces:
            tokens_ref[at : at + ref.shape[0], :] = ref[:, cols]
            at += ref.shape[0]
        out = mm(block_ref[...], tokens_ref[...], 1, 0)
        kept_ref[:, cols] = out[0:share]
        theirs_ref[:, cols] = out[share : 2 * share]
        cross_ref[:, cols] = out[2 * share : 3 * share].astype(BF)
        cross_theirs_ref[:, cols] = out[3 * share : 4 * share].astype(BF)


def add_kernel(a_ref, b_ref, out_ref):
    out_ref[...] = (a_ref[...].astype(F32) + b_ref[...].astype(F32)).astype(BF)


def last_add_kernel(kept_ref, core_ref, other_ref, out_ref):
    out_ref[...] = (
        kept_ref[...] + core_ref[...].astype(F32) + other_ref[...].astype(F32)
    ).astype(BF)


def shape(dims, dtype=BF):
    return jax.ShapeDtypeStruct(dims, dtype)


def call(body, outs, name, flops, moved, args, after=(), scratch=()):
    return pl.pallas_call(
        body,
        in_specs=[pl.BlockSpec(a.shape, lambda n=a.ndim: (0,) * n) for a in args]
        + [pl.BlockSpec(memory_space=pltpu.VMEM)] * len(after),
        out_shape=outs,
        scratch_shapes=list(scratch),
        compiler_params=PARAMS,
        name=name,
        cost_estimate=pl.CostEstimate(flops=flops, bytes_accessed=moved, transcendentals=0),
    )(*args, *after)


def exchange(array):
    return lax.all_to_all(array, "seq", 0, 0, tiled=True)


def body(cotangent, queries, key_proj, value_proj, log_decay, out_weight):
    tokens, cols = queries.shape
    share = out_weight.shape[0]
    half = share // 2
    features = NZ * share
    row = shape((tokens, cols))
    row32 = shape((tokens, cols), F32)
    piece = shape((share, cols))
    state = shape((N_SEQ, ROWS, HEAD_DIM))

    below, above = [send(out_weight, Z_UP)], [send(out_weight, Z_DOWN)]

    log_decay = jnp.transpose(log_decay)
    terms = pl.pallas_call(
        key_terms_kernel,
        in_specs=[pl.BlockSpec(memory_space=pltpu.VMEM)] + [pl.BlockSpec(memory_space=pltpu.HBM)] * 2,
        out_shape=shape((N_SEQ, ROWS + 16, HEAD_DIM)),
        scratch_shapes=[pltpu.VMEM((tokens, cols), BF)] * 2 + [pltpu.SemaphoreType.DMA((2,))],
        compiler_params=PARAMS,
        name="key_terms",
        cost_estimate=pl.CostEstimate(flops=40_000_000, bytes_accessed=1_000_000, transcendentals=0),
    )(log_decay, key_proj, value_proj)
    parts = call(
        cotangent_kernel, (shape((2 * share, tokens)),) * 2, "cotangent_parts", 40_000_000_000, 400_000,
        (cotangent,), (below[0], above[0]),
    )
    below.append(send(below[0], Z_UP))
    above.append(send(above[0], Z_DOWN))
    pieces = []
    for a in range(2):
        for b in range(2):
            table = pairs(lambda yl, z, c, yh, x, a=a, b=b: (yh, z, c ^ a, yl ^ b, x))
            pieces.append(send(parts[a], table))
    gathered = exchange(terms)
    own = call(collect_kernel, shape((2 * share, 4 * tokens)), "collect", 0, 800_000, pieces)
    left, right = send(own, X_UP), send(own, X_DOWN)

    befores = call(
        functools.partial(recurrence_kernel, False), state, "states_before", 1_000_000, 1_000_000,
        (gathered, gathered),
    )
    states = exchange(befores).reshape(cols, HEAD_DIM)
    attended, scores = call(
        attended_kernel, (row, row), "attended", 110_000_000, 2_000_000,
        (log_decay, queries, key_proj, value_proj, states), (below[1], above[1]),
    )
    below.append(send(below[1], Z_UP))
    above.append(send(above[1], Z_DOWN))
    att_below, att_above = [send(attended, Z_UP)], [send(attended, Z_DOWN)]
    opposite = send(left, X_UP)
    block_t = call(
        functools.partial(assemble_kernel, share), shape((4 * tokens, features)), "assemble",
        1_000_000, 3_000_000, (own, left, right, opposite),
        scratch=[pltpu.VMEM((features, 4 * tokens), BF)],
    )
    far_low = send(below[2][:half], Z_UP)
    far_high = send(above[2][half:], Z_DOWN)
    for _ in range(2):
        att_below.append(send(att_below[-1], Z_UP))
        att_above.append(send(att_above[-1], Z_DOWN))
    att_low = send(att_below[2][: tokens // 2], Z_UP)
    att_high = send(att_above[2][tokens // 2 :], Z_DOWN)

    halves = call(
        halves_kernel, (shape((2 * share, tokens)),) * 2, "cotangent_halves", 0, 400_000,
        (cotangent,), (own,),
    )
    turned = []
    for r in range(2):
        table = pairs(
            lambda yl, z, c, yh, x, r=r: (yl, 2 * x + ((z % 2) ^ r), c, yh, z // 2)
        )
        turned.append(send(halves[r], table))
    pair = call(pair_kernel, shape((2 * share, 2 * tokens)), "pair", 0, 400_000, turned)
    joined = call(
        join_kernel, shape((4 * share, 2 * tokens)), "join", 0, 800_000, (*turned, send(pair, Y_HI))
    )
    joined_left, joined_right = send(joined, X_UP), send(joined, X_DOWN)
    joined_opposite = send(joined_left, X_UP)
    block = call(
        functools.partial(assemble_weight_kernel, share), shape((4 * share, NZ * tokens)),
        "assemble_weight", 1_000_000, 3_000_000,
        (joined, joined_left, joined_right, joined_opposite),
    )

    weights = [out_weight] + above + [far_low, far_high] + below[::-1]
    kept, theirs, cross, cross_theirs = call(
        project_kernel, (row32, row32, row, row), "project", 1_600_000_000, 6_000_000,
        (block_t, *weights), scratch=[pltpu.VMEM((features, cols // TILES), BF)],
    )
    from_core_theirs = send(cross_theirs, CORE)
    from_core = send(cross, CORE)
    passed = call(add_kernel, row, "sum_theirs", 100_000, 1_000_000, (theirs, from_core_theirs))
    arrived = send(passed, Y_LO)
    grad_attn, query_terms = call(
        query_terms_kernel, (row, state), "query_terms", 40_000_000, 1_000_000,
        (log_decay, queries, kept, from_core, arrived),
    )
    returned = exchange(query_terms)
    afters = call(
        functools.partial(recurrence_kernel, True), state, "states_after", 1_000_000, 1_000_000,
        (gathered, returned),
    )
    after = exchange(afters).reshape(cols, HEAD_DIM)
    grad_queries, inner_k, inner_v = call(
        inner_grads_kernel, (row, row32, row32), "inner_grads", 200_000_000, 3_000_000,
        (log_decay, queries, key_proj, value_proj, grad_attn, scores, states),
    )

    attendeds = [attended] + att_above + [att_low, att_high] + att_below[::-1]
    piece32 = shape((share, cols), F32)
    w_kept, w_theirs, w_cross, w_cross_theirs = call(
        weight_kernel, (piece32, piece32, piece, piece), "weight_terms", 1_600_000_000, 6_000_000,
        (block, *attendeds), scratch=[pltpu.VMEM((NZ * tokens, cols // TILES), BF)],
    )
    w_from_core_theirs = send(w_cross_theirs, CORE)
    w_from_core = send(w_cross, CORE)
    w_passed = call(
        add_kernel, piece, "sum_weight_theirs", 200_000, 1_500_000, (w_theirs, w_from_core_theirs)
    )
    w_arrived = send(w_passed, Y_LO)
    grad_weight = call(
        last_add_kernel, piece, "weight_sum", 400_000, 2_000_000, (w_kept, w_from_core, w_arrived)
    )
    grad_keys, grad_values = call(
        outer_grads_kernel, (row, row), "outer_grads", 70_000_000, 3_000_000,
        (log_decay, key_proj, value_proj, inner_k, inner_v, after),
    )
    return grad_queries, grad_keys, grad_values, grad_weight


def solution(mesh):
    placed = P("seq", "head")
    return jax.shard_map(
        body,
        mesh=mesh,
        in_specs=(placed,) * 6,
        out_specs=(placed,) * 4,
        check_vma=False,
    )
```

```python
import functools

import jax
import jax.numpy as jnp
from jax import lax
from jax.experimental import pallas as pl
from jax.experimental.pallas import tpu as pltpu
from jax.sharding import PartitionSpec as P

HEAD_DIM = 128
BLOCK = 128
HEADS_LOCAL = 8
CHIPS = 16
HALF_ROWS = 512
ROWS = 32
NZ = 8
TILES = 4
BF = jnp.bfloat16
F32 = jnp.float32
AXES = ("seq", "head")
PARAMS = pltpu.CompilerParams(vmem_limit_bytes=16 * 1024 * 1024)


def pairs(move):
    out = []
    for yl in range(2):
        for z in range(8):
            for c in range(2):
                for yh in range(2):
                    for x in range(4):
                        a, b, d, e, f = move(yl, z, c, yh, x)
                        out.append(
                            (
                                (yl * 16 + z * 2 + c) * 8 + yh * 4 + x,
                                (a * 16 + (b % 8) * 2 + d) * 8 + e * 4 + f % 4,
                            )
                        )
    return out


Z_UP = pairs(lambda yl, z, c, yh, x: (yl, z + 1, c, yh, x))
Z_DOWN = pairs(lambda yl, z, c, yh, x: (yl, z + 7, c, yh, x))
X_UP = pairs(lambda yl, z, c, yh, x: (yl, z, c, yh, x + 1))
X_DOWN = pairs(lambda yl, z, c, yh, x: (yl, z, c, yh, x + 3))
CORE = pairs(lambda yl, z, c, yh, x: (yl, z, 1 - c, yh, x))
Y_LO = pairs(lambda yl, z, c, yh, x: (1 - yl, z, c, yh, x))


CHIP_GROUPS = [[2 * p + c for p in range(CHIPS)] for c in range(2)]


def send(array, table):
    return lax.ppermute(array, AXES, table)


def mm(a, b, ca, cb):
    return lax.dot_general(a, b, (((ca,), (cb,)), ((), ())), preferred_element_type=F32)


def coordinates():
    seq, head = lax.axis_index("seq"), lax.axis_index("head")
    y_lo = seq // 16
    rest = seq - 16 * y_lo
    z = rest // 2
    core = rest - 2 * z
    y_hi = head // 4
    return y_lo, z, core, y_hi, head - 4 * y_hi


def flip_bit():
    y_lo, _, _, y_hi, _ = coordinates()
    return y_lo + y_hi - 2 * y_lo * y_hi


def within_columns(decay):
    at = lax.broadcasted_iota(jnp.int32, (BLOCK, BLOCK), 0)
    of = lax.broadcasted_iota(jnp.int32, (BLOCK, BLOCK), 1)
    lower = (of <= at).astype(F32)
    return lax.dot_general(
        lower, decay, (((1,), (1,)), ((), ())),
        precision=lax.Precision.HIGHEST, preferred_element_type=F32,
    )


def causal_mask(within_col):
    gaps = within_col - jnp.transpose(within_col)
    at = lax.broadcasted_iota(jnp.int32, (BLOCK, BLOCK), 0)
    of = lax.broadcasted_iota(jnp.int32, (BLOCK, BLOCK), 1)
    return jnp.exp(jnp.where(at >= of, gaps, -jnp.inf))


def head_cols(h):
    return pl.ds(h * HEAD_DIM, HEAD_DIM)


def cotangent_kernel(cot_ref, *rest):
    same_ref, swap_ref = rest[-2:]
    _, _, core, _, _ = coordinates()
    turned = jnp.transpose(cot_ref[...])
    share = turned.shape[0] // 4
    for i in range(2):
        first = turned[(2 * i) * share : (2 * i + 1) * share]
        second = turned[(2 * i + 1) * share : (2 * i + 2) * share]
        rows = pl.ds(i * share, share)

        @pl.when(core == 0)
        def _():
            same_ref[rows, :] = first
            swap_ref[rows, :] = second

        @pl.when(core == 1)
        def _():
            same_ref[rows, :] = second
            swap_ref[rows, :] = first


def key_terms_kernel(decay_ref, key_hbm, value_hbm, mine_ref, cross_ref, key_ref, value_ref, sems):
    copies = (
        pltpu.make_async_copy(key_hbm, key_ref, sems.at[0]),
        pltpu.make_async_copy(value_hbm, value_ref, sems.at[1]),
    )
    for copy in copies:
        copy.start()
    within = within_columns(decay_ref[...])
    for copy in copies:
        copy.wait()
    _, _, core, _, _ = coordinates()
    row = lax.broadcasted_iota(jnp.int32, (16, HEAD_DIM), 0)
    for half in range(2):
        decays = jnp.zeros((16, HEAD_DIM), F32)
        for i in range(4):
            h = 4 * half + i
            col = within[:, h : h + 1]
            last = col[BLOCK - 1 : BLOCK]
            scaled = (jnp.exp(last - col) * key_ref[:, head_cols(h)].astype(F32)).astype(BF)
            terms = mm(scaled, value_ref[:, head_cols(h)], 0, 0).astype(BF)
            decays = put_parts(decays, row, 3 * i, last)
            store_half(core, half, i, terms, mine_ref, cross_ref)
        decays = decays.astype(BF)
        rows = pl.ds(HALF_ROWS, 16)

        @pl.when(core == half)
        def _():
            mine_ref[rows, :] = decays

        @pl.when(core != half)
        def _():
            cross_ref[rows, :] = decays


def put_parts(decays, row, at, value):
    high = value.astype(BF).astype(F32)
    middle = (value - high).astype(BF).astype(F32)
    low = value - high - middle
    decays = jnp.where(row == at, high, decays)
    decays = jnp.where(row == at + 1, middle, decays)
    return jnp.where(row == at + 2, low, decays)


def add_parts(decays, at):
    return decays[at : at + 1] + (decays[at + 1 : at + 2] + decays[at + 2 : at + 3])


def store_half(core, half, i, value, mine_ref, cross_ref):
    rows = pl.ds(i * HEAD_DIM, HEAD_DIM)

    @pl.when(core == half)
    def _():
        mine_ref[rows, :] = value

    @pl.when(core != half)
    def _():
        cross_ref[rows, :] = value


def merge_kernel(lead, mine_decay_ref, other_decay_ref, mine_ref, other_ref, *rest):
    out_ref = rest[-1]
    _, _, core, _, _ = coordinates()
    row = lax.broadcasted_iota(jnp.int32, (16, HEAD_DIM), 0)
    mine_decays = mine_decay_ref[HALF_ROWS : HALF_ROWS + 16, :].astype(F32)
    other_decays = other_decay_ref[HALF_ROWS : HALF_ROWS + 16, :].astype(F32)
    for j in range(4):
        rows = slice(j * HEAD_DIM, (j + 1) * HEAD_DIM)
        mine_decay, other_decay = add_parts(mine_decays, 3 * j), add_parts(other_decays, 3 * j)
        mine, other = mine_ref[rows, :].astype(F32), other_ref[rows, :].astype(F32)
        is_lead = core == lead
        mine = mine * jnp.where(is_lead, jnp.exp(other_decay), 1.0)
        other = other * jnp.where(is_lead, 1.0, jnp.exp(mine_decay))
        terms = (mine + other).astype(BF)
        for i in range(4):
            out_ref[4 * j + i, 0:ROWS, :] = terms[i * ROWS : (i + 1) * ROWS]
        if out_ref.shape[1] > ROWS:
            parts = put_parts(jnp.zeros((16, HEAD_DIM), F32), row, 0, mine_decay + other_decay)
            parts = parts.astype(BF)
            for i in range(4):
                out_ref[4 * j + i, ROWS : ROWS + 16, :] = parts


def spread_kernel(
    lead, mine_decay_ref, other_decay_ref, mine_ref, other_ref, state_ref, *rest
):
    own_out_ref, cross_out_ref = rest[-2:]
    _, _, core, _, _ = coordinates()
    mine_decays = mine_decay_ref[HALF_ROWS : HALF_ROWS + 16, :].astype(F32)
    other_decays = other_decay_ref[HALF_ROWS : HALF_ROWS + 16, :].astype(F32)
    for j in range(4):
        rows = slice(j * HEAD_DIM, (j + 1) * HEAD_DIM)
        state = state_ref[rows, :]
        wide = state.astype(F32)
        mine_moved = jnp.exp(add_parts(mine_decays, 3 * j)) * wide + mine_ref[rows, :].astype(F32)
        other_moved = jnp.exp(add_parts(other_decays, 3 * j)) * wide + other_ref[rows, :].astype(F32)

        @pl.when(core == lead)
        def _():
            own_out_ref[rows, :] = state
            cross_out_ref[rows, :] = mine_moved.astype(BF)

        @pl.when(core != lead)
        def _():
            own_out_ref[rows, :] = other_moved.astype(BF)
            cross_out_ref[rows, :] = state


def recurrence_kernel(reverse, decay_ref, terms_ref, *rest):
    out_ref = rest[-1]
    state = jnp.zeros((ROWS, HEAD_DIM), F32)
    for k in reversed(range(CHIPS)) if reverse else range(CHIPS):
        out_ref[k] = state.astype(BF)
        factor = jnp.exp(add_parts(decay_ref[k, ROWS : ROWS + 16, :].astype(F32), 0))
        state = factor * state + terms_ref[k, 0:ROWS, :].astype(F32)


def gather_halves(own_ref, other_ref, out_ref):
    _, _, core, _, _ = coordinates()
    out_ref[pl.ds(pl.multiple_of(core * HALF_ROWS, HALF_ROWS), HALF_ROWS), :] = own_ref[...]
    out_ref[pl.ds(pl.multiple_of((1 - core) * HALF_ROWS, HALF_ROWS), HALF_ROWS), :] = other_ref[...]


def attended_kernel(decay_ref, query_ref, key_ref, value_ref, own_ref, other_ref, *rest):
    att_ref, score_ref, state_ref = rest[-3:]
    gather_halves(own_ref, other_ref, state_ref)
    within = within_columns(decay_ref[...])
    for h in range(HEADS_LOCAL):
        cols = head_cols(h)
        col = within[:, h : h + 1]
        query = query_ref[:, cols]
        scores = (mm(query, key_ref[:, cols], 1, 1) * causal_mask(col)).astype(BF)
        score_ref[:, cols] = scores
        att = jnp.exp(col) * mm(query, state_ref[pl.ds(h * HEAD_DIM, HEAD_DIM), :], 1, 0)
        att_ref[:, cols] = (att + mm(scores, value_ref[:, cols], 1, 0)).astype(BF)


def query_terms_kernel(decay_ref, query_ref, own_ref, core_ref, other_ref, *rest):
    grad_ref, mine_ref, cross_ref = rest[-3:]
    _, _, core, _, _ = coordinates()
    within = within_columns(decay_ref[...])
    for h in range(HEADS_LOCAL):
        cols = head_cols(h)
        grad = own_ref[:, cols] + core_ref[:, cols].astype(F32) + other_ref[:, cols].astype(F32)
        grad = grad.astype(BF)
        grad_ref[:, cols] = grad
        scaled = (jnp.exp(within[:, h : h + 1]) * query_ref[:, cols].astype(F32)).astype(BF)
        terms = mm(scaled, grad, 0, 0).astype(BF)
        store_half(core, h // 4, h % 4, terms, mine_ref, cross_ref)


def inner_grads_kernel(
    decay_ref, query_ref, key_ref, value_ref, grad_ref, score_ref, state_ref, *rest
):
    gq_ref, gk_ref, gv_ref = rest[-3:]
    within = within_columns(decay_ref[...])
    for h in range(HEADS_LOCAL):
        cols = head_cols(h)
        col = within[:, h : h + 1]
        grad, key = grad_ref[:, cols], key_ref[:, cols]
        grad_scores = (mm(grad, value_ref[:, cols], 1, 1) * causal_mask(col)).astype(BF)
        state = state_ref[pl.ds(h * HEAD_DIM, HEAD_DIM), :]
        gq = jnp.exp(col) * mm(grad, state, 1, 1) + mm(grad_scores, key, 1, 0)
        gq_ref[:, cols] = gq.astype(BF)
        gk_ref[:, cols] = mm(grad_scores, query_ref[:, cols], 0, 0)
        gv_ref[:, cols] = mm(score_ref[:, cols], grad, 0, 0)


def outer_grads_kernel(
    decay_ref, key_ref, value_ref, inner_k_ref, inner_v_ref, own_ref, other_ref,
    gk_ref, gv_ref, after_ref,
):
    gather_halves(own_ref, other_ref, after_ref)
    within = within_columns(decay_ref[...])
    for h in range(HEADS_LOCAL):
        cols = head_cols(h)
        key_weight = jnp.exp(within[BLOCK - 1 : BLOCK, h : h + 1] - within[:, h : h + 1])
        after = after_ref[pl.ds(h * HEAD_DIM, HEAD_DIM), :]
        gk = key_weight * mm(value_ref[:, cols], after, 1, 1) + inner_k_ref[:, cols]
        gk_ref[:, cols] = gk.astype(BF)
        gv = key_weight * mm(key_ref[:, cols], after, 1, 0) + inner_v_ref[:, cols]
        gv_ref[:, cols] = gv.astype(BF)


def collect_kernel(a_ref, b_ref, c_ref, d_ref, *rest):
    out_ref = rest[-1]
    flip = flip_bit()
    for i, ref in ((flip, a_ref), (1 - flip, b_ref), (2 + flip, c_ref), (3 - flip, d_ref)):
        out_ref[:, pl.ds(pl.multiple_of(i * BLOCK, BLOCK), BLOCK)] = ref[...]


def assemble_kernel(share, own_ref, left_ref, right_ref, opposite_ref, out_ref, out_t_ref):
    _, z, _, _, x = coordinates()
    for off, ref, start, part in (
        (0, own_ref, 0, 0), (0, own_ref, share, 1),
        (1, right_ref, 0, 0), (1, right_ref, share, 1),
        (2, opposite_ref, 0, 0), (2, opposite_ref, share, 1),
        (3, left_ref, 0, 0), (3, left_ref, share, 1),
    ):
        k = (2 * ((x + off) % 4) + part - z + NZ) % NZ
        at = pl.multiple_of(k * share, 64)
        out_ref[pl.ds(at, share), :] = ref[start : start + share, :]
    for i in range(NZ * share // 256):
        rows = pl.ds(i * 256, 256)
        out_t_ref[:, rows] = jnp.transpose(out_ref[rows, :])


def project_kernel(block_ref, *refs):
    pieces, (kept_ref, theirs_ref, cross_ref, cross_theirs_ref), weight_ref = refs[:9], refs[-5:-1], refs[-1]
    width = weight_ref.shape[1]
    for tile in range(kept_ref.shape[1] // width):
        cols = slice(tile * width, (tile + 1) * width)
        at = 0
        for ref in pieces:
            weight_ref[at : at + ref.shape[0], :] = ref[:, cols]
            at += ref.shape[0]
        out = mm(block_ref[...], weight_ref[...], 1, 0)
        kept_ref[:, cols] = out[0:BLOCK]
        theirs_ref[:, cols] = out[BLOCK : 2 * BLOCK]
        cross_ref[:, cols] = out[2 * BLOCK : 3 * BLOCK].astype(BF)
        cross_theirs_ref[:, cols] = out[3 * BLOCK : 4 * BLOCK].astype(BF)


def weight_kernel(block_ref, own_ref, neighbour_ref, across_ref, diagonal_ref, *rest):
    outs, tokens_ref = rest[-10:-1], rest[-1]
    width = tokens_ref.shape[1]
    for tile in range(own_ref.shape[1] // width):
        cols = slice(tile * width, (tile + 1) * width)
        for i, ref in enumerate((own_ref, neighbour_ref, across_ref, diagonal_ref)):
            tokens_ref[i * BLOCK : (i + 1) * BLOCK, :] = ref[:, cols]
        at = 0
        for ref in outs:
            rows = slice(at, at + ref.shape[0])
            ref[:, cols] = mm(block_ref[rows, :], tokens_ref[...], 1, 0).astype(BF)
            at += ref.shape[0]


def add_kernel(a_ref, b_ref, out_ref):
    out_ref[...] = (a_ref[...].astype(F32) + b_ref[...].astype(F32)).astype(BF)


def first_adds_kernel(up_part_ref, up_ref, down_part_ref, down_ref, *rest):
    up_out_ref, down_out_ref = rest[-2:]
    half = up_ref.shape[0]
    up_out_ref[:half] = (up_part_ref[:half].astype(F32) + up_ref[...].astype(F32)).astype(BF)
    up_out_ref[half:] = up_part_ref[half:]
    down_out_ref[:half] = down_part_ref[:half]
    down_out_ref[half:] = (down_part_ref[half:].astype(F32) + down_ref[...].astype(F32)).astype(BF)


def adds_kernel(up_part_ref, up_ref, down_part_ref, down_ref, *rest):
    up_out_ref, down_out_ref = rest[-2:]
    up_out_ref[...] = (up_part_ref[...].astype(F32) + up_ref[...].astype(F32)).astype(BF)
    down_out_ref[...] = (down_part_ref[...].astype(F32) + down_ref[...].astype(F32)).astype(BF)


def last_add_kernel(part_ref, up_ref, down_ref, out_ref):
    out_ref[...] = (
        part_ref[...].astype(F32) + (up_ref[...].astype(F32) + down_ref[...].astype(F32))
    ).astype(BF)


def shape(dims, dtype=BF):
    return jax.ShapeDtypeStruct(dims, dtype)


def call(body, outs, name, flops, moved, args, after=(), scratch=()):
    return pl.pallas_call(
        body,
        in_specs=[pl.BlockSpec(a.shape, lambda n=a.ndim: (0,) * n) for a in args]
        + [pl.BlockSpec(memory_space=pltpu.VMEM)] * len(after),
        out_shape=outs,
        scratch_shapes=list(scratch),
        compiler_params=PARAMS,
        name=name,
        cost_estimate=pl.CostEstimate(flops=flops, bytes_accessed=moved, transcendentals=0),
    )(*args, *after)


def exchange(array):
    return lax.all_to_all(array, "seq", 0, 0, tiled=True, axis_index_groups=CHIP_GROUPS)


def body(cotangent, queries, key_proj, value_proj, log_decay, out_weight):
    tokens, cols = queries.shape
    share = out_weight.shape[0]
    half = share // 2
    features = NZ * share
    row = shape((tokens, cols))
    row32 = shape((tokens, cols), F32)
    piece = shape((share, cols))
    slices = shape((CHIPS, ROWS, HEAD_DIM))
    half_state = shape((HALF_ROWS, HEAD_DIM))
    tagged = shape((HALF_ROWS + 16, HEAD_DIM))

    below, above = [send(out_weight, Z_UP)], [send(out_weight, Z_DOWN)]

    log_decay = jnp.transpose(log_decay)
    key_mine, key_cross = pl.pallas_call(
        key_terms_kernel,
        in_specs=[pl.BlockSpec(memory_space=pltpu.VMEM)] + [pl.BlockSpec(memory_space=pltpu.HBM)] * 2,
        out_shape=(tagged, tagged),
        scratch_shapes=[pltpu.VMEM((tokens, cols), BF)] * 2 + [pltpu.SemaphoreType.DMA((2,))],
        compiler_params=PARAMS,
        name="key_terms",
        cost_estimate=pl.CostEstimate(flops=40_000_000, bytes_accessed=1_000_000, transcendentals=0),
    )(log_decay, key_proj, value_proj)
    key_other = send(key_cross, CORE)
    merged = call(
        functools.partial(merge_kernel, 0), shape((CHIPS, ROWS + 16, HEAD_DIM)), "merge_keys",
        1_000_000, 500_000, (key_mine, key_other, key_mine, key_other),
    )
    parts = call(
        cotangent_kernel, (shape((2 * share, tokens)),) * 2, "cotangent_parts", 40_000_000_000, 400_000,
        (cotangent,), (below[0], above[0], merged),
    )
    below.append(send(below[0], Z_UP))
    above.append(send(above[0], Z_DOWN))
    pieces = []
    for a in range(2):
        for b in range(2):
            table = pairs(lambda yl, z, c, yh, x, a=a, b=b: (yh, z, c ^ a, yl ^ b, x))
            pieces.append(send(parts[a], table))
    gathered = exchange(merged)

    befores = call(
        functools.partial(recurrence_kernel, False), slices, "states_before", 1_000_000, 1_000_000,
        (gathered, gathered),
    )
    own = call(collect_kernel, shape((2 * share, 4 * tokens)), "collect", 0, 800_000, pieces, (befores,))
    left, right = send(own, X_UP), send(own, X_DOWN)
    before = exchange(befores).reshape(HALF_ROWS, HEAD_DIM)
    before_own, before_cross = call(
        functools.partial(spread_kernel, 0), (half_state, half_state), "spread_before",
        20_000_000_000, 500_000, (key_mine, key_other, key_mine, key_other, before),
    )
    before_other = send(before_cross, CORE)
    attended, scores, states = call(
        attended_kernel, (row, row, shape((cols, HEAD_DIM))), "attended", 110_000_000, 2_000_000,
        (log_decay, queries, key_proj, value_proj, before_own, before_other), (below[1], above[1]),
    )
    below.append(send(below[-1], Z_UP))
    above.append(send(above[-1], Z_DOWN))
    across = send(attended, CORE)
    neighbour = send(attended, Y_LO)
    opposite = send(left, X_UP)
    block, block_t = call(
        functools.partial(assemble_kernel, share),
        (shape((features, 4 * tokens)), shape((4 * tokens, features))), "assemble",
        1_000_000, 5_000_000, (own, left, right, opposite),
    )
    diagonal = send(neighbour, CORE)
    far_low = send(below[2][:half], Z_UP)
    far_high = send(above[2][half:], Z_DOWN)

    weights = [out_weight] + above + [far_low, far_high] + below[::-1]
    kept, theirs, cross, cross_theirs = pl.pallas_call(
        project_kernel,
        out_shape=[row32, row32, row, row],
        scratch_shapes=[pltpu.VMEM((features, cols // TILES), BF)],
        compiler_params=PARAMS,
        name="project",
        cost_estimate=pl.CostEstimate(
            flops=1_600_000_000, bytes_accessed=6_000_000, transcendentals=0
        ),
    )(block_t, *weights)
    from_core_theirs = send(cross_theirs, CORE)
    from_core = send(cross, CORE)
    passed = call(add_kernel, row, "sum_theirs", 100_000, 1_000_000, (theirs, from_core_theirs))
    arrived = send(passed, Y_LO)

    part = pl.pallas_call(
        weight_kernel,
        in_specs=[pl.BlockSpec(memory_space=pltpu.VMEM)] * 6,
        out_shape=[piece] * 4 + [shape((half, cols))] * 2 + [piece] * 3,
        scratch_shapes=[pltpu.VMEM((4 * tokens, cols // TILES), BF)],
        compiler_params=PARAMS,
        name="weight_partial",
        cost_estimate=pl.CostEstimate(
            flops=1_600_000_000, bytes_accessed=6_000_000, transcendentals=0
        ),
    )(block, attended, neighbour, across, diagonal, passed)
    up, down = send(part[4], Z_UP), send(part[5], Z_DOWN)

    grad_attn, query_mine, query_cross = call(
        query_terms_kernel, (row, half_state, half_state), "query_terms", 40_000_000, 1_000_000,
        (log_decay, queries, kept, from_core, arrived),
    )
    up, down = call(
        first_adds_kernel, (piece, piece), "ring_sum_3", 400_000, 2_000_000,
        (part[3], up, part[6], down), (grad_attn,),
    )
    up, down = send(up, Z_UP), send(down, Z_DOWN)
    query_other = send(query_cross, CORE)
    query_merged = call(
        functools.partial(merge_kernel, 1), slices, "merge_queries", 1_000_000, 500_000,
        (key_mine, key_other, query_mine, query_other),
    )
    returned = exchange(query_merged)
    up, down = call(
        adds_kernel, (piece, piece), "ring_sum_2", 400_000, 2_000_000, (part[2], up, part[7], down),
        (query_merged,),
    )
    afters = call(
        functools.partial(recurrence_kernel, True), slices, "states_after", 1_000_000, 1_000_000,
        (gathered, returned), (up, down),
    )
    up, down = send(up, Z_UP), send(down, Z_DOWN)
    after = exchange(afters).reshape(HALF_ROWS, HEAD_DIM)
    grad_queries, inner_k, inner_v = call(
        inner_grads_kernel, (row, row32, row32), "inner_grads", 25_000_000_000, 3_000_000,
        (log_decay, queries, key_proj, value_proj, grad_attn, scores, states), (afters,),
    )
    after_own, after_cross = call(
        functools.partial(spread_kernel, 1), (half_state, half_state), "spread_after",
        25_000_000_000, 500_000, (key_mine, key_other, query_mine, query_other, after), (inner_k,),
    )
    after_other = send(after_cross, CORE)
    up, down = call(
        adds_kernel, (piece, piece), "ring_sum_1", 400_000, 2_000_000, (part[1], up, part[8], down),
        (inner_k,),
    )
    up, down = send(up, Z_UP), send(down, Z_DOWN)
    grad_keys, grad_values = call(
        outer_grads_kernel, (row, row), "outer_grads", 70_000_000, 3_000_000,
        (log_decay, key_proj, value_proj, inner_k, inner_v, after_own, after_other),
        scratch=[pltpu.VMEM((cols, HEAD_DIM), BF)],
    )
    grad_weight = call(last_add_kernel, piece, "ring_sum_0", 400_000, 2_000_000, (part[0], up, down))
    return grad_queries, grad_keys, grad_values, grad_weight


def solution(mesh):
    placed = P("seq", "head")
    return jax.shard_map(
        body,
        mesh=mesh,
        in_specs=(placed,) * 6,
        out_specs=(placed,) * 4,
        check_vma=False,
    )
```

```python
import functools

import jax
import jax.numpy as jnp
from jax import lax
from jax.experimental import pallas as pl
from jax.experimental.pallas import tpu as pltpu
from jax.sharding import PartitionSpec as P

HEAD_DIM = 128
BLOCK = 128
HEADS_LOCAL = 8
CHIPS = 16
HALF_ROWS = 512
ROWS = 32
NZ = 8
TILES = 4
BF = jnp.bfloat16
F32 = jnp.float32
AXES = ("seq", "head")
PARAMS = pltpu.CompilerParams(vmem_limit_bytes=16 * 1024 * 1024)


def pairs(move):
    out = []
    for yl in range(2):
        for z in range(8):
            for c in range(2):
                for yh in range(2):
                    for x in range(4):
                        a, b, d, e, f = move(yl, z, c, yh, x)
                        out.append(
                            (
                                (yl * 16 + z * 2 + c) * 8 + yh * 4 + x,
                                (a * 16 + (b % 8) * 2 + d) * 8 + e * 4 + f % 4,
                            )
                        )
    return out


Z_UP = pairs(lambda yl, z, c, yh, x: (yl, z + 1, c, yh, x))
Z_DOWN = pairs(lambda yl, z, c, yh, x: (yl, z + 7, c, yh, x))
X_UP = pairs(lambda yl, z, c, yh, x: (yl, z, c, yh, x + 1))
X_DOWN = pairs(lambda yl, z, c, yh, x: (yl, z, c, yh, x + 3))
CORE = pairs(lambda yl, z, c, yh, x: (yl, z, 1 - c, yh, x))
Y_LO = pairs(lambda yl, z, c, yh, x: (1 - yl, z, c, yh, x))


CHIP_GROUPS = [[2 * p + c for p in range(CHIPS)] for c in range(2)]


def send(array, table):
    return lax.ppermute(array, AXES, table)


def mm(a, b, ca, cb):
    return lax.dot_general(a, b, (((ca,), (cb,)), ((), ())), preferred_element_type=F32)


def coordinates():
    seq, head = lax.axis_index("seq"), lax.axis_index("head")
    y_lo = seq // 16
    rest = seq - 16 * y_lo
    z = rest // 2
    core = rest - 2 * z
    y_hi = head // 4
    return y_lo, z, core, y_hi, head - 4 * y_hi


def flip_bit():
    y_lo, _, _, y_hi, _ = coordinates()
    return y_lo + y_hi - 2 * y_lo * y_hi


def within_columns(decay):
    at = lax.broadcasted_iota(jnp.int32, (BLOCK, BLOCK), 0)
    of = lax.broadcasted_iota(jnp.int32, (BLOCK, BLOCK), 1)
    lower = (of <= at).astype(F32)
    return lax.dot_general(
        lower, decay, (((1,), (1,)), ((), ())),
        precision=lax.Precision.HIGHEST, preferred_element_type=F32,
    )


def causal_mask(within_col):
    gaps = within_col - jnp.transpose(within_col)
    at = lax.broadcasted_iota(jnp.int32, (BLOCK, BLOCK), 0)
    of = lax.broadcasted_iota(jnp.int32, (BLOCK, BLOCK), 1)
    return jnp.exp(jnp.where(at >= of, gaps, -jnp.inf))


def head_cols(h):
    return pl.ds(h * HEAD_DIM, HEAD_DIM)


def cotangent_kernel(cot_ref, *rest):
    same_ref, swap_ref = rest[-2:]
    _, _, core, _, _ = coordinates()
    turned = jnp.transpose(cot_ref[...])
    share = turned.shape[0] // 4
    for i in range(2):
        first = turned[(2 * i) * share : (2 * i + 1) * share]
        second = turned[(2 * i + 1) * share : (2 * i + 2) * share]
        rows = pl.ds(i * share, share)

        @pl.when(core == 0)
        def _():
            same_ref[rows, :] = first
            swap_ref[rows, :] = second

        @pl.when(core == 1)
        def _():
            same_ref[rows, :] = second
            swap_ref[rows, :] = first


def key_terms_kernel(decay_ref, key_hbm, value_hbm, mine_ref, cross_ref, key_ref, value_ref, sems):
    copies = (
        pltpu.make_async_copy(key_hbm, key_ref, sems.at[0]),
        pltpu.make_async_copy(value_hbm, value_ref, sems.at[1]),
    )
    for copy in copies:
        copy.start()
    within = within_columns(decay_ref[...])
    for copy in copies:
        copy.wait()
    _, _, core, _, _ = coordinates()
    row = lax.broadcasted_iota(jnp.int32, (16, HEAD_DIM), 0)
    for half in range(2):
        decays = jnp.zeros((16, HEAD_DIM), F32)
        for i in range(4):
            h = 4 * half + i
            col = within[:, h : h + 1]
            last = col[BLOCK - 1 : BLOCK]
            scaled = (jnp.exp(last - col) * key_ref[:, head_cols(h)].astype(F32)).astype(BF)
            terms = mm(scaled, value_ref[:, head_cols(h)], 0, 0).astype(BF)
            decays = put_parts(decays, row, 3 * i, last)
            store_half(core, half, i, terms, mine_ref, cross_ref)
        decays = decays.astype(BF)
        rows = pl.ds(HALF_ROWS, 16)

        @pl.when(core == half)
        def _():
            mine_ref[rows, :] = decays

        @pl.when(core != half)
        def _():
            cross_ref[rows, :] = decays


def put_parts(decays, row, at, value):
    high = value.astype(BF).astype(F32)
    middle = (value - high).astype(BF).astype(F32)
    low = value - high - middle
    decays = jnp.where(row == at, high, decays)
    decays = jnp.where(row == at + 1, middle, decays)
    return jnp.where(row == at + 2, low, decays)


def add_parts(decays, at):
    return decays[at : at + 1] + (decays[at + 1 : at + 2] + decays[at + 2 : at + 3])


def store_half(core, half, i, value, mine_ref, cross_ref):
    rows = pl.ds(i * HEAD_DIM, HEAD_DIM)

    @pl.when(core == half)
    def _():
        mine_ref[rows, :] = value

    @pl.when(core != half)
    def _():
        cross_ref[rows, :] = value


def merge_kernel(lead, mine_decay_ref, other_decay_ref, mine_ref, other_ref, *rest):
    out_ref = rest[-1]
    _, _, core, _, _ = coordinates()
    row = lax.broadcasted_iota(jnp.int32, (16, HEAD_DIM), 0)
    mine_decays = mine_decay_ref[HALF_ROWS : HALF_ROWS + 16, :].astype(F32)
    other_decays = other_decay_ref[HALF_ROWS : HALF_ROWS + 16, :].astype(F32)
    for j in range(4):
        rows = slice(j * HEAD_DIM, (j + 1) * HEAD_DIM)
        mine_decay, other_decay = add_parts(mine_decays, 3 * j), add_parts(other_decays, 3 * j)
        mine, other = mine_ref[rows, :].astype(F32), other_ref[rows, :].astype(F32)
        is_lead = core == lead
        mine = mine * jnp.where(is_lead, jnp.exp(other_decay), 1.0)
        other = other * jnp.where(is_lead, 1.0, jnp.exp(mine_decay))
        terms = (mine + other).astype(BF)
        for i in range(4):
            out_ref[4 * j + i, 0:ROWS, :] = terms[i * ROWS : (i + 1) * ROWS]
        if out_ref.shape[1] > ROWS:
            parts = put_parts(jnp.zeros((16, HEAD_DIM), F32), row, 0, mine_decay + other_decay)
            parts = parts.astype(BF)
            for i in range(4):
                out_ref[4 * j + i, ROWS : ROWS + 16, :] = parts


def spread_kernel(
    lead, mine_decay_ref, other_decay_ref, mine_ref, other_ref, state_ref, *rest
):
    own_out_ref, cross_out_ref = rest[-2:]
    _, _, core, _, _ = coordinates()
    mine_decays = mine_decay_ref[HALF_ROWS : HALF_ROWS + 16, :].astype(F32)
    other_decays = other_decay_ref[HALF_ROWS : HALF_ROWS + 16, :].astype(F32)
    for j in range(4):
        rows = slice(j * HEAD_DIM, (j + 1) * HEAD_DIM)
        state = state_ref[rows, :]
        wide = state.astype(F32)
        mine_moved = jnp.exp(add_parts(mine_decays, 3 * j)) * wide + mine_ref[rows, :].astype(F32)
        other_moved = jnp.exp(add_parts(other_decays, 3 * j)) * wide + other_ref[rows, :].astype(F32)

        @pl.when(core == lead)
        def _():
            own_out_ref[rows, :] = state
            cross_out_ref[rows, :] = mine_moved.astype(BF)

        @pl.when(core != lead)
        def _():
            own_out_ref[rows, :] = other_moved.astype(BF)
            cross_out_ref[rows, :] = state


def recurrence_kernel(reverse, decay_ref, terms_ref, *rest):
    out_ref = rest[-1]
    state = jnp.zeros((ROWS, HEAD_DIM), F32)
    for k in reversed(range(CHIPS)) if reverse else range(CHIPS):
        out_ref[k] = state.astype(BF)
        factor = jnp.exp(add_parts(decay_ref[k, ROWS : ROWS + 16, :].astype(F32), 0))
        state = factor * state + terms_ref[k, 0:ROWS, :].astype(F32)


def gather_halves(own_ref, other_ref, out_ref):
    _, _, core, _, _ = coordinates()
    out_ref[pl.ds(pl.multiple_of(core * HALF_ROWS, HALF_ROWS), HALF_ROWS), :] = own_ref[...]
    out_ref[pl.ds(pl.multiple_of((1 - core) * HALF_ROWS, HALF_ROWS), HALF_ROWS), :] = other_ref[...]


def attended_kernel(decay_ref, query_ref, key_ref, value_ref, own_ref, other_ref, *rest):
    att_ref, score_ref, state_ref = rest[-3:]
    gather_halves(own_ref, other_ref, state_ref)
    within = within_columns(decay_ref[...])
    for h in range(HEADS_LOCAL):
        cols = head_cols(h)
        col = within[:, h : h + 1]
        query = query_ref[:, cols]
        scores = (mm(query, key_ref[:, cols], 1, 1) * causal_mask(col)).astype(BF)
        score_ref[:, cols] = scores
        att = jnp.exp(col) * mm(query, state_ref[pl.ds(h * HEAD_DIM, HEAD_DIM), :], 1, 0)
        att_ref[:, cols] = (att + mm(scores, value_ref[:, cols], 1, 0)).astype(BF)


def query_terms_kernel(decay_ref, query_ref, own_ref, core_ref, other_ref, *rest):
    grad_ref, mine_ref, cross_ref = rest[-3:]
    _, _, core, _, _ = coordinates()
    within = within_columns(decay_ref[...])
    for h in range(HEADS_LOCAL):
        cols = head_cols(h)
        grad = own_ref[:, cols] + core_ref[:, cols].astype(F32) + other_ref[:, cols].astype(F32)
        grad = grad.astype(BF)
        grad_ref[:, cols] = grad
        scaled = (jnp.exp(within[:, h : h + 1]) * query_ref[:, cols].astype(F32)).astype(BF)
        terms = mm(scaled, grad, 0, 0).astype(BF)
        store_half(core, h // 4, h % 4, terms, mine_ref, cross_ref)


def inner_grads_kernel(
    decay_ref, query_ref, key_ref, value_ref, grad_ref, score_ref, state_ref, *rest
):
    gq_ref, gk_ref, gv_ref = rest[-3:]
    within = within_columns(decay_ref[...])
    for h in range(HEADS_LOCAL):
        cols = head_cols(h)
        col = within[:, h : h + 1]
        grad, key = grad_ref[:, cols], key_ref[:, cols]
        grad_scores = (mm(grad, value_ref[:, cols], 1, 1) * causal_mask(col)).astype(BF)
        state = state_ref[pl.ds(h * HEAD_DIM, HEAD_DIM), :]
        gq = jnp.exp(col) * mm(grad, state, 1, 1) + mm(grad_scores, key, 1, 0)
        gq_ref[:, cols] = gq.astype(BF)
        gk_ref[:, cols] = mm(grad_scores, query_ref[:, cols], 0, 0)
        gv_ref[:, cols] = mm(score_ref[:, cols], grad, 0, 0)


def outer_grads_kernel(
    decay_ref, key_ref, value_ref, inner_k_ref, inner_v_ref, own_ref, other_ref,
    gk_ref, gv_ref, after_ref,
):
    gather_halves(own_ref, other_ref, after_ref)
    within = within_columns(decay_ref[...])
    for h in range(HEADS_LOCAL):
        cols = head_cols(h)
        key_weight = jnp.exp(within[BLOCK - 1 : BLOCK, h : h + 1] - within[:, h : h + 1])
        after = after_ref[pl.ds(h * HEAD_DIM, HEAD_DIM), :]
        gk = key_weight * mm(value_ref[:, cols], after, 1, 1) + inner_k_ref[:, cols]
        gk_ref[:, cols] = gk.astype(BF)
        gv = key_weight * mm(key_ref[:, cols], after, 1, 0) + inner_v_ref[:, cols]
        gv_ref[:, cols] = gv.astype(BF)


def collect_kernel(a_ref, b_ref, c_ref, d_ref, *rest):
    out_ref = rest[-1]
    flip = flip_bit()
    for i, ref in ((flip, a_ref), (1 - flip, b_ref), (2 + flip, c_ref), (3 - flip, d_ref)):
        out_ref[:, pl.ds(pl.multiple_of(i * BLOCK, BLOCK), BLOCK)] = ref[...]


def assemble_kernel(share, own_ref, left_ref, right_ref, opposite_ref, out_ref, out_t_ref):
    _, z, _, _, x = coordinates()
    for off, ref, start, part in (
        (0, own_ref, 0, 0), (0, own_ref, share, 1),
        (1, right_ref, 0, 0), (1, right_ref, share, 1),
        (2, opposite_ref, 0, 0), (2, opposite_ref, share, 1),
        (3, left_ref, 0, 0), (3, left_ref, share, 1),
    ):
        k = (2 * ((x + off) % 4) + part - z + NZ) % NZ
        at = pl.multiple_of(k * share, 64)
        out_ref[pl.ds(at, share), :] = ref[start : start + share, :]
    for i in range(NZ * share // 256):
        rows = pl.ds(i * 256, 256)
        out_t_ref[:, rows] = jnp.transpose(out_ref[rows, :])


def project_kernel(block_ref, *refs):
    pieces, (kept_ref, theirs_ref, cross_ref, cross_theirs_ref), weight_ref = refs[:9], refs[-5:-1], refs[-1]
    width = weight_ref.shape[1]
    for tile in range(kept_ref.shape[1] // width):
        cols = slice(tile * width, (tile + 1) * width)
        at = 0
        for ref in pieces:
            weight_ref[at : at + ref.shape[0], :] = ref[:, cols]
            at += ref.shape[0]
        out = mm(block_ref[...], weight_ref[...], 1, 0)
        kept_ref[:, cols] = out[0:BLOCK]
        theirs_ref[:, cols] = out[BLOCK : 2 * BLOCK]
        cross_ref[:, cols] = out[2 * BLOCK : 3 * BLOCK].astype(BF)
        cross_theirs_ref[:, cols] = out[3 * BLOCK : 4 * BLOCK].astype(BF)


def weight_kernel(block_ref, own_ref, neighbour_ref, across_ref, diagonal_ref, *rest):
    outs, tokens_ref = rest[-10:-1], rest[-1]
    width = tokens_ref.shape[1]
    for tile in range(own_ref.shape[1] // width):
        cols = slice(tile * width, (tile + 1) * width)
        for i, ref in enumerate((own_ref, neighbour_ref, across_ref, diagonal_ref)):
            tokens_ref[i * BLOCK : (i + 1) * BLOCK, :] = ref[:, cols]
        at = 0
        for ref in outs:
            rows = slice(at, at + ref.shape[0])
            ref[:, cols] = mm(block_ref[rows, :], tokens_ref[...], 1, 0).astype(BF)
            at += ref.shape[0]


def add_kernel(a_ref, b_ref, out_ref):
    out_ref[...] = (a_ref[...].astype(F32) + b_ref[...].astype(F32)).astype(BF)


def first_adds_kernel(up_part_ref, up_ref, down_part_ref, down_ref, *rest):
    up_out_ref, down_out_ref = rest[-2:]
    half = up_ref.shape[0]
    up_out_ref[:half] = (up_part_ref[:half].astype(F32) + up_ref[...].astype(F32)).astype(BF)
    up_out_ref[half:] = up_part_ref[half:]
    down_out_ref[:half] = down_part_ref[:half]
    down_out_ref[half:] = (down_part_ref[half:].astype(F32) + down_ref[...].astype(F32)).astype(BF)


def adds_kernel(up_part_ref, up_ref, down_part_ref, down_ref, *rest):
    up_out_ref, down_out_ref = rest[-2:]
    up_out_ref[...] = (up_part_ref[...].astype(F32) + up_ref[...].astype(F32)).astype(BF)
    down_out_ref[...] = (down_part_ref[...].astype(F32) + down_ref[...].astype(F32)).astype(BF)


def last_add_kernel(part_ref, up_ref, down_ref, out_ref):
    out_ref[...] = (
        part_ref[...].astype(F32) + (up_ref[...].astype(F32) + down_ref[...].astype(F32))
    ).astype(BF)


def shape(dims, dtype=BF):
    return jax.ShapeDtypeStruct(dims, dtype)


def call(body, outs, name, flops, moved, args, after=(), scratch=()):
    return pl.pallas_call(
        body,
        in_specs=[pl.BlockSpec(a.shape, lambda n=a.ndim: (0,) * n) for a in args]
        + [pl.BlockSpec(memory_space=pltpu.VMEM)] * len(after),
        out_shape=outs,
        scratch_shapes=list(scratch),
        compiler_params=PARAMS,
        name=name,
        cost_estimate=pl.CostEstimate(flops=flops, bytes_accessed=moved, transcendentals=0),
    )(*args, *after)


def exchange(array):
    return lax.all_to_all(array, "seq", 0, 0, tiled=True, axis_index_groups=CHIP_GROUPS)


def body(cotangent, queries, key_proj, value_proj, log_decay, out_weight):
    tokens, cols = queries.shape
    share = out_weight.shape[0]
    half = share // 2
    features = NZ * share
    row = shape((tokens, cols))
    row32 = shape((tokens, cols), F32)
    piece = shape((share, cols))
    slices = shape((CHIPS, ROWS, HEAD_DIM))
    half_state = shape((HALF_ROWS, HEAD_DIM))
    tagged = shape((HALF_ROWS + 16, HEAD_DIM))

    below, above = [send(out_weight, Z_UP)], [send(out_weight, Z_DOWN)]

    log_decay = jnp.transpose(log_decay)
    key_mine, key_cross = pl.pallas_call(
        key_terms_kernel,
        in_specs=[pl.BlockSpec(memory_space=pltpu.VMEM)] + [pl.BlockSpec(memory_space=pltpu.HBM)] * 2,
        out_shape=(tagged, tagged),
        scratch_shapes=[pltpu.VMEM((tokens, cols), BF)] * 2 + [pltpu.SemaphoreType.DMA((2,))],
        compiler_params=PARAMS,
        name="key_terms",
        cost_estimate=pl.CostEstimate(flops=40_000_000, bytes_accessed=1_000_000, transcendentals=0),
    )(log_decay, key_proj, value_proj)
    key_other = send(key_cross, CORE)
    merged = call(
        functools.partial(merge_kernel, 0), shape((CHIPS, ROWS + 16, HEAD_DIM)), "merge_keys",
        1_000_000, 500_000, (key_mine, key_other, key_mine, key_other),
    )
    parts = call(
        cotangent_kernel, (shape((2 * share, tokens)),) * 2, "cotangent_parts", 40_000_000_000, 400_000,
        (cotangent,), (below[0], above[0], merged),
    )
    below.append(send(below[0], Z_UP))
    above.append(send(above[0], Z_DOWN))
    pieces = []
    for a in range(2):
        for b in range(2):
            table = pairs(lambda yl, z, c, yh, x, a=a, b=b: (yh, z, c ^ a, yl ^ b, x))
            pieces.append(send(parts[a], table))
    gathered = exchange(merged)

    befores = call(
        functools.partial(recurrence_kernel, False), slices, "states_before", 1_000_000, 1_000_000,
        (gathered, gathered),
    )
    own = call(
        collect_kernel, shape((2 * share, 4 * tokens)), "collect", 0, 800_000, pieces,
        (befores, below[1], above[1]),
    )
    left, right = send(own, X_UP), send(own, X_DOWN)
    below.append(send(below[1], Z_UP))
    above.append(send(above[1], Z_DOWN))
    before = exchange(befores).reshape(HALF_ROWS, HEAD_DIM)
    before_own, before_cross = call(
        functools.partial(spread_kernel, 0), (half_state, half_state), "spread_before",
        20_000_000_000, 500_000, (key_mine, key_other, key_mine, key_other, before), (below[2], above[2]),
    )
    before_other = send(before_cross, CORE)
    attended, scores, states = call(
        attended_kernel, (row, row, shape((cols, HEAD_DIM))), "attended", 110_000_000, 2_000_000,
        (log_decay, queries, key_proj, value_proj, before_own, before_other),
    )
    across = send(attended, CORE)
    neighbour = send(attended, Y_LO)
    opposite = send(left, X_UP)
    block, block_t = call(
        functools.partial(assemble_kernel, share),
        (shape((features, 4 * tokens)), shape((4 * tokens, features))), "assemble",
        1_000_000, 5_000_000, (own, left, right, opposite),
    )
    diagonal = send(neighbour, CORE)
    far_low = send(below[2][:half], Z_UP)
    far_high = send(above[2][half:], Z_DOWN)

    weights = [out_weight] + above + [far_low, far_high] + below[::-1]
    kept, theirs, cross, cross_theirs = pl.pallas_call(
        project_kernel,
        out_shape=[row32, row32, row, row],
        scratch_shapes=[pltpu.VMEM((features, cols // TILES), BF)],
        compiler_params=PARAMS,
        name="project",
        cost_estimate=pl.CostEstimate(
            flops=1_600_000_000, bytes_accessed=6_000_000, transcendentals=0
        ),
    )(block_t, *weights)
    from_core_theirs = send(cross_theirs, CORE)
    from_core = send(cross, CORE)
    passed = call(add_kernel, row, "sum_theirs", 100_000, 1_000_000, (theirs, from_core_theirs))
    arrived = send(passed, Y_LO)

    part = pl.pallas_call(
        weight_kernel,
        in_specs=[pl.BlockSpec(memory_space=pltpu.VMEM)] * 6,
        out_shape=[piece] * 4 + [shape((half, cols))] * 2 + [piece] * 3,
        scratch_shapes=[pltpu.VMEM((4 * tokens, cols // TILES), BF)],
        compiler_params=PARAMS,
        name="weight_partial",
        cost_estimate=pl.CostEstimate(
            flops=1_600_000_000, bytes_accessed=6_000_000, transcendentals=0
        ),
    )(block, attended, neighbour, across, diagonal, passed)
    up, down = send(part[4], Z_UP), send(part[5], Z_DOWN)

    grad_attn, query_mine, query_cross = call(
        query_terms_kernel, (row, half_state, half_state), "query_terms", 40_000_000, 1_000_000,
        (log_decay, queries, kept, from_core, arrived),
    )
    up, down = call(
        first_adds_kernel, (piece, piece), "ring_sum_3", 400_000, 2_000_000,
        (part[3], up, part[6], down), (grad_attn,),
    )
    up, down = send(up, Z_UP), send(down, Z_DOWN)
    query_other = send(query_cross, CORE)
    query_merged = call(
        functools.partial(merge_kernel, 1), slices, "merge_queries", 1_000_000, 500_000,
        (key_mine, key_other, query_mine, query_other),
    )
    returned = exchange(query_merged)
    up, down = call(
        adds_kernel, (piece, piece), "ring_sum_2", 400_000, 2_000_000, (part[2], up, part[7], down),
        (query_merged,),
    )
    afters = call(
        functools.partial(recurrence_kernel, True), slices, "states_after", 1_000_000, 1_000_000,
        (gathered, returned), (up, down),
    )
    up, down = send(up, Z_UP), send(down, Z_DOWN)
    after = exchange(afters).reshape(HALF_ROWS, HEAD_DIM)
    grad_queries, inner_k, inner_v = call(
        inner_grads_kernel, (row, row32, row32), "inner_grads", 25_000_000_000, 3_000_000,
        (log_decay, queries, key_proj, value_proj, grad_attn, scores, states), (afters,),
    )
    after_own, after_cross = call(
        functools.partial(spread_kernel, 1), (half_state, half_state), "spread_after",
        25_000_000_000, 500_000, (key_mine, key_other, query_mine, query_other, after), (inner_k,),
    )
    after_other = send(after_cross, CORE)
    up, down = call(
        adds_kernel, (piece, piece), "ring_sum_1", 400_000, 2_000_000, (part[1], up, part[8], down),
        (inner_k,),
    )
    up, down = send(up, Z_UP), send(down, Z_DOWN)
    grad_keys, grad_values = call(
        outer_grads_kernel, (row, row), "outer_grads", 70_000_000, 3_000_000,
        (log_decay, key_proj, value_proj, inner_k, inner_v, after_own, after_other),
        scratch=[pltpu.VMEM((cols, HEAD_DIM), BF)],
    )
    grad_weight = call(last_add_kernel, piece, "ring_sum_0", 400_000, 2_000_000, (part[0], up, down))
    return grad_queries, grad_keys, grad_values, grad_weight


def solution(mesh):
    placed = P("seq", "head")
    return jax.shard_map(
        body,
        mesh=mesh,
        in_specs=(placed,) * 6,
        out_specs=(placed,) * 4,
        check_vma=False,
    )
```

```python
import functools

import jax
import jax.numpy as jnp
from jax import lax
from jax.experimental import pallas as pl
from jax.experimental.pallas import tpu as pltpu
from jax.sharding import PartitionSpec as P

HEAD_DIM = 128
BLOCK = 128
HEADS_LOCAL = 8
CHIPS = 16
HALF_ROWS = 512
ROWS = 32
NZ = 8
TILES = 4
BF = jnp.bfloat16
F32 = jnp.float32
AXES = ("seq", "head")
PARAMS = pltpu.CompilerParams(vmem_limit_bytes=16 * 1024 * 1024)


def pairs(move):
    out = []
    for yl in range(2):
        for z in range(8):
            for c in range(2):
                for yh in range(2):
                    for x in range(4):
                        a, b, d, e, f = move(yl, z, c, yh, x)
                        out.append(
                            (
                                (yl * 16 + z * 2 + c) * 8 + yh * 4 + x,
                                (a * 16 + (b % 8) * 2 + d) * 8 + e * 4 + f % 4,
                            )
                        )
    return out


Z_UP = pairs(lambda yl, z, c, yh, x: (yl, z + 1, c, yh, x))
Z_DOWN = pairs(lambda yl, z, c, yh, x: (yl, z + 7, c, yh, x))
X_UP = pairs(lambda yl, z, c, yh, x: (yl, z, c, yh, x + 1))
X_DOWN = pairs(lambda yl, z, c, yh, x: (yl, z, c, yh, x + 3))
CORE = pairs(lambda yl, z, c, yh, x: (yl, z, 1 - c, yh, x))
Y_LO = pairs(lambda yl, z, c, yh, x: (1 - yl, z, c, yh, x))


CHIP_GROUPS = [[2 * p + c for p in range(CHIPS)] for c in range(2)]


def send(array, table):
    return lax.ppermute(array, AXES, table)


def mm(a, b, ca, cb):
    return lax.dot_general(a, b, (((ca,), (cb,)), ((), ())), preferred_element_type=F32)


def coordinates():
    seq, head = lax.axis_index("seq"), lax.axis_index("head")
    y_lo = seq // 16
    rest = seq - 16 * y_lo
    z = rest // 2
    core = rest - 2 * z
    y_hi = head // 4
    return y_lo, z, core, y_hi, head - 4 * y_hi


def flip_bit():
    y_lo, _, _, y_hi, _ = coordinates()
    return y_lo + y_hi - 2 * y_lo * y_hi


def within_columns(decay):
    at = lax.broadcasted_iota(jnp.int32, (BLOCK, BLOCK), 0)
    of = lax.broadcasted_iota(jnp.int32, (BLOCK, BLOCK), 1)
    lower = (of <= at).astype(F32)
    return lax.dot_general(
        lower, decay, (((1,), (1,)), ((), ())),
        precision=lax.Precision.HIGHEST, preferred_element_type=F32,
    )


def causal_mask(within_col):
    gaps = within_col - jnp.transpose(within_col)
    at = lax.broadcasted_iota(jnp.int32, (BLOCK, BLOCK), 0)
    of = lax.broadcasted_iota(jnp.int32, (BLOCK, BLOCK), 1)
    return jnp.exp(jnp.where(at >= of, gaps, -jnp.inf))


def head_cols(h):
    return pl.ds(h * HEAD_DIM, HEAD_DIM)


def cotangent_kernel(cot_ref, *rest):
    same_ref, swap_ref = rest[-2:]
    _, _, core, _, _ = coordinates()
    turned = jnp.transpose(cot_ref[...])
    share = turned.shape[0] // 4
    for i in range(2):
        first = turned[(2 * i) * share : (2 * i + 1) * share]
        second = turned[(2 * i + 1) * share : (2 * i + 2) * share]
        rows = pl.ds(i * share, share)

        @pl.when(core == 0)
        def _():
            same_ref[rows, :] = first
            swap_ref[rows, :] = second

        @pl.when(core == 1)
        def _():
            same_ref[rows, :] = second
            swap_ref[rows, :] = first


def key_terms_kernel(decay_ref, key_hbm, value_hbm, mine_ref, cross_ref, key_ref, value_ref, sems):
    copies = (
        pltpu.make_async_copy(key_hbm, key_ref, sems.at[0]),
        pltpu.make_async_copy(value_hbm, value_ref, sems.at[1]),
    )
    for copy in copies:
        copy.start()
    within = within_columns(decay_ref[...])
    for copy in copies:
        copy.wait()
    _, _, core, _, _ = coordinates()
    row = lax.broadcasted_iota(jnp.int32, (16, HEAD_DIM), 0)
    for half in range(2):
        decays = jnp.zeros((16, HEAD_DIM), F32)
        for i in range(4):
            h = 4 * half + i
            col = within[:, h : h + 1]
            last = col[BLOCK - 1 : BLOCK]
            scaled = (jnp.exp(last - col) * key_ref[:, head_cols(h)].astype(F32)).astype(BF)
            terms = mm(scaled, value_ref[:, head_cols(h)], 0, 0).astype(BF)
            decays = put_parts(decays, row, 3 * i, last)
            store_half(core, half, i, terms, mine_ref, cross_ref)
        decays = decays.astype(BF)
        rows = pl.ds(HALF_ROWS, 16)

        @pl.when(core == half)
        def _():
            mine_ref[rows, :] = decays

        @pl.when(core != half)
        def _():
            cross_ref[rows, :] = decays


def put_parts(decays, row, at, value):
    high = value.astype(BF).astype(F32)
    middle = (value - high).astype(BF).astype(F32)
    low = value - high - middle
    decays = jnp.where(row == at, high, decays)
    decays = jnp.where(row == at + 1, middle, decays)
    return jnp.where(row == at + 2, low, decays)


def add_parts(decays, at):
    return decays[at : at + 1] + (decays[at + 1 : at + 2] + decays[at + 2 : at + 3])


def store_half(core, half, i, value, mine_ref, cross_ref):
    rows = pl.ds(i * HEAD_DIM, HEAD_DIM)

    @pl.when(core == half)
    def _():
        mine_ref[rows, :] = value

    @pl.when(core != half)
    def _():
        cross_ref[rows, :] = value


def merge_kernel(lead, mine_decay_ref, other_decay_ref, mine_ref, other_ref, *rest):
    out_ref = rest[-1]
    _, _, core, _, _ = coordinates()
    row = lax.broadcasted_iota(jnp.int32, (16, HEAD_DIM), 0)
    mine_decays = mine_decay_ref[HALF_ROWS : HALF_ROWS + 16, :].astype(F32)
    other_decays = other_decay_ref[HALF_ROWS : HALF_ROWS + 16, :].astype(F32)
    for j in range(4):
        rows = slice(j * HEAD_DIM, (j + 1) * HEAD_DIM)
        mine_decay, other_decay = add_parts(mine_decays, 3 * j), add_parts(other_decays, 3 * j)
        mine, other = mine_ref[rows, :].astype(F32), other_ref[rows, :].astype(F32)
        is_lead = core == lead
        mine = mine * jnp.where(is_lead, jnp.exp(other_decay), 1.0)
        other = other * jnp.where(is_lead, 1.0, jnp.exp(mine_decay))
        terms = (mine + other).astype(BF)
        for i in range(4):
            out_ref[4 * j + i, 0:ROWS, :] = terms[i * ROWS : (i + 1) * ROWS]
        if out_ref.shape[1] > ROWS:
            parts = put_parts(jnp.zeros((16, HEAD_DIM), F32), row, 0, mine_decay + other_decay)
            parts = parts.astype(BF)
            for i in range(4):
                out_ref[4 * j + i, ROWS : ROWS + 16, :] = parts


def spread_kernel(
    lead, mine_decay_ref, other_decay_ref, mine_ref, other_ref, state_ref, *rest
):
    own_out_ref, cross_out_ref = rest[-2:]
    _, _, core, _, _ = coordinates()
    mine_decays = mine_decay_ref[HALF_ROWS : HALF_ROWS + 16, :].astype(F32)
    other_decays = other_decay_ref[HALF_ROWS : HALF_ROWS + 16, :].astype(F32)
    for j in range(4):
        rows = slice(j * HEAD_DIM, (j + 1) * HEAD_DIM)
        state = state_ref[rows, :]
        wide = state.astype(F32)
        mine_moved = jnp.exp(add_parts(mine_decays, 3 * j)) * wide + mine_ref[rows, :].astype(F32)
        other_moved = jnp.exp(add_parts(other_decays, 3 * j)) * wide + other_ref[rows, :].astype(F32)

        @pl.when(core == lead)
        def _():
            own_out_ref[rows, :] = state
            cross_out_ref[rows, :] = mine_moved.astype(BF)

        @pl.when(core != lead)
        def _():
            own_out_ref[rows, :] = other_moved.astype(BF)
            cross_out_ref[rows, :] = state


def recurrence_kernel(reverse, decay_ref, terms_ref, *rest):
    out_ref = rest[-1]
    state = jnp.zeros((ROWS, HEAD_DIM), F32)
    for k in reversed(range(CHIPS)) if reverse else range(CHIPS):
        out_ref[k] = state.astype(BF)
        factor = jnp.exp(add_parts(decay_ref[k, ROWS : ROWS + 16, :].astype(F32), 0))
        state = factor * state + terms_ref[k, 0:ROWS, :].astype(F32)


def gather_halves(own_ref, other_ref, out_ref):
    _, _, core, _, _ = coordinates()
    out_ref[pl.ds(pl.multiple_of(core * HALF_ROWS, HALF_ROWS), HALF_ROWS), :] = own_ref[...]
    out_ref[pl.ds(pl.multiple_of((1 - core) * HALF_ROWS, HALF_ROWS), HALF_ROWS), :] = other_ref[...]


def attended_kernel(decay_ref, query_ref, key_ref, value_ref, own_ref, other_ref, *rest):
    att_ref, score_ref, state_ref = rest[-3:]
    gather_halves(own_ref, other_ref, state_ref)
    within = within_columns(decay_ref[...])
    for h in range(HEADS_LOCAL):
        cols = head_cols(h)
        col = within[:, h : h + 1]
        query = query_ref[:, cols]
        scores = (mm(query, key_ref[:, cols], 1, 1) * causal_mask(col)).astype(BF)
        score_ref[:, cols] = scores
        att = jnp.exp(col) * mm(query, state_ref[pl.ds(h * HEAD_DIM, HEAD_DIM), :], 1, 0)
        att_ref[:, cols] = (att + mm(scores, value_ref[:, cols], 1, 0)).astype(BF)


def query_terms_kernel(decay_ref, query_ref, own_ref, core_ref, other_ref, *rest):
    grad_ref, mine_ref, cross_ref = rest[-3:]
    _, _, core, _, _ = coordinates()
    within = within_columns(decay_ref[...])
    for h in range(HEADS_LOCAL):
        cols = head_cols(h)
        grad = own_ref[:, cols] + core_ref[:, cols].astype(F32) + other_ref[:, cols].astype(F32)
        grad = grad.astype(BF)
        grad_ref[:, cols] = grad
        scaled = (jnp.exp(within[:, h : h + 1]) * query_ref[:, cols].astype(F32)).astype(BF)
        terms = mm(scaled, grad, 0, 0).astype(BF)
        store_half(core, h // 4, h % 4, terms, mine_ref, cross_ref)


def inner_grads_kernel(
    decay_ref, query_ref, key_ref, value_ref, grad_ref, score_ref, state_ref, *rest
):
    gq_ref, gk_ref, gv_ref = rest[-3:]
    within = within_columns(decay_ref[...])
    for h in range(HEADS_LOCAL):
        cols = head_cols(h)
        col = within[:, h : h + 1]
        grad, key = grad_ref[:, cols], key_ref[:, cols]
        grad_scores = (mm(grad, value_ref[:, cols], 1, 1) * causal_mask(col)).astype(BF)
        state = state_ref[pl.ds(h * HEAD_DIM, HEAD_DIM), :]
        gq = jnp.exp(col) * mm(grad, state, 1, 1) + mm(grad_scores, key, 1, 0)
        gq_ref[:, cols] = gq.astype(BF)
        gk_ref[:, cols] = mm(grad_scores, query_ref[:, cols], 0, 0)
        gv_ref[:, cols] = mm(score_ref[:, cols], grad, 0, 0)


def outer_grads_kernel(
    decay_ref, key_ref, value_ref, inner_k_ref, inner_v_ref, own_ref, other_ref,
    gk_ref, gv_ref, after_ref,
):
    gather_halves(own_ref, other_ref, after_ref)
    within = within_columns(decay_ref[...])
    for h in range(HEADS_LOCAL):
        cols = head_cols(h)
        key_weight = jnp.exp(within[BLOCK - 1 : BLOCK, h : h + 1] - within[:, h : h + 1])
        after = after_ref[pl.ds(h * HEAD_DIM, HEAD_DIM), :]
        gk = key_weight * mm(value_ref[:, cols], after, 1, 1) + inner_k_ref[:, cols]
        gk_ref[:, cols] = gk.astype(BF)
        gv = key_weight * mm(key_ref[:, cols], after, 1, 0) + inner_v_ref[:, cols]
        gv_ref[:, cols] = gv.astype(BF)


def collect_kernel(a_ref, b_ref, c_ref, d_ref, *rest):
    out_ref = rest[-1]
    flip = flip_bit()
    for i, ref in ((flip, a_ref), (1 - flip, b_ref), (2 + flip, c_ref), (3 - flip, d_ref)):
        out_ref[:, pl.ds(pl.multiple_of(i * BLOCK, BLOCK), BLOCK)] = ref[...]


def assemble_kernel(share, own_ref, left_ref, right_ref, opposite_ref, out_ref, out_t_ref):
    _, z, _, _, x = coordinates()
    for off, ref, start, part in (
        (0, own_ref, 0, 0), (0, own_ref, share, 1),
        (1, right_ref, 0, 0), (1, right_ref, share, 1),
        (2, opposite_ref, 0, 0), (2, opposite_ref, share, 1),
        (3, left_ref, 0, 0), (3, left_ref, share, 1),
    ):
        k = (2 * ((x + off) % 4) + part - z + NZ) % NZ
        at = pl.multiple_of(k * share, 64)
        out_ref[pl.ds(at, share), :] = ref[start : start + share, :]
    for i in range(NZ * share // 256):
        rows = pl.ds(i * 256, 256)
        out_t_ref[:, rows] = jnp.transpose(out_ref[rows, :])


def project_kernel(block_ref, *refs):
    pieces, (kept_ref, theirs_ref, cross_ref, cross_theirs_ref), weight_ref = refs[:9], refs[-5:-1], refs[-1]
    width = weight_ref.shape[1]
    for tile in range(kept_ref.shape[1] // width):
        cols = slice(tile * width, (tile + 1) * width)
        at = 0
        for ref in pieces:
            weight_ref[at : at + ref.shape[0], :] = ref[:, cols]
            at += ref.shape[0]
        out = mm(block_ref[...], weight_ref[...], 1, 0)
        kept_ref[:, cols] = out[0:BLOCK]
        theirs_ref[:, cols] = out[BLOCK : 2 * BLOCK]
        cross_ref[:, cols] = out[2 * BLOCK : 3 * BLOCK].astype(BF)
        cross_theirs_ref[:, cols] = out[3 * BLOCK : 4 * BLOCK].astype(BF)


def weight_kernel(block_ref, own_ref, neighbour_ref, across_ref, diagonal_ref, *rest):
    outs, tokens_ref = rest[-10:-1], rest[-1]
    width = tokens_ref.shape[1]
    for tile in range(own_ref.shape[1] // width):
        cols = slice(tile * width, (tile + 1) * width)
        for i, ref in enumerate((own_ref, neighbour_ref, across_ref, diagonal_ref)):
            tokens_ref[i * BLOCK : (i + 1) * BLOCK, :] = ref[:, cols]
        at = 0
        for ref in outs:
            rows = slice(at, at + ref.shape[0])
            ref[:, cols] = mm(block_ref[rows, :], tokens_ref[...], 1, 0).astype(BF)
            at += ref.shape[0]


def add_kernel(a_ref, b_ref, out_ref):
    out_ref[...] = (a_ref[...].astype(F32) + b_ref[...].astype(F32)).astype(BF)


def first_adds_kernel(up_part_ref, up_ref, down_part_ref, down_ref, *rest):
    up_out_ref, down_out_ref = rest[-2:]
    half = up_ref.shape[0]
    up_out_ref[:half] = (up_part_ref[:half].astype(F32) + up_ref[...].astype(F32)).astype(BF)
    up_out_ref[half:] = up_part_ref[half:]
    down_out_ref[:half] = down_part_ref[:half]
    down_out_ref[half:] = (down_part_ref[half:].astype(F32) + down_ref[...].astype(F32)).astype(BF)


def adds_kernel(up_part_ref, up_ref, down_part_ref, down_ref, *rest):
    up_out_ref, down_out_ref = rest[-2:]
    up_out_ref[...] = (up_part_ref[...].astype(F32) + up_ref[...].astype(F32)).astype(BF)
    down_out_ref[...] = (down_part_ref[...].astype(F32) + down_ref[...].astype(F32)).astype(BF)


def last_add_kernel(part_ref, up_ref, down_ref, out_ref):
    out_ref[...] = (
        part_ref[...].astype(F32) + (up_ref[...].astype(F32) + down_ref[...].astype(F32))
    ).astype(BF)


def shape(dims, dtype=BF):
    return jax.ShapeDtypeStruct(dims, dtype)


def call(body, outs, name, flops, moved, args, after=(), scratch=()):
    return pl.pallas_call(
        body,
        in_specs=[pl.BlockSpec(a.shape, lambda n=a.ndim: (0,) * n) for a in args]
        + [pl.BlockSpec(memory_space=pltpu.VMEM)] * len(after),
        out_shape=outs,
        scratch_shapes=list(scratch),
        compiler_params=PARAMS,
        name=name,
        cost_estimate=pl.CostEstimate(flops=flops, bytes_accessed=moved, transcendentals=0),
    )(*args, *after)


def add_pieces(a, b):
    return (a.astype(F32) + b.astype(F32)).astype(BF)


def exchange(array):
    return lax.all_to_all(array, "seq", 0, 0, tiled=True, axis_index_groups=CHIP_GROUPS)


def body(cotangent, queries, key_proj, value_proj, log_decay, out_weight):
    tokens, cols = queries.shape
    share = out_weight.shape[0]
    half = share // 2
    features = NZ * share
    row = shape((tokens, cols))
    row32 = shape((tokens, cols), F32)
    piece = shape((share, cols))
    slices = shape((CHIPS, ROWS, HEAD_DIM))
    half_state = shape((HALF_ROWS, HEAD_DIM))
    tagged = shape((HALF_ROWS + 16, HEAD_DIM))

    below, above = [send(out_weight, Z_UP)], [send(out_weight, Z_DOWN)]

    log_decay = jnp.transpose(log_decay)
    key_mine, key_cross = pl.pallas_call(
        key_terms_kernel,
        in_specs=[pl.BlockSpec(memory_space=pltpu.VMEM)] + [pl.BlockSpec(memory_space=pltpu.HBM)] * 2,
        out_shape=(tagged, tagged),
        scratch_shapes=[pltpu.VMEM((tokens, cols), BF)] * 2 + [pltpu.SemaphoreType.DMA((2,))],
        compiler_params=PARAMS,
        name="key_terms",
        cost_estimate=pl.CostEstimate(flops=40_000_000, bytes_accessed=1_000_000, transcendentals=0),
    )(log_decay, key_proj, value_proj)
    key_other = send(key_cross, CORE)
    merged = call(
        functools.partial(merge_kernel, 0), shape((CHIPS, ROWS + 16, HEAD_DIM)), "merge_keys",
        1_000_000, 500_000, (key_mine, key_other, key_mine, key_other),
    )
    parts = call(
        cotangent_kernel, (shape((2 * share, tokens)),) * 2, "cotangent_parts", 40_000_000_000, 400_000,
        (cotangent,), (below[0], above[0], merged),
    )
    below.append(send(below[0], Z_UP))
    above.append(send(above[0], Z_DOWN))
    pieces = []
    for a in range(2):
        for b in range(2):
            table = pairs(lambda yl, z, c, yh, x, a=a, b=b: (yh, z, c ^ a, yl ^ b, x))
            pieces.append(send(parts[a], table))
    gathered = exchange(merged)

    befores = call(
        functools.partial(recurrence_kernel, False), slices, "states_before", 1_000_000, 1_000_000,
        (gathered, gathered),
    )
    own = call(collect_kernel, shape((2 * share, 4 * tokens)), "collect", 0, 800_000, pieces, (befores,))
    left, right = send(own, X_UP), send(own, X_DOWN)
    before = exchange(befores).reshape(HALF_ROWS, HEAD_DIM)
    before_own, before_cross = call(
        functools.partial(spread_kernel, 0), (half_state, half_state), "spread_before",
        20_000_000_000, 500_000, (key_mine, key_other, key_mine, key_other, before),
    )
    before_other = send(before_cross, CORE)
    attended, scores, states = call(
        attended_kernel, (row, row, shape((cols, HEAD_DIM))), "attended", 110_000_000, 2_000_000,
        (log_decay, queries, key_proj, value_proj, before_own, before_other), (below[1], above[1]),
    )
    below.append(send(below[-1], Z_UP))
    above.append(send(above[-1], Z_DOWN))
    across = send(attended, CORE)
    neighbour = send(attended, Y_LO)
    opposite = send(left, X_UP)
    block, block_t = call(
        functools.partial(assemble_kernel, share),
        (shape((features, 4 * tokens)), shape((4 * tokens, features))), "assemble",
        1_000_000, 5_000_000, (own, left, right, opposite),
    )
    diagonal = send(neighbour, CORE)
    far_low = send(below[2][:half], Z_UP)
    far_high = send(above[2][half:], Z_DOWN)

    weights = [out_weight] + above + [far_low, far_high] + below[::-1]
    kept, theirs, cross, cross_theirs = pl.pallas_call(
        project_kernel,
        out_shape=[row32, row32, row, row],
        scratch_shapes=[pltpu.VMEM((features, cols // TILES), BF)],
        compiler_params=PARAMS,
        name="project",
        cost_estimate=pl.CostEstimate(
            flops=1_600_000_000, bytes_accessed=6_000_000, transcendentals=0
        ),
    )(block_t, *weights)
    from_core_theirs = send(cross_theirs, CORE)
    from_core = send(cross, CORE)
    passed = call(add_kernel, row, "sum_theirs", 100_000, 1_000_000, (theirs, from_core_theirs))
    arrived = send(passed, Y_LO)

    part = pl.pallas_call(
        weight_kernel,
        in_specs=[pl.BlockSpec(memory_space=pltpu.VMEM)] * 6,
        out_shape=[piece] * 4 + [shape((half, cols))] * 2 + [piece] * 3,
        scratch_shapes=[pltpu.VMEM((4 * tokens, cols // TILES), BF)],
        compiler_params=PARAMS,
        name="weight_partial",
        cost_estimate=pl.CostEstimate(
            flops=1_600_000_000, bytes_accessed=6_000_000, transcendentals=0
        ),
    )(block, attended, neighbour, across, diagonal, passed)
    up, down = send(part[4], Z_UP), send(part[5], Z_DOWN)

    grad_attn, query_mine, query_cross = call(
        query_terms_kernel, (row, half_state, half_state), "query_terms", 40_000_000, 1_000_000,
        (log_decay, queries, kept, from_core, arrived),
    )
    up, down = call(
        first_adds_kernel, (piece, piece), "ring_sum_3", 400_000, 2_000_000,
        (part[3], up, part[6], down), (grad_attn,),
    )
    up, down = send(up, Z_UP), send(down, Z_DOWN)
    query_other = send(query_cross, CORE)
    query_merged = call(
        functools.partial(merge_kernel, 1), slices, "merge_queries", 1_000_000, 500_000,
        (key_mine, key_other, query_mine, query_other),
    )
    returned = exchange(query_merged)
    up, down = add_pieces(part[2], up), add_pieces(part[7], down)
    afters = call(
        functools.partial(recurrence_kernel, True), slices, "states_after", 1_000_000, 1_000_000,
        (gathered, returned), (up, down),
    )
    up, down = send(up, Z_UP), send(down, Z_DOWN)
    after = exchange(afters).reshape(HALF_ROWS, HEAD_DIM)
    up, down = add_pieces(part[1], up), add_pieces(part[8], down)
    grad_queries, inner_k, inner_v = call(
        inner_grads_kernel, (row, row32, row32), "inner_grads", 200_000_000, 3_000_000,
        (log_decay, queries, key_proj, value_proj, grad_attn, scores, states), (up, down),
    )
    after_own, after_cross = call(
        functools.partial(spread_kernel, 1), (half_state, half_state), "spread_after",
        25_000_000_000, 500_000, (key_mine, key_other, query_mine, query_other, after), (inner_k,),
    )
    after_other = send(after_cross, CORE)
    up, down = send(up, Z_UP), send(down, Z_DOWN)
    grad_keys, grad_values = call(
        outer_grads_kernel, (row, row), "outer_grads", 70_000_000, 3_000_000,
        (log_decay, key_proj, value_proj, inner_k, inner_v, after_own, after_other),
        scratch=[pltpu.VMEM((cols, HEAD_DIM), BF)],
    )
    grad_weight = call(last_add_kernel, piece, "ring_sum_0", 400_000, 2_000_000, (part[0], up, down))
    return grad_queries, grad_keys, grad_values, grad_weight


def solution(mesh):
    placed = P("seq", "head")
    return jax.shard_map(
        body,
        mesh=mesh,
        in_specs=(placed,) * 6,
        out_specs=(placed,) * 4,
        check_vma=False,
    )
```

```python
import functools

import jax
import jax.numpy as jnp
from jax import lax
from jax.experimental import pallas as pl
from jax.experimental.pallas import tpu as pltpu
from jax.sharding import PartitionSpec as P

HEAD_DIM = 128
BLOCK = 128
HEADS_LOCAL = 8
CHIPS = 16
HALF_ROWS = 512
ROWS = 32
NZ = 8
TILES = 4
BF = jnp.bfloat16
F32 = jnp.float32
AXES = ("seq", "head")
PARAMS = pltpu.CompilerParams(vmem_limit_bytes=16 * 1024 * 1024)


def pairs(move):
    out = []
    for yl in range(2):
        for z in range(8):
            for c in range(2):
                for yh in range(2):
                    for x in range(4):
                        a, b, d, e, f = move(yl, z, c, yh, x)
                        out.append(
                            (
                                (yl * 16 + z * 2 + c) * 8 + yh * 4 + x,
                                (a * 16 + (b % 8) * 2 + d) * 8 + e * 4 + f % 4,
                            )
                        )
    return out


Z_UP = pairs(lambda yl, z, c, yh, x: (yl, z + 1, c, yh, x))
Z_DOWN = pairs(lambda yl, z, c, yh, x: (yl, z + 7, c, yh, x))
X_UP = pairs(lambda yl, z, c, yh, x: (yl, z, c, yh, x + 1))
X_DOWN = pairs(lambda yl, z, c, yh, x: (yl, z, c, yh, x + 3))
CORE = pairs(lambda yl, z, c, yh, x: (yl, z, 1 - c, yh, x))
Y_LO = pairs(lambda yl, z, c, yh, x: (1 - yl, z, c, yh, x))


CHIP_GROUPS = [[2 * p + c for p in range(CHIPS)] for c in range(2)]


def send(array, table):
    return lax.ppermute(array, AXES, table)


def mm(a, b, ca, cb):
    return lax.dot_general(a, b, (((ca,), (cb,)), ((), ())), preferred_element_type=F32)


def coordinates():
    seq, head = lax.axis_index("seq"), lax.axis_index("head")
    y_lo = seq // 16
    rest = seq - 16 * y_lo
    z = rest // 2
    core = rest - 2 * z
    y_hi = head // 4
    return y_lo, z, core, y_hi, head - 4 * y_hi


def flip_bit():
    y_lo, _, _, y_hi, _ = coordinates()
    return y_lo + y_hi - 2 * y_lo * y_hi


def within_columns(decay):
    at = lax.broadcasted_iota(jnp.int32, (BLOCK, BLOCK), 0)
    of = lax.broadcasted_iota(jnp.int32, (BLOCK, BLOCK), 1)
    lower = (of <= at).astype(F32)
    return lax.dot_general(
        lower, decay, (((1,), (1,)), ((), ())),
        precision=lax.Precision.HIGHEST, preferred_element_type=F32,
    )


def causal_mask(within_col):
    gaps = within_col - jnp.transpose(within_col)
    at = lax.broadcasted_iota(jnp.int32, (BLOCK, BLOCK), 0)
    of = lax.broadcasted_iota(jnp.int32, (BLOCK, BLOCK), 1)
    return jnp.exp(jnp.where(at >= of, gaps, -jnp.inf))


def head_cols(h):
    return pl.ds(h * HEAD_DIM, HEAD_DIM)


def cotangent_kernel(cot_ref, *rest):
    same_ref, swap_ref = rest[-2:]
    _, _, core, _, _ = coordinates()
    turned = jnp.transpose(cot_ref[...])
    share = turned.shape[0] // 4
    for i in range(2):
        first = turned[(2 * i) * share : (2 * i + 1) * share]
        second = turned[(2 * i + 1) * share : (2 * i + 2) * share]
        rows = pl.ds(i * share, share)

        @pl.when(core == 0)
        def _():
            same_ref[rows, :] = first
            swap_ref[rows, :] = second

        @pl.when(core == 1)
        def _():
            same_ref[rows, :] = second
            swap_ref[rows, :] = first


def key_terms_kernel(decay_ref, key_hbm, value_hbm, mine_ref, cross_ref, key_ref, value_ref, sems):
    copies = (
        pltpu.make_async_copy(key_hbm, key_ref, sems.at[0]),
        pltpu.make_async_copy(value_hbm, value_ref, sems.at[1]),
    )
    for copy in copies:
        copy.start()
    within = within_columns(decay_ref[...])
    for copy in copies:
        copy.wait()
    _, _, core, _, _ = coordinates()
    row = lax.broadcasted_iota(jnp.int32, (16, HEAD_DIM), 0)
    for half in range(2):
        decays = jnp.zeros((16, HEAD_DIM), F32)
        for i in range(4):
            h = 4 * half + i
            col = within[:, h : h + 1]
            last = col[BLOCK - 1 : BLOCK]
            scaled = (jnp.exp(last - col) * key_ref[:, head_cols(h)].astype(F32)).astype(BF)
            terms = mm(scaled, value_ref[:, head_cols(h)], 0, 0).astype(BF)
            decays = put_parts(decays, row, 3 * i, last)
            store_half(core, half, i, terms, mine_ref, cross_ref)
        decays = decays.astype(BF)
        rows = pl.ds(HALF_ROWS, 16)

        @pl.when(core == half)
        def _():
            mine_ref[rows, :] = decays

        @pl.when(core != half)
        def _():
            cross_ref[rows, :] = decays


def put_parts(decays, row, at, value):
    high = value.astype(BF).astype(F32)
    middle = (value - high).astype(BF).astype(F32)
    low = value - high - middle
    decays = jnp.where(row == at, high, decays)
    decays = jnp.where(row == at + 1, middle, decays)
    return jnp.where(row == at + 2, low, decays)


def add_parts(decays, at):
    return decays[at : at + 1] + (decays[at + 1 : at + 2] + decays[at + 2 : at + 3])


def store_half(core, half, i, value, mine_ref, cross_ref):
    rows = pl.ds(i * HEAD_DIM, HEAD_DIM)

    @pl.when(core == half)
    def _():
        mine_ref[rows, :] = value

    @pl.when(core != half)
    def _():
        cross_ref[rows, :] = value


def merge_kernel(lead, mine_decay_ref, other_decay_ref, mine_ref, other_ref, *rest):
    out_ref = rest[-1]
    _, _, core, _, _ = coordinates()
    row = lax.broadcasted_iota(jnp.int32, (16, HEAD_DIM), 0)
    mine_decays = mine_decay_ref[HALF_ROWS : HALF_ROWS + 16, :].astype(F32)
    other_decays = other_decay_ref[HALF_ROWS : HALF_ROWS + 16, :].astype(F32)
    for j in range(4):
        rows = slice(j * HEAD_DIM, (j + 1) * HEAD_DIM)
        mine_decay, other_decay = add_parts(mine_decays, 3 * j), add_parts(other_decays, 3 * j)
        mine, other = mine_ref[rows, :].astype(F32), other_ref[rows, :].astype(F32)
        is_lead = core == lead
        mine = mine * jnp.where(is_lead, jnp.exp(other_decay), 1.0)
        other = other * jnp.where(is_lead, 1.0, jnp.exp(mine_decay))
        terms = (mine + other).astype(BF)
        for i in range(4):
            out_ref[4 * j + i, 0:ROWS, :] = terms[i * ROWS : (i + 1) * ROWS]
        if out_ref.shape[1] > ROWS:
            parts = put_parts(jnp.zeros((16, HEAD_DIM), F32), row, 0, mine_decay + other_decay)
            parts = parts.astype(BF)
            for i in range(4):
                out_ref[4 * j + i, ROWS : ROWS + 16, :] = parts


def spread_kernel(
    lead, mine_decay_ref, other_decay_ref, mine_ref, other_ref, state_ref, *rest
):
    own_out_ref, cross_out_ref = rest[-2:]
    _, _, core, _, _ = coordinates()
    mine_decays = mine_decay_ref[HALF_ROWS : HALF_ROWS + 16, :].astype(F32)
    other_decays = other_decay_ref[HALF_ROWS : HALF_ROWS + 16, :].astype(F32)
    for j in range(4):
        rows = slice(j * HEAD_DIM, (j + 1) * HEAD_DIM)
        state = state_ref[rows, :]
        wide = state.astype(F32)
        mine_moved = jnp.exp(add_parts(mine_decays, 3 * j)) * wide + mine_ref[rows, :].astype(F32)
        other_moved = jnp.exp(add_parts(other_decays, 3 * j)) * wide + other_ref[rows, :].astype(F32)

        @pl.when(core == lead)
        def _():
            own_out_ref[rows, :] = state
            cross_out_ref[rows, :] = mine_moved.astype(BF)

        @pl.when(core != lead)
        def _():
            own_out_ref[rows, :] = other_moved.astype(BF)
            cross_out_ref[rows, :] = state


def recurrence_kernel(reverse, decay_ref, terms_ref, *rest):
    out_ref = rest[-1]
    state = jnp.zeros((ROWS, HEAD_DIM), F32)
    for k in reversed(range(CHIPS)) if reverse else range(CHIPS):
        out_ref[k] = state.astype(BF)
        factor = jnp.exp(add_parts(decay_ref[k, ROWS : ROWS + 16, :].astype(F32), 0))
        state = factor * state + terms_ref[k, 0:ROWS, :].astype(F32)


def gather_halves(own_ref, other_ref, out_ref):
    _, _, core, _, _ = coordinates()
    out_ref[pl.ds(pl.multiple_of(core * HALF_ROWS, HALF_ROWS), HALF_ROWS), :] = own_ref[...]
    out_ref[pl.ds(pl.multiple_of((1 - core) * HALF_ROWS, HALF_ROWS), HALF_ROWS), :] = other_ref[...]


def attended_kernel(decay_ref, query_ref, key_ref, value_ref, own_ref, other_ref, *rest):
    att_ref, score_ref, state_ref = rest[-3:]
    gather_halves(own_ref, other_ref, state_ref)
    within = within_columns(decay_ref[...])
    for h in range(HEADS_LOCAL):
        cols = head_cols(h)
        col = within[:, h : h + 1]
        query = query_ref[:, cols]
        scores = (mm(query, key_ref[:, cols], 1, 1) * causal_mask(col)).astype(BF)
        score_ref[:, cols] = scores
        att = jnp.exp(col) * mm(query, state_ref[pl.ds(h * HEAD_DIM, HEAD_DIM), :], 1, 0)
        att_ref[:, cols] = (att + mm(scores, value_ref[:, cols], 1, 0)).astype(BF)


def query_terms_kernel(decay_ref, query_ref, own_ref, core_ref, other_ref, *rest):
    grad_ref, mine_ref, cross_ref = rest[-3:]
    _, _, core, _, _ = coordinates()
    within = within_columns(decay_ref[...])
    for h in range(HEADS_LOCAL):
        cols = head_cols(h)
        grad = own_ref[:, cols] + core_ref[:, cols].astype(F32) + other_ref[:, cols].astype(F32)
        grad = grad.astype(BF)
        grad_ref[:, cols] = grad
        scaled = (jnp.exp(within[:, h : h + 1]) * query_ref[:, cols].astype(F32)).astype(BF)
        terms = mm(scaled, grad, 0, 0).astype(BF)
        store_half(core, h // 4, h % 4, terms, mine_ref, cross_ref)


def inner_grads_kernel(
    decay_ref, query_ref, key_ref, value_ref, grad_ref, score_ref, state_ref, *rest
):
    gq_ref, gk_ref, gv_ref = rest[-3:]
    within = within_columns(decay_ref[...])
    for h in range(HEADS_LOCAL):
        cols = head_cols(h)
        col = within[:, h : h + 1]
        grad, key = grad_ref[:, cols], key_ref[:, cols]
        grad_scores = (mm(grad, value_ref[:, cols], 1, 1) * causal_mask(col)).astype(BF)
        state = state_ref[pl.ds(h * HEAD_DIM, HEAD_DIM), :]
        gq = jnp.exp(col) * mm(grad, state, 1, 1) + mm(grad_scores, key, 1, 0)
        gq_ref[:, cols] = gq.astype(BF)
        gk_ref[:, cols] = mm(grad_scores, query_ref[:, cols], 0, 0)
        gv_ref[:, cols] = mm(score_ref[:, cols], grad, 0, 0)


def outer_grads_kernel(
    decay_ref, key_ref, value_ref, inner_k_ref, inner_v_ref, own_ref, other_ref,
    gk_ref, gv_ref, after_ref,
):
    gather_halves(own_ref, other_ref, after_ref)
    within = within_columns(decay_ref[...])
    for h in range(HEADS_LOCAL):
        cols = head_cols(h)
        key_weight = jnp.exp(within[BLOCK - 1 : BLOCK, h : h + 1] - within[:, h : h + 1])
        after = after_ref[pl.ds(h * HEAD_DIM, HEAD_DIM), :]
        gk = key_weight * mm(value_ref[:, cols], after, 1, 1) + inner_k_ref[:, cols]
        gk_ref[:, cols] = gk.astype(BF)
        gv = key_weight * mm(key_ref[:, cols], after, 1, 0) + inner_v_ref[:, cols]
        gv_ref[:, cols] = gv.astype(BF)


def collect_kernel(a_ref, b_ref, c_ref, d_ref, *rest):
    out_ref = rest[-1]
    flip = flip_bit()
    for i, ref in ((flip, a_ref), (1 - flip, b_ref), (2 + flip, c_ref), (3 - flip, d_ref)):
        out_ref[:, pl.ds(pl.multiple_of(i * BLOCK, BLOCK), BLOCK)] = ref[...]


def assemble_kernel(share, own_ref, left_ref, right_ref, opposite_ref, out_ref, out_t_ref):
    _, z, _, _, x = coordinates()
    for off, ref, start, part in (
        (0, own_ref, 0, 0), (0, own_ref, share, 1),
        (1, right_ref, 0, 0), (1, right_ref, share, 1),
        (2, opposite_ref, 0, 0), (2, opposite_ref, share, 1),
        (3, left_ref, 0, 0), (3, left_ref, share, 1),
    ):
        k = (2 * ((x + off) % 4) + part - z + NZ) % NZ
        at = pl.multiple_of(k * share, 64)
        out_ref[pl.ds(at, share), :] = ref[start : start + share, :]
    for i in range(NZ * share // 256):
        rows = pl.ds(i * 256, 256)
        out_t_ref[:, rows] = jnp.transpose(out_ref[rows, :])


def project_kernel(block_ref, *refs):
    pieces, (kept_ref, theirs_ref, cross_ref, cross_theirs_ref), weight_ref = refs[:9], refs[-5:-1], refs[-1]
    width = weight_ref.shape[1]
    for tile in range(kept_ref.shape[1] // width):
        cols = slice(tile * width, (tile + 1) * width)
        at = 0
        for ref in pieces:
            weight_ref[at : at + ref.shape[0], :] = ref[:, cols]
            at += ref.shape[0]
        out = mm(block_ref[...], weight_ref[...], 1, 0)
        kept_ref[:, cols] = out[0:BLOCK]
        theirs_ref[:, cols] = out[BLOCK : 2 * BLOCK]
        cross_ref[:, cols] = out[2 * BLOCK : 3 * BLOCK].astype(BF)
        cross_theirs_ref[:, cols] = out[3 * BLOCK : 4 * BLOCK].astype(BF)


def weight_kernel(block_ref, own_ref, neighbour_ref, across_ref, diagonal_ref, *rest):
    outs, tokens_ref = rest[-10:-1], rest[-1]
    width = tokens_ref.shape[1]
    for tile in range(own_ref.shape[1] // width):
        cols = slice(tile * width, (tile + 1) * width)
        for i, ref in enumerate((own_ref, neighbour_ref, across_ref, diagonal_ref)):
            tokens_ref[i * BLOCK : (i + 1) * BLOCK, :] = ref[:, cols]
        at = 0
        for ref in outs:
            rows = slice(at, at + ref.shape[0])
            ref[:, cols] = mm(block_ref[rows, :], tokens_ref[...], 1, 0).astype(BF)
            at += ref.shape[0]


def add_kernel(a_ref, b_ref, out_ref):
    out_ref[...] = (a_ref[...].astype(F32) + b_ref[...].astype(F32)).astype(BF)


def first_adds_kernel(up_part_ref, up_ref, down_part_ref, down_ref, *rest):
    up_out_ref, down_out_ref = rest[-2:]
    half = up_ref.shape[0]
    up_out_ref[:half] = (up_part_ref[:half].astype(F32) + up_ref[...].astype(F32)).astype(BF)
    up_out_ref[half:] = up_part_ref[half:]
    down_out_ref[:half] = down_part_ref[:half]
    down_out_ref[half:] = (down_part_ref[half:].astype(F32) + down_ref[...].astype(F32)).astype(BF)


def adds_kernel(up_part_ref, up_ref, down_part_ref, down_ref, *rest):
    up_out_ref, down_out_ref = rest[-2:]
    up_out_ref[...] = (up_part_ref[...].astype(F32) + up_ref[...].astype(F32)).astype(BF)
    down_out_ref[...] = (down_part_ref[...].astype(F32) + down_ref[...].astype(F32)).astype(BF)


def last_add_kernel(part_ref, up_ref, down_ref, out_ref):
    out_ref[...] = (
        part_ref[...].astype(F32) + (up_ref[...].astype(F32) + down_ref[...].astype(F32))
    ).astype(BF)


def shape(dims, dtype=BF):
    return jax.ShapeDtypeStruct(dims, dtype)


def call(body, outs, name, flops, moved, args, after=(), scratch=()):
    return pl.pallas_call(
        body,
        in_specs=[pl.BlockSpec(a.shape, lambda n=a.ndim: (0,) * n) for a in args]
        + [pl.BlockSpec(memory_space=pltpu.VMEM)] * len(after),
        out_shape=outs,
        scratch_shapes=list(scratch),
        compiler_params=PARAMS,
        name=name,
        cost_estimate=pl.CostEstimate(flops=flops, bytes_accessed=moved, transcendentals=0),
    )(*args, *after)


def add_pieces(a, b):
    return (a.astype(F32) + b.astype(F32)).astype(BF)


def exchange(array):
    return lax.all_to_all(array, "seq", 0, 0, tiled=True, axis_index_groups=CHIP_GROUPS)


def body(cotangent, queries, key_proj, value_proj, log_decay, out_weight):
    tokens, cols = queries.shape
    share = out_weight.shape[0]
    half = share // 2
    features = NZ * share
    row = shape((tokens, cols))
    row32 = shape((tokens, cols), F32)
    piece = shape((share, cols))
    slices = shape((CHIPS, ROWS, HEAD_DIM))
    half_state = shape((HALF_ROWS, HEAD_DIM))
    tagged = shape((HALF_ROWS + 16, HEAD_DIM))

    below, above = [send(out_weight, Z_UP)], [send(out_weight, Z_DOWN)]

    log_decay = jnp.transpose(log_decay)
    key_mine, key_cross = pl.pallas_call(
        key_terms_kernel,
        in_specs=[pl.BlockSpec(memory_space=pltpu.VMEM)] + [pl.BlockSpec(memory_space=pltpu.HBM)] * 2,
        out_shape=(tagged, tagged),
        scratch_shapes=[pltpu.VMEM((tokens, cols), BF)] * 2 + [pltpu.SemaphoreType.DMA((2,))],
        compiler_params=PARAMS,
        name="key_terms",
        cost_estimate=pl.CostEstimate(flops=40_000_000, bytes_accessed=1_000_000, transcendentals=0),
    )(log_decay, key_proj, value_proj)
    key_other = send(key_cross, CORE)
    merged = call(
        functools.partial(merge_kernel, 0), shape((CHIPS, ROWS + 16, HEAD_DIM)), "merge_keys",
        1_000_000, 500_000, (key_mine, key_other, key_mine, key_other),
    )
    parts = call(
        cotangent_kernel, (shape((2 * share, tokens)),) * 2, "cotangent_parts", 40_000_000_000, 400_000,
        (cotangent,), (below[0], above[0], merged),
    )
    below.append(send(below[0], Z_UP))
    above.append(send(above[0], Z_DOWN))
    pieces = []
    for a in range(2):
        for b in range(2):
            table = pairs(lambda yl, z, c, yh, x, a=a, b=b: (yh, z, c ^ a, yl ^ b, x))
            pieces.append(send(parts[a], table))
    gathered = exchange(merged)

    befores = call(
        functools.partial(recurrence_kernel, False), slices, "states_before", 1_000_000, 1_000_000,
        (gathered, gathered),
    )
    own = call(
        collect_kernel, shape((2 * share, 4 * tokens)), "collect", 0, 800_000, pieces,
        (befores, below[1], above[1]),
    )
    left, right = send(own, X_UP), send(own, X_DOWN)
    below.append(send(below[1], Z_UP))
    above.append(send(above[1], Z_DOWN))
    far_low = send(below[2][:half], Z_UP)
    far_high = send(above[2][half:], Z_DOWN)
    before = exchange(befores).reshape(HALF_ROWS, HEAD_DIM)
    before_own, before_cross = call(
        functools.partial(spread_kernel, 0), (half_state, half_state), "spread_before",
        1_000_000, 500_000, (key_mine, key_other, key_mine, key_other, before), (far_low, far_high),
    )
    before_other = send(before_cross, CORE)
    attended, scores, states = call(
        attended_kernel, (row, row, shape((cols, HEAD_DIM))), "attended", 110_000_000, 2_000_000,
        (log_decay, queries, key_proj, value_proj, before_own, before_other),
    )
    across = send(attended, CORE)
    neighbour = send(attended, Y_LO)
    opposite = send(left, X_UP)
    block, block_t = call(
        functools.partial(assemble_kernel, share),
        (shape((features, 4 * tokens)), shape((4 * tokens, features))), "assemble",
        1_000_000, 5_000_000, (own, left, right, opposite),
    )
    diagonal = send(neighbour, CORE)

    weights = [out_weight] + above + [far_low, far_high] + below[::-1]
    kept, theirs, cross, cross_theirs = pl.pallas_call(
        project_kernel,
        out_shape=[row32, row32, row, row],
        scratch_shapes=[pltpu.VMEM((features, cols // TILES), BF)],
        compiler_params=PARAMS,
        name="project",
        cost_estimate=pl.CostEstimate(
            flops=1_600_000_000, bytes_accessed=6_000_000, transcendentals=0
        ),
    )(block_t, *weights)
    from_core_theirs = send(cross_theirs, CORE)
    from_core = send(cross, CORE)
    passed = call(add_kernel, row, "sum_theirs", 100_000, 1_000_000, (theirs, from_core_theirs))
    arrived = send(passed, Y_LO)

    part = pl.pallas_call(
        weight_kernel,
        in_specs=[pl.BlockSpec(memory_space=pltpu.VMEM)] * 6,
        out_shape=[piece] * 4 + [shape((half, cols))] * 2 + [piece] * 3,
        scratch_shapes=[pltpu.VMEM((4 * tokens, cols // TILES), BF)],
        compiler_params=PARAMS,
        name="weight_partial",
        cost_estimate=pl.CostEstimate(
            flops=1_600_000_000, bytes_accessed=6_000_000, transcendentals=0
        ),
    )(block, attended, neighbour, across, diagonal, passed)
    up, down = send(part[4], Z_UP), send(part[5], Z_DOWN)

    grad_attn, query_mine, query_cross = call(
        query_terms_kernel, (row, half_state, half_state), "query_terms", 40_000_000, 1_000_000,
        (log_decay, queries, kept, from_core, arrived),
    )
    up, down = call(
        first_adds_kernel, (piece, piece), "ring_sum_3", 400_000, 2_000_000,
        (part[3], up, part[6], down), (grad_attn,),
    )
    up, down = send(up, Z_UP), send(down, Z_DOWN)
    query_other = send(query_cross, CORE)
    query_merged = call(
        functools.partial(merge_kernel, 1), slices, "merge_queries", 1_000_000, 500_000,
        (key_mine, key_other, query_mine, query_other),
    )
    returned = exchange(query_merged)
    up, down = add_pieces(part[2], up), add_pieces(part[7], down)
    afters = call(
        functools.partial(recurrence_kernel, True), slices, "states_after", 1_000_000, 1_000_000,
        (gathered, returned), (up, down),
    )
    up, down = send(up, Z_UP), send(down, Z_DOWN)
    after = exchange(afters).reshape(HALF_ROWS, HEAD_DIM)
    up, down = add_pieces(part[1], up), add_pieces(part[8], down)
    grad_queries, inner_k, inner_v = call(
        inner_grads_kernel, (row, row32, row32), "inner_grads", 200_000_000, 3_000_000,
        (log_decay, queries, key_proj, value_proj, grad_attn, scores, states), (up, down),
    )
    after_own, after_cross = call(
        functools.partial(spread_kernel, 1), (half_state, half_state), "spread_after",
        25_000_000_000, 500_000, (key_mine, key_other, query_mine, query_other, after), (inner_k,),
    )
    after_other = send(after_cross, CORE)
    up, down = send(up, Z_UP), send(down, Z_DOWN)
    grad_keys, grad_values = call(
        outer_grads_kernel, (row, row), "outer_grads", 70_000_000, 3_000_000,
        (log_decay, key_proj, value_proj, inner_k, inner_v, after_own, after_other),
        scratch=[pltpu.VMEM((cols, HEAD_DIM), BF)],
    )
    grad_weight = call(last_add_kernel, piece, "ring_sum_0", 400_000, 2_000_000, (part[0], up, down))
    return grad_queries, grad_keys, grad_values, grad_weight


def solution(mesh):
    placed = P("seq", "head")
    return jax.shard_map(
        body,
        mesh=mesh,
        in_specs=(placed,) * 6,
        out_specs=(placed,) * 4,
        check_vma=False,
    )
```

```python
import functools

import jax
import jax.numpy as jnp
from jax import lax
from jax.experimental import pallas as pl
from jax.experimental.pallas import tpu as pltpu
from jax.sharding import PartitionSpec as P

HEAD_DIM = 128
BLOCK = 128
HEADS_LOCAL = 8
CHIPS = 16
HALF_ROWS = 512
ROWS = 32
NZ = 8
TILES = 4
BF = jnp.bfloat16
F32 = jnp.float32
AXES = ("seq", "head")
PARAMS = pltpu.CompilerParams(vmem_limit_bytes=16 * 1024 * 1024)


def pairs(move):
    out = []
    for yl in range(2):
        for z in range(8):
            for c in range(2):
                for yh in range(2):
                    for x in range(4):
                        a, b, d, e, f = move(yl, z, c, yh, x)
                        out.append(
                            (
                                (yl * 16 + z * 2 + c) * 8 + yh * 4 + x,
                                (a * 16 + (b % 8) * 2 + d) * 8 + e * 4 + f % 4,
                            )
                        )
    return out


Z_UP = pairs(lambda yl, z, c, yh, x: (yl, z + 1, c, yh, x))
Z_DOWN = pairs(lambda yl, z, c, yh, x: (yl, z + 7, c, yh, x))
X_UP = pairs(lambda yl, z, c, yh, x: (yl, z, c, yh, x + 1))
X_DOWN = pairs(lambda yl, z, c, yh, x: (yl, z, c, yh, x + 3))
CORE = pairs(lambda yl, z, c, yh, x: (yl, z, 1 - c, yh, x))
Y_LO = pairs(lambda yl, z, c, yh, x: (1 - yl, z, c, yh, x))


CHIP_GROUPS = [[2 * p + c for p in range(CHIPS)] for c in range(2)]


def send(array, table):
    return lax.ppermute(array, AXES, table)


def mm(a, b, ca, cb):
    return lax.dot_general(a, b, (((ca,), (cb,)), ((), ())), preferred_element_type=F32)


def coordinates():
    seq, head = lax.axis_index("seq"), lax.axis_index("head")
    y_lo = seq // 16
    rest = seq - 16 * y_lo
    z = rest // 2
    core = rest - 2 * z
    y_hi = head // 4
    return y_lo, z, core, y_hi, head - 4 * y_hi


def flip_bit():
    y_lo, _, _, y_hi, _ = coordinates()
    return y_lo + y_hi - 2 * y_lo * y_hi


def within_columns(decay):
    at = lax.broadcasted_iota(jnp.int32, (BLOCK, BLOCK), 0)
    of = lax.broadcasted_iota(jnp.int32, (BLOCK, BLOCK), 1)
    lower = (of <= at).astype(F32)
    return lax.dot_general(
        lower, decay, (((1,), (1,)), ((), ())),
        precision=lax.Precision.HIGHEST, preferred_element_type=F32,
    )


def causal_mask(within_col):
    gaps = within_col - jnp.transpose(within_col)
    at = lax.broadcasted_iota(jnp.int32, (BLOCK, BLOCK), 0)
    of = lax.broadcasted_iota(jnp.int32, (BLOCK, BLOCK), 1)
    return jnp.exp(jnp.where(at >= of, gaps, -jnp.inf))


def head_cols(h):
    return pl.ds(h * HEAD_DIM, HEAD_DIM)


def cotangent_kernel(cot_ref, *rest):
    same_ref, swap_ref = rest[-2:]
    _, _, core, _, _ = coordinates()
    turned = jnp.transpose(cot_ref[...])
    share = turned.shape[0] // 4
    for i in range(2):
        first = turned[(2 * i) * share : (2 * i + 1) * share]
        second = turned[(2 * i + 1) * share : (2 * i + 2) * share]
        rows = pl.ds(i * share, share)

        @pl.when(core == 0)
        def _():
            same_ref[rows, :] = first
            swap_ref[rows, :] = second

        @pl.when(core == 1)
        def _():
            same_ref[rows, :] = second
            swap_ref[rows, :] = first


def key_terms_kernel(decay_ref, key_hbm, value_hbm, mine_ref, cross_ref, key_ref, value_ref, sems):
    copies = (
        pltpu.make_async_copy(key_hbm, key_ref, sems.at[0]),
        pltpu.make_async_copy(value_hbm, value_ref, sems.at[1]),
    )
    for copy in copies:
        copy.start()
    within = within_columns(decay_ref[...])
    for copy in copies:
        copy.wait()
    _, _, core, _, _ = coordinates()
    row = lax.broadcasted_iota(jnp.int32, (16, HEAD_DIM), 0)
    for half in range(2):
        decays = jnp.zeros((16, HEAD_DIM), F32)
        for i in range(4):
            h = 4 * half + i
            col = within[:, h : h + 1]
            last = col[BLOCK - 1 : BLOCK]
            scaled = (jnp.exp(last - col) * key_ref[:, head_cols(h)].astype(F32)).astype(BF)
            terms = mm(scaled, value_ref[:, head_cols(h)], 0, 0).astype(BF)
            decays = put_parts(decays, row, 3 * i, last)
            store_half(core, half, i, terms, mine_ref, cross_ref)
        decays = decays.astype(BF)
        rows = pl.ds(HALF_ROWS, 16)

        @pl.when(core == half)
        def _():
            mine_ref[rows, :] = decays

        @pl.when(core != half)
        def _():
            cross_ref[rows, :] = decays


def put_parts(decays, row, at, value):
    high = value.astype(BF).astype(F32)
    middle = (value - high).astype(BF).astype(F32)
    low = value - high - middle
    decays = jnp.where(row == at, high, decays)
    decays = jnp.where(row == at + 1, middle, decays)
    return jnp.where(row == at + 2, low, decays)


def add_parts(decays, at):
    return decays[at : at + 1] + (decays[at + 1 : at + 2] + decays[at + 2 : at + 3])


def store_half(core, half, i, value, mine_ref, cross_ref):
    rows = pl.ds(i * HEAD_DIM, HEAD_DIM)

    @pl.when(core == half)
    def _():
        mine_ref[rows, :] = value

    @pl.when(core != half)
    def _():
        cross_ref[rows, :] = value


def merge_kernel(lead, mine_decay_ref, other_decay_ref, mine_ref, other_ref, *rest):
    out_ref = rest[-1]
    _, _, core, _, _ = coordinates()
    row = lax.broadcasted_iota(jnp.int32, (16, HEAD_DIM), 0)
    mine_decays = mine_decay_ref[HALF_ROWS : HALF_ROWS + 16, :].astype(F32)
    other_decays = other_decay_ref[HALF_ROWS : HALF_ROWS + 16, :].astype(F32)
    for j in range(4):
        rows = slice(j * HEAD_DIM, (j + 1) * HEAD_DIM)
        mine_decay, other_decay = add_parts(mine_decays, 3 * j), add_parts(other_decays, 3 * j)
        mine, other = mine_ref[rows, :].astype(F32), other_ref[rows, :].astype(F32)
        is_lead = core == lead
        mine = mine * jnp.where(is_lead, jnp.exp(other_decay), 1.0)
        other = other * jnp.where(is_lead, 1.0, jnp.exp(mine_decay))
        terms = (mine + other).astype(BF)
        for i in range(4):
            out_ref[4 * j + i, 0:ROWS, :] = terms[i * ROWS : (i + 1) * ROWS]
        if out_ref.shape[1] > ROWS:
            parts = put_parts(jnp.zeros((16, HEAD_DIM), F32), row, 0, mine_decay + other_decay)
            parts = parts.astype(BF)
            for i in range(4):
                out_ref[4 * j + i, ROWS : ROWS + 16, :] = parts


def spread_kernel(
    lead, mine_decay_ref, other_decay_ref, mine_ref, other_ref, state_ref, *rest
):
    own_out_ref, cross_out_ref = rest[-2:]
    _, _, core, _, _ = coordinates()
    mine_decays = mine_decay_ref[HALF_ROWS : HALF_ROWS + 16, :].astype(F32)
    other_decays = other_decay_ref[HALF_ROWS : HALF_ROWS + 16, :].astype(F32)
    for j in range(4):
        rows = slice(j * HEAD_DIM, (j + 1) * HEAD_DIM)
        state = state_ref[rows, :]
        wide = state.astype(F32)
        mine_moved = jnp.exp(add_parts(mine_decays, 3 * j)) * wide + mine_ref[rows, :].astype(F32)
        other_moved = jnp.exp(add_parts(other_decays, 3 * j)) * wide + other_ref[rows, :].astype(F32)

        @pl.when(core == lead)
        def _():
            own_out_ref[rows, :] = state
            cross_out_ref[rows, :] = mine_moved.astype(BF)

        @pl.when(core != lead)
        def _():
            own_out_ref[rows, :] = other_moved.astype(BF)
            cross_out_ref[rows, :] = state


def recurrence_kernel(reverse, decay_ref, terms_ref, *rest):
    out_ref = rest[-1]
    state = jnp.zeros((ROWS, HEAD_DIM), F32)
    for k in reversed(range(CHIPS)) if reverse else range(CHIPS):
        out_ref[k] = state.astype(BF)
        factor = jnp.exp(add_parts(decay_ref[k, ROWS : ROWS + 16, :].astype(F32), 0))
        state = factor * state + terms_ref[k, 0:ROWS, :].astype(F32)


def gather_halves(own_ref, other_ref, out_ref):
    _, _, core, _, _ = coordinates()
    out_ref[pl.ds(pl.multiple_of(core * HALF_ROWS, HALF_ROWS), HALF_ROWS), :] = own_ref[...]
    out_ref[pl.ds(pl.multiple_of((1 - core) * HALF_ROWS, HALF_ROWS), HALF_ROWS), :] = other_ref[...]


def attended_kernel(decay_ref, query_ref, key_ref, value_ref, own_ref, other_ref, *rest):
    att_ref, score_ref, state_ref = rest[-3:]
    gather_halves(own_ref, other_ref, state_ref)
    within = within_columns(decay_ref[...])
    for h in range(HEADS_LOCAL):
        cols = head_cols(h)
        col = within[:, h : h + 1]
        query = query_ref[:, cols]
        scores = (mm(query, key_ref[:, cols], 1, 1) * causal_mask(col)).astype(BF)
        score_ref[:, cols] = scores
        att = jnp.exp(col) * mm(query, state_ref[pl.ds(h * HEAD_DIM, HEAD_DIM), :], 1, 0)
        att_ref[:, cols] = (att + mm(scores, value_ref[:, cols], 1, 0)).astype(BF)


def query_terms_kernel(decay_ref, query_ref, own_ref, core_ref, other_ref, *rest):
    grad_ref, mine_ref, cross_ref = rest[-3:]
    _, _, core, _, _ = coordinates()
    within = within_columns(decay_ref[...])
    for h in range(HEADS_LOCAL):
        cols = head_cols(h)
        grad = own_ref[:, cols] + core_ref[:, cols].astype(F32) + other_ref[:, cols].astype(F32)
        grad = grad.astype(BF)
        grad_ref[:, cols] = grad
        scaled = (jnp.exp(within[:, h : h + 1]) * query_ref[:, cols].astype(F32)).astype(BF)
        terms = mm(scaled, grad, 0, 0).astype(BF)
        store_half(core, h // 4, h % 4, terms, mine_ref, cross_ref)


def inner_grads_kernel(
    decay_ref, query_ref, key_ref, value_ref, grad_ref, score_ref, state_ref, *rest
):
    gq_ref, gk_ref, gv_ref = rest[-3:]
    within = within_columns(decay_ref[...])
    for h in range(HEADS_LOCAL):
        cols = head_cols(h)
        col = within[:, h : h + 1]
        grad, key = grad_ref[:, cols], key_ref[:, cols]
        grad_scores = (mm(grad, value_ref[:, cols], 1, 1) * causal_mask(col)).astype(BF)
        state = state_ref[pl.ds(h * HEAD_DIM, HEAD_DIM), :]
        gq = jnp.exp(col) * mm(grad, state, 1, 1) + mm(grad_scores, key, 1, 0)
        gq_ref[:, cols] = gq.astype(BF)
        gk_ref[:, cols] = mm(grad_scores, query_ref[:, cols], 0, 0)
        gv_ref[:, cols] = mm(score_ref[:, cols], grad, 0, 0)


def outer_grads_kernel(
    decay_ref, key_ref, value_ref, inner_k_ref, inner_v_ref, own_ref, other_ref,
    gk_ref, gv_ref, after_ref,
):
    gather_halves(own_ref, other_ref, after_ref)
    within = within_columns(decay_ref[...])
    for h in range(HEADS_LOCAL):
        cols = head_cols(h)
        key_weight = jnp.exp(within[BLOCK - 1 : BLOCK, h : h + 1] - within[:, h : h + 1])
        after = after_ref[pl.ds(h * HEAD_DIM, HEAD_DIM), :]
        gk = key_weight * mm(value_ref[:, cols], after, 1, 1) + inner_k_ref[:, cols]
        gk_ref[:, cols] = gk.astype(BF)
        gv = key_weight * mm(key_ref[:, cols], after, 1, 0) + inner_v_ref[:, cols]
        gv_ref[:, cols] = gv.astype(BF)


def collect_kernel(a_ref, b_ref, c_ref, d_ref, *rest):
    out_ref = rest[-1]
    flip = flip_bit()
    for i, ref in ((flip, a_ref), (1 - flip, b_ref), (2 + flip, c_ref), (3 - flip, d_ref)):
        out_ref[:, pl.ds(pl.multiple_of(i * BLOCK, BLOCK), BLOCK)] = ref[...]


def assemble_kernel(share, own_ref, left_ref, right_ref, opposite_ref, out_ref, out_t_ref):
    _, z, _, _, x = coordinates()
    for off, ref, start, part in (
        (0, own_ref, 0, 0), (0, own_ref, share, 1),
        (1, right_ref, 0, 0), (1, right_ref, share, 1),
        (2, opposite_ref, 0, 0), (2, opposite_ref, share, 1),
        (3, left_ref, 0, 0), (3, left_ref, share, 1),
    ):
        k = (2 * ((x + off) % 4) + part - z + NZ) % NZ
        at = pl.multiple_of(k * share, 64)
        out_ref[pl.ds(at, share), :] = ref[start : start + share, :]
    for i in range(NZ * share // 256):
        rows = pl.ds(i * 256, 256)
        out_t_ref[:, rows] = jnp.transpose(out_ref[rows, :])


def project_kernel(block_ref, *refs):
    pieces, (kept_ref, theirs_ref, cross_ref, cross_theirs_ref), weight_ref = refs[:9], refs[-5:-1], refs[-1]
    width = weight_ref.shape[1]
    for tile in range(kept_ref.shape[1] // width):
        cols = slice(tile * width, (tile + 1) * width)
        at = 0
        for ref in pieces:
            weight_ref[at : at + ref.shape[0], :] = ref[:, cols]
            at += ref.shape[0]
        out = mm(block_ref[...], weight_ref[...], 1, 0)
        kept_ref[:, cols] = out[0:BLOCK]
        theirs_ref[:, cols] = out[BLOCK : 2 * BLOCK]
        cross_ref[:, cols] = out[2 * BLOCK : 3 * BLOCK].astype(BF)
        cross_theirs_ref[:, cols] = out[3 * BLOCK : 4 * BLOCK].astype(BF)


def weight_kernel(block_ref, own_ref, neighbour_ref, across_ref, diagonal_ref, *rest):
    outs, tokens_ref = rest[-10:-1], rest[-1]
    width = tokens_ref.shape[1]
    for tile in range(own_ref.shape[1] // width):
        cols = slice(tile * width, (tile + 1) * width)
        for i, ref in enumerate((own_ref, neighbour_ref, across_ref, diagonal_ref)):
            tokens_ref[i * BLOCK : (i + 1) * BLOCK, :] = ref[:, cols]
        at = 0
        for ref in outs:
            rows = slice(at, at + ref.shape[0])
            ref[:, cols] = mm(block_ref[rows, :], tokens_ref[...], 1, 0).astype(BF)
            at += ref.shape[0]


def add_kernel(a_ref, b_ref, out_ref):
    out_ref[...] = (a_ref[...].astype(F32) + b_ref[...].astype(F32)).astype(BF)


def first_adds_kernel(up_part_ref, up_ref, down_part_ref, down_ref, *rest):
    up_out_ref, down_out_ref = rest[-2:]
    half = up_ref.shape[0]
    up_out_ref[:half] = (up_part_ref[:half].astype(F32) + up_ref[...].astype(F32)).astype(BF)
    up_out_ref[half:] = up_part_ref[half:]
    down_out_ref[:half] = down_part_ref[:half]
    down_out_ref[half:] = (down_part_ref[half:].astype(F32) + down_ref[...].astype(F32)).astype(BF)


def adds_kernel(up_part_ref, up_ref, down_part_ref, down_ref, *rest):
    up_out_ref, down_out_ref = rest[-2:]
    up_out_ref[...] = (up_part_ref[...].astype(F32) + up_ref[...].astype(F32)).astype(BF)
    down_out_ref[...] = (down_part_ref[...].astype(F32) + down_ref[...].astype(F32)).astype(BF)


def last_add_kernel(part_ref, up_ref, down_ref, out_ref):
    out_ref[...] = (
        part_ref[...].astype(F32) + (up_ref[...].astype(F32) + down_ref[...].astype(F32))
    ).astype(BF)


def shape(dims, dtype=BF):
    return jax.ShapeDtypeStruct(dims, dtype)


def call(body, outs, name, flops, moved, args, after=(), scratch=()):
    return pl.pallas_call(
        body,
        in_specs=[pl.BlockSpec(a.shape, lambda n=a.ndim: (0,) * n) for a in args]
        + [pl.BlockSpec(memory_space=pltpu.VMEM)] * len(after),
        out_shape=outs,
        scratch_shapes=list(scratch),
        compiler_params=PARAMS,
        name=name,
        cost_estimate=pl.CostEstimate(flops=flops, bytes_accessed=moved, transcendentals=0),
    )(*args, *after)


def add_pieces(a, b):
    return (a.astype(F32) + b.astype(F32)).astype(BF)


def exchange(array):
    return lax.all_to_all(array, "seq", 0, 0, tiled=True, axis_index_groups=CHIP_GROUPS)


def body(cotangent, queries, key_proj, value_proj, log_decay, out_weight):
    tokens, cols = queries.shape
    share = out_weight.shape[0]
    half = share // 2
    features = NZ * share
    row = shape((tokens, cols))
    row32 = shape((tokens, cols), F32)
    piece = shape((share, cols))
    slices = shape((CHIPS, ROWS, HEAD_DIM))
    half_state = shape((HALF_ROWS, HEAD_DIM))
    tagged = shape((HALF_ROWS + 16, HEAD_DIM))

    below, above = [send(out_weight, Z_UP)], [send(out_weight, Z_DOWN)]

    log_decay = jnp.transpose(log_decay)
    key_mine, key_cross = pl.pallas_call(
        key_terms_kernel,
        in_specs=[pl.BlockSpec(memory_space=pltpu.VMEM)] + [pl.BlockSpec(memory_space=pltpu.HBM)] * 2,
        out_shape=(tagged, tagged),
        scratch_shapes=[pltpu.VMEM((tokens, cols), BF)] * 2 + [pltpu.SemaphoreType.DMA((2,))],
        compiler_params=pltpu.CompilerParams(vmem_limit_bytes=60 * 1024 * 1024),
        name="key_terms",
        cost_estimate=pl.CostEstimate(flops=40_000_000, bytes_accessed=1_000_000, transcendentals=0),
    )(log_decay, key_proj, value_proj)
    key_other = send(key_cross, CORE)
    merged = call(
        functools.partial(merge_kernel, 0), shape((CHIPS, ROWS + 16, HEAD_DIM)), "merge_keys",
        1_000_000, 500_000, (key_mine, key_other, key_mine, key_other),
    )
    parts = call(
        cotangent_kernel, (shape((2 * share, tokens)),) * 2, "cotangent_parts", 40_000_000_000, 400_000,
        (cotangent,), (below[0], above[0], merged),
    )
    below.append(send(below[0], Z_UP))
    above.append(send(above[0], Z_DOWN))
    pieces = []
    for a in range(2):
        for b in range(2):
            table = pairs(lambda yl, z, c, yh, x, a=a, b=b: (yh, z, c ^ a, yl ^ b, x))
            pieces.append(send(parts[a], table))
    gathered = exchange(merged)

    befores = call(
        functools.partial(recurrence_kernel, False), slices, "states_before", 1_000_000, 1_000_000,
        (gathered, gathered),
    )
    own = call(collect_kernel, shape((2 * share, 4 * tokens)), "collect", 0, 800_000, pieces, (befores,))
    left, right = send(own, X_UP), send(own, X_DOWN)
    before = exchange(befores).reshape(HALF_ROWS, HEAD_DIM)
    before_own, before_cross = call(
        functools.partial(spread_kernel, 0), (half_state, half_state), "spread_before",
        20_000_000_000, 500_000, (key_mine, key_other, key_mine, key_other, before),
    )
    before_other = send(before_cross, CORE)
    attended, scores, states = call(
        attended_kernel, (row, row, shape((cols, HEAD_DIM))), "attended", 110_000_000, 2_000_000,
        (log_decay, queries, key_proj, value_proj, before_own, before_other), (below[1], above[1]),
    )
    below.append(send(below[-1], Z_UP))
    above.append(send(above[-1], Z_DOWN))
    across = send(attended, CORE)
    neighbour = send(attended, Y_LO)
    opposite = send(left, X_UP)
    block, block_t = call(
        functools.partial(assemble_kernel, share),
        (shape((features, 4 * tokens)), shape((4 * tokens, features))), "assemble",
        1_000_000, 5_000_000, (own, left, right, opposite),
    )
    diagonal = send(neighbour, CORE)
    far_low = send(below[2][:half], Z_UP)
    far_high = send(above[2][half:], Z_DOWN)

    weights = [out_weight] + above + [far_low, far_high] + below[::-1]
    kept, theirs, cross, cross_theirs = pl.pallas_call(
        project_kernel,
        out_shape=[row32, row32, row, row],
        scratch_shapes=[pltpu.VMEM((features, cols // TILES), BF)],
        compiler_params=PARAMS,
        name="project",
        cost_estimate=pl.CostEstimate(
            flops=1_600_000_000, bytes_accessed=6_000_000, transcendentals=0
        ),
    )(block_t, *weights)
    from_core_theirs = send(cross_theirs, CORE)
    from_core = send(cross, CORE)
    passed = call(add_kernel, row, "sum_theirs", 100_000, 1_000_000, (theirs, from_core_theirs))
    arrived = send(passed, Y_LO)

    part = pl.pallas_call(
        weight_kernel,
        in_specs=[pl.BlockSpec(memory_space=pltpu.VMEM)] * 6,
        out_shape=[piece] * 4 + [shape((half, cols))] * 2 + [piece] * 3,
        scratch_shapes=[pltpu.VMEM((4 * tokens, cols // TILES), BF)],
        compiler_params=PARAMS,
        name="weight_partial",
        cost_estimate=pl.CostEstimate(
            flops=1_600_000_000, bytes_accessed=6_000_000, transcendentals=0
        ),
    )(block, attended, neighbour, across, diagonal, passed)
    up, down = send(part[4], Z_UP), send(part[5], Z_DOWN)

    grad_attn, query_mine, query_cross = call(
        query_terms_kernel, (row, half_state, half_state), "query_terms", 40_000_000, 1_000_000,
        (log_decay, queries, kept, from_core, arrived),
    )
    up, down = call(
        first_adds_kernel, (piece, piece), "ring_sum_3", 400_000, 2_000_000,
        (part[3], up, part[6], down), (grad_attn,),
    )
    up, down = send(up, Z_UP), send(down, Z_DOWN)
    query_other = send(query_cross, CORE)
    query_merged = call(
        functools.partial(merge_kernel, 1), slices, "merge_queries", 1_000_000, 500_000,
        (key_mine, key_other, query_mine, query_other),
    )
    returned = exchange(query_merged)
    up, down = add_pieces(part[2], up), add_pieces(part[7], down)
    afters = call(
        functools.partial(recurrence_kernel, True), slices, "states_after", 1_000_000, 1_000_000,
        (gathered, returned), (up, down),
    )
    up, down = send(up, Z_UP), send(down, Z_DOWN)
    after = exchange(afters).reshape(HALF_ROWS, HEAD_DIM)
    up, down = add_pieces(part[1], up), add_pieces(part[8], down)
    grad_queries, inner_k, inner_v = call(
        inner_grads_kernel, (row, row32, row32), "inner_grads", 200_000_000, 3_000_000,
        (log_decay, queries, key_proj, value_proj, grad_attn, scores, states), (up, down),
    )
    after_own, after_cross = call(
        functools.partial(spread_kernel, 1), (half_state, half_state), "spread_after",
        25_000_000_000, 500_000, (key_mine, key_other, query_mine, query_other, after), (inner_k,),
    )
    after_other = send(after_cross, CORE)
    up, down = send(up, Z_UP), send(down, Z_DOWN)
    grad_keys, grad_values = call(
        outer_grads_kernel, (row, row), "outer_grads", 70_000_000, 3_000_000,
        (log_decay, key_proj, value_proj, inner_k, inner_v, after_own, after_other),
        scratch=[pltpu.VMEM((cols, HEAD_DIM), BF)],
    )
    grad_weight = call(last_add_kernel, piece, "ring_sum_0", 400_000, 2_000_000, (part[0], up, down))
    return grad_queries, grad_keys, grad_values, grad_weight


def solution(mesh):
    placed = P("seq", "head")
    return jax.shard_map(
        body,
        mesh=mesh,
        in_specs=(placed,) * 6,
        out_specs=(placed,) * 4,
        check_vma=False,
    )
```

```python
import functools

import jax
import jax.numpy as jnp
from jax import lax
from jax.experimental import pallas as pl
from jax.experimental.pallas import tpu as pltpu
from jax.sharding import PartitionSpec as P

HEAD_DIM = 128
BLOCK = 128
HEADS_LOCAL = 8
CHIPS = 16
HALF_ROWS = 512
ROWS = 32
NZ = 8
TILES = 4
BF = jnp.bfloat16
F32 = jnp.float32
AXES = ("seq", "head")
PARAMS = pltpu.CompilerParams(vmem_limit_bytes=16 * 1024 * 1024)


def pairs(move):
    out = []
    for yl in range(2):
        for z in range(8):
            for c in range(2):
                for yh in range(2):
                    for x in range(4):
                        a, b, d, e, f = move(yl, z, c, yh, x)
                        out.append(
                            (
                                (yl * 16 + z * 2 + c) * 8 + yh * 4 + x,
                                (a * 16 + (b % 8) * 2 + d) * 8 + e * 4 + f % 4,
                            )
                        )
    return out


Z_UP = pairs(lambda yl, z, c, yh, x: (yl, z + 1, c, yh, x))
Z_DOWN = pairs(lambda yl, z, c, yh, x: (yl, z + 7, c, yh, x))
X_UP = pairs(lambda yl, z, c, yh, x: (yl, z, c, yh, x + 1))
X_DOWN = pairs(lambda yl, z, c, yh, x: (yl, z, c, yh, x + 3))
CORE = pairs(lambda yl, z, c, yh, x: (yl, z, 1 - c, yh, x))
Y_LO = pairs(lambda yl, z, c, yh, x: (1 - yl, z, c, yh, x))


CHIP_GROUPS = [[2 * p + c for p in range(CHIPS)] for c in range(2)]


def send(array, table):
    return lax.ppermute(array, AXES, table)


def mm(a, b, ca, cb):
    return lax.dot_general(a, b, (((ca,), (cb,)), ((), ())), preferred_element_type=F32)


def coordinates():
    seq, head = lax.axis_index("seq"), lax.axis_index("head")
    y_lo = seq // 16
    rest = seq - 16 * y_lo
    z = rest // 2
    core = rest - 2 * z
    y_hi = head // 4
    return y_lo, z, core, y_hi, head - 4 * y_hi


def flip_bit():
    y_lo, _, _, y_hi, _ = coordinates()
    return y_lo + y_hi - 2 * y_lo * y_hi


def within_columns(decay):
    at = lax.broadcasted_iota(jnp.int32, (BLOCK, BLOCK), 0)
    of = lax.broadcasted_iota(jnp.int32, (BLOCK, BLOCK), 1)
    lower = (of <= at).astype(F32)
    return lax.dot_general(
        lower, decay, (((1,), (1,)), ((), ())),
        precision=lax.Precision.HIGHEST, preferred_element_type=F32,
    )


def causal_mask(within_col):
    gaps = within_col - jnp.transpose(within_col)
    at = lax.broadcasted_iota(jnp.int32, (BLOCK, BLOCK), 0)
    of = lax.broadcasted_iota(jnp.int32, (BLOCK, BLOCK), 1)
    return jnp.exp(jnp.where(at >= of, gaps, -jnp.inf))


def head_cols(h):
    return pl.ds(h * HEAD_DIM, HEAD_DIM)


def cotangent_kernel(cot_ref, *rest):
    same_ref, swap_ref = rest[-2:]
    _, _, core, _, _ = coordinates()
    turned = jnp.transpose(cot_ref[...])
    share = turned.shape[0] // 4
    for i in range(2):
        first = turned[(2 * i) * share : (2 * i + 1) * share]
        second = turned[(2 * i + 1) * share : (2 * i + 2) * share]
        rows = pl.ds(i * share, share)

        @pl.when(core == 0)
        def _():
            same_ref[rows, :] = first
            swap_ref[rows, :] = second

        @pl.when(core == 1)
        def _():
            same_ref[rows, :] = second
            swap_ref[rows, :] = first


def key_terms_kernel(decay_ref, key_hbm, value_hbm, mine_ref, cross_ref, key_ref, value_ref, sems):
    copies = (
        pltpu.make_async_copy(key_hbm, key_ref, sems.at[0]),
        pltpu.make_async_copy(value_hbm, value_ref, sems.at[1]),
    )
    for copy in copies:
        copy.start()
    within = within_columns(decay_ref[...])
    for copy in copies:
        copy.wait()
    _, _, core, _, _ = coordinates()
    row = lax.broadcasted_iota(jnp.int32, (16, HEAD_DIM), 0)
    for half in range(2):
        decays = jnp.zeros((16, HEAD_DIM), F32)
        for i in range(4):
            h = 4 * half + i
            col = within[:, h : h + 1]
            last = col[BLOCK - 1 : BLOCK]
            scaled = (jnp.exp(last - col) * key_ref[:, head_cols(h)].astype(F32)).astype(BF)
            terms = mm(scaled, value_ref[:, head_cols(h)], 0, 0).astype(BF)
            decays = put_parts(decays, row, 3 * i, last)
            store_half(core, half, i, terms, mine_ref, cross_ref)
        decays = decays.astype(BF)
        rows = pl.ds(HALF_ROWS, 16)

        @pl.when(core == half)
        def _():
            mine_ref[rows, :] = decays

        @pl.when(core != half)
        def _():
            cross_ref[rows, :] = decays


def put_parts(decays, row, at, value):
    high = value.astype(BF).astype(F32)
    middle = (value - high).astype(BF).astype(F32)
    low = value - high - middle
    decays = jnp.where(row == at, high, decays)
    decays = jnp.where(row == at + 1, middle, decays)
    return jnp.where(row == at + 2, low, decays)


def add_parts(decays, at):
    return decays[at : at + 1] + (decays[at + 1 : at + 2] + decays[at + 2 : at + 3])


def store_half(core, half, i, value, mine_ref, cross_ref):
    rows = pl.ds(i * HEAD_DIM, HEAD_DIM)

    @pl.when(core == half)
    def _():
        mine_ref[rows, :] = value

    @pl.when(core != half)
    def _():
        cross_ref[rows, :] = value


def merge_kernel(lead, mine_decay_ref, other_decay_ref, mine_ref, other_ref, *rest):
    out_ref = rest[-1]
    _, _, core, _, _ = coordinates()
    row = lax.broadcasted_iota(jnp.int32, (16, HEAD_DIM), 0)
    mine_decays = mine_decay_ref[HALF_ROWS : HALF_ROWS + 16, :].astype(F32)
    other_decays = other_decay_ref[HALF_ROWS : HALF_ROWS + 16, :].astype(F32)
    for j in range(4):
        rows = slice(j * HEAD_DIM, (j + 1) * HEAD_DIM)
        mine_decay, other_decay = add_parts(mine_decays, 3 * j), add_parts(other_decays, 3 * j)
        mine, other = mine_ref[rows, :].astype(F32), other_ref[rows, :].astype(F32)
        is_lead = core == lead
        mine = mine * jnp.where(is_lead, jnp.exp(other_decay), 1.0)
        other = other * jnp.where(is_lead, 1.0, jnp.exp(mine_decay))
        terms = (mine + other).astype(BF)
        for i in range(4):
            out_ref[4 * j + i, 0:ROWS, :] = terms[i * ROWS : (i + 1) * ROWS]
        if out_ref.shape[1] > ROWS:
            parts = put_parts(jnp.zeros((16, HEAD_DIM), F32), row, 0, mine_decay + other_decay)
            parts = parts.astype(BF)
            for i in range(4):
                out_ref[4 * j + i, ROWS : ROWS + 16, :] = parts


def spread_kernel(
    lead, mine_decay_ref, other_decay_ref, mine_ref, other_ref, state_ref, *rest
):
    own_out_ref, cross_out_ref = rest[-2:]
    _, _, core, _, _ = coordinates()
    mine_decays = mine_decay_ref[HALF_ROWS : HALF_ROWS + 16, :].astype(F32)
    other_decays = other_decay_ref[HALF_ROWS : HALF_ROWS + 16, :].astype(F32)
    for j in range(4):
        rows = slice(j * HEAD_DIM, (j + 1) * HEAD_DIM)
        state = state_ref[rows, :]
        wide = state.astype(F32)
        mine_moved = jnp.exp(add_parts(mine_decays, 3 * j)) * wide + mine_ref[rows, :].astype(F32)
        other_moved = jnp.exp(add_parts(other_decays, 3 * j)) * wide + other_ref[rows, :].astype(F32)

        @pl.when(core == lead)
        def _():
            own_out_ref[rows, :] = state
            cross_out_ref[rows, :] = mine_moved.astype(BF)

        @pl.when(core != lead)
        def _():
            own_out_ref[rows, :] = other_moved.astype(BF)
            cross_out_ref[rows, :] = state


def recurrence_kernel(reverse, decay_ref, terms_ref, *rest):
    out_ref = rest[-1]
    state = jnp.zeros((ROWS, HEAD_DIM), F32)
    for k in reversed(range(CHIPS)) if reverse else range(CHIPS):
        out_ref[k] = state.astype(BF)
        factor = jnp.exp(add_parts(decay_ref[k, ROWS : ROWS + 16, :].astype(F32), 0))
        state = factor * state + terms_ref[k, 0:ROWS, :].astype(F32)


def gather_halves(own_ref, other_ref, out_ref):
    _, _, core, _, _ = coordinates()
    out_ref[pl.ds(pl.multiple_of(core * HALF_ROWS, HALF_ROWS), HALF_ROWS), :] = own_ref[...]
    out_ref[pl.ds(pl.multiple_of((1 - core) * HALF_ROWS, HALF_ROWS), HALF_ROWS), :] = other_ref[...]


def attended_kernel(decay_ref, query_ref, key_ref, value_ref, own_ref, other_ref, *rest):
    att_ref, score_ref, state_ref = rest[-3:]
    gather_halves(own_ref, other_ref, state_ref)
    within = within_columns(decay_ref[...])
    for h in range(HEADS_LOCAL):
        cols = head_cols(h)
        col = within[:, h : h + 1]
        query = query_ref[:, cols]
        scores = (mm(query, key_ref[:, cols], 1, 1) * causal_mask(col)).astype(BF)
        score_ref[:, cols] = scores
        att = jnp.exp(col) * mm(query, state_ref[pl.ds(h * HEAD_DIM, HEAD_DIM), :], 1, 0)
        att_ref[:, cols] = (att + mm(scores, value_ref[:, cols], 1, 0)).astype(BF)


def query_terms_kernel(decay_ref, query_ref, own_ref, core_ref, other_ref, *rest):
    grad_ref, mine_ref, cross_ref = rest[-3:]
    _, _, core, _, _ = coordinates()
    within = within_columns(decay_ref[...])
    for h in range(HEADS_LOCAL):
        cols = head_cols(h)
        grad = own_ref[:, cols] + core_ref[:, cols].astype(F32) + other_ref[:, cols].astype(F32)
        grad = grad.astype(BF)
        grad_ref[:, cols] = grad
        scaled = (jnp.exp(within[:, h : h + 1]) * query_ref[:, cols].astype(F32)).astype(BF)
        terms = mm(scaled, grad, 0, 0).astype(BF)
        store_half(core, h // 4, h % 4, terms, mine_ref, cross_ref)


def inner_grads_kernel(
    decay_ref, query_ref, key_ref, value_ref, grad_ref, score_ref, state_ref, *rest
):
    gq_ref, gk_ref, gv_ref = rest[-3:]
    within = within_columns(decay_ref[...])
    for h in range(HEADS_LOCAL):
        cols = head_cols(h)
        col = within[:, h : h + 1]
        grad, key = grad_ref[:, cols], key_ref[:, cols]
        grad_scores = (mm(grad, value_ref[:, cols], 1, 1) * causal_mask(col)).astype(BF)
        state = state_ref[pl.ds(h * HEAD_DIM, HEAD_DIM), :]
        gq = jnp.exp(col) * mm(grad, state, 1, 1) + mm(grad_scores, key, 1, 0)
        gq_ref[:, cols] = gq.astype(BF)
        gk_ref[:, cols] = mm(grad_scores, query_ref[:, cols], 0, 0)
        gv_ref[:, cols] = mm(score_ref[:, cols], grad, 0, 0)


def outer_grads_kernel(
    decay_ref, key_ref, value_ref, inner_k_ref, inner_v_ref, own_ref, other_ref,
    gk_ref, gv_ref, after_ref,
):
    gather_halves(own_ref, other_ref, after_ref)
    within = within_columns(decay_ref[...])
    for h in range(HEADS_LOCAL):
        cols = head_cols(h)
        key_weight = jnp.exp(within[BLOCK - 1 : BLOCK, h : h + 1] - within[:, h : h + 1])
        after = after_ref[pl.ds(h * HEAD_DIM, HEAD_DIM), :]
        gk = key_weight * mm(value_ref[:, cols], after, 1, 1) + inner_k_ref[:, cols]
        gk_ref[:, cols] = gk.astype(BF)
        gv = key_weight * mm(key_ref[:, cols], after, 1, 0) + inner_v_ref[:, cols]
        gv_ref[:, cols] = gv.astype(BF)


def collect_kernel(a_ref, b_ref, c_ref, d_ref, *rest):
    out_ref = rest[-1]
    flip = flip_bit()
    for i, ref in ((flip, a_ref), (1 - flip, b_ref), (2 + flip, c_ref), (3 - flip, d_ref)):
        out_ref[:, pl.ds(pl.multiple_of(i * BLOCK, BLOCK), BLOCK)] = ref[...]


def assemble_kernel(share, own_ref, left_ref, right_ref, opposite_ref, out_ref, out_t_ref):
    _, z, _, _, x = coordinates()
    for off, ref, start, part in (
        (0, own_ref, 0, 0), (0, own_ref, share, 1),
        (1, right_ref, 0, 0), (1, right_ref, share, 1),
        (2, opposite_ref, 0, 0), (2, opposite_ref, share, 1),
        (3, left_ref, 0, 0), (3, left_ref, share, 1),
    ):
        k = (2 * ((x + off) % 4) + part - z + NZ) % NZ
        at = pl.multiple_of(k * share, 64)
        out_ref[pl.ds(at, share), :] = ref[start : start + share, :]
    for i in range(NZ * share // 256):
        rows = pl.ds(i * 256, 256)
        out_t_ref[:, rows] = jnp.transpose(out_ref[rows, :])


def project_kernel(block_ref, *refs):
    pieces, (kept_ref, theirs_ref, cross_ref, cross_theirs_ref), weight_ref = refs[:9], refs[-5:-1], refs[-1]
    width = weight_ref.shape[1]
    for tile in range(kept_ref.shape[1] // width):
        cols = slice(tile * width, (tile + 1) * width)
        at = 0
        for ref in pieces:
            weight_ref[at : at + ref.shape[0], :] = ref[:, cols]
            at += ref.shape[0]
        out = mm(block_ref[...], weight_ref[...], 1, 0)
        kept_ref[:, cols] = out[0:BLOCK]
        theirs_ref[:, cols] = out[BLOCK : 2 * BLOCK]
        cross_ref[:, cols] = out[2 * BLOCK : 3 * BLOCK].astype(BF)
        cross_theirs_ref[:, cols] = out[3 * BLOCK : 4 * BLOCK].astype(BF)


def weight_kernel(block_ref, own_ref, neighbour_ref, across_ref, diagonal_ref, *rest):
    outs, tokens_ref = rest[-10:-1], rest[-1]
    width = tokens_ref.shape[1]
    for tile in range(own_ref.shape[1] // width):
        cols = slice(tile * width, (tile + 1) * width)
        for i, ref in enumerate((own_ref, neighbour_ref, across_ref, diagonal_ref)):
            tokens_ref[i * BLOCK : (i + 1) * BLOCK, :] = ref[:, cols]
        at = 0
        for ref in outs:
            rows = slice(at, at + ref.shape[0])
            ref[:, cols] = mm(block_ref[rows, :], tokens_ref[...], 1, 0).astype(BF)
            at += ref.shape[0]


def add_kernel(a_ref, b_ref, out_ref):
    out_ref[...] = (a_ref[...].astype(F32) + b_ref[...].astype(F32)).astype(BF)


def first_adds_kernel(up_part_ref, up_ref, down_part_ref, down_ref, *rest):
    up_out_ref, down_out_ref = rest[-2:]
    half = up_ref.shape[0]
    up_out_ref[:half] = (up_part_ref[:half].astype(F32) + up_ref[...].astype(F32)).astype(BF)
    up_out_ref[half:] = up_part_ref[half:]
    down_out_ref[:half] = down_part_ref[:half]
    down_out_ref[half:] = (down_part_ref[half:].astype(F32) + down_ref[...].astype(F32)).astype(BF)


def adds_kernel(up_part_ref, up_ref, down_part_ref, down_ref, *rest):
    up_out_ref, down_out_ref = rest[-2:]
    up_out_ref[...] = (up_part_ref[...].astype(F32) + up_ref[...].astype(F32)).astype(BF)
    down_out_ref[...] = (down_part_ref[...].astype(F32) + down_ref[...].astype(F32)).astype(BF)


def last_add_kernel(part_ref, up_ref, down_ref, out_ref):
    out_ref[...] = (
        part_ref[...].astype(F32) + (up_ref[...].astype(F32) + down_ref[...].astype(F32))
    ).astype(BF)


def shape(dims, dtype=BF):
    return jax.ShapeDtypeStruct(dims, dtype)


def call(body, outs, name, flops, moved, args, after=(), scratch=()):
    return pl.pallas_call(
        body,
        in_specs=[pl.BlockSpec(a.shape, lambda n=a.ndim: (0,) * n) for a in args]
        + [pl.BlockSpec(memory_space=pltpu.VMEM)] * len(after),
        out_shape=outs,
        scratch_shapes=list(scratch),
        compiler_params=PARAMS,
        name=name,
        cost_estimate=pl.CostEstimate(flops=flops, bytes_accessed=moved, transcendentals=0),
    )(*args, *after)


def add_pieces(a, b):
    return (a.astype(F32) + b.astype(F32)).astype(BF)


def exchange(array):
    return lax.all_to_all(array, "seq", 0, 0, tiled=True, axis_index_groups=CHIP_GROUPS)


def body(cotangent, queries, key_proj, value_proj, log_decay, out_weight):
    tokens, cols = queries.shape
    share = out_weight.shape[0]
    half = share // 2
    features = NZ * share
    row = shape((tokens, cols))
    row32 = shape((tokens, cols), F32)
    piece = shape((share, cols))
    slices = shape((CHIPS, ROWS, HEAD_DIM))
    half_state = shape((HALF_ROWS, HEAD_DIM))
    tagged = shape((HALF_ROWS + 16, HEAD_DIM))

    below, above = [send(out_weight, Z_UP)], [send(out_weight, Z_DOWN)]

    log_decay = jnp.transpose(log_decay)
    key_mine, key_cross = pl.pallas_call(
        key_terms_kernel,
        in_specs=[pl.BlockSpec(memory_space=pltpu.VMEM)] + [pl.BlockSpec(memory_space=pltpu.HBM)] * 2,
        out_shape=(tagged, tagged),
        scratch_shapes=[pltpu.VMEM((tokens, cols), BF)] * 2 + [pltpu.SemaphoreType.DMA((2,))],
        compiler_params=PARAMS,
        name="key_terms",
        cost_estimate=pl.CostEstimate(flops=40_000_000, bytes_accessed=1_000_000, transcendentals=0),
    )(log_decay, key_proj, value_proj)
    key_other = send(key_cross, CORE)
    merged = call(
        functools.partial(merge_kernel, 0), shape((CHIPS, ROWS + 16, HEAD_DIM)), "merge_keys",
        1_000_000, 500_000, (key_mine, key_other, key_mine, key_other),
    )
    parts = call(
        cotangent_kernel, (shape((2 * share, tokens)),) * 2, "cotangent_parts", 40_000_000_000, 400_000,
        (cotangent,), (below[0], above[0], merged),
    )
    below.append(send(below[0], Z_UP))
    above.append(send(above[0], Z_DOWN))
    pieces = []
    for a in range(2):
        for b in range(2):
            table = pairs(lambda yl, z, c, yh, x, a=a, b=b: (yh, z, c ^ a, yl ^ b, x))
            pieces.append(send(parts[a], table))
    gathered = exchange(merged)

    befores = call(
        functools.partial(recurrence_kernel, False), slices, "states_before", 1_000_000, 1_000_000,
        (gathered, gathered),
    )
    own = call(
        collect_kernel, shape((2 * share, 4 * tokens)), "collect", 0, 800_000, pieces,
        (befores, below[1], above[1]),
    )
    left, right = send(own, X_UP), send(own, X_DOWN)
    below.append(send(below[1], Z_UP))
    above.append(send(above[1], Z_DOWN))
    far_low = send(below[2][:half], Z_UP)
    far_high = send(above[2][half:], Z_DOWN)
    before = exchange(befores).reshape(HALF_ROWS, HEAD_DIM)
    before_own, before_cross = call(
        functools.partial(spread_kernel, 0), (half_state, half_state), "spread_before",
        1_000_000, 500_000, (key_mine, key_other, key_mine, key_other, before), (far_low, far_high, right),
    )
    before_other = send(before_cross, CORE)
    attended, scores, states = call(
        attended_kernel, (row, row, shape((cols, HEAD_DIM))), "attended", 110_000_000, 2_000_000,
        (log_decay, queries, key_proj, value_proj, before_own, before_other),
    )
    across = send(attended, CORE)
    neighbour = send(attended, Y_LO)
    opposite = send(left, X_UP)
    block, block_t = call(
        functools.partial(assemble_kernel, share),
        (shape((features, 4 * tokens)), shape((4 * tokens, features))), "assemble",
        1_000_000, 5_000_000, (own, left, right, opposite),
    )
    diagonal = send(neighbour, CORE)

    weights = [out_weight] + above + [far_low, far_high] + below[::-1]
    kept, theirs, cross, cross_theirs = pl.pallas_call(
        project_kernel,
        out_shape=[row32, row32, row, row],
        scratch_shapes=[pltpu.VMEM((features, cols // TILES), BF)],
        compiler_params=PARAMS,
        name="project",
        cost_estimate=pl.CostEstimate(
            flops=1_600_000_000, bytes_accessed=6_000_000, transcendentals=0
        ),
    )(block_t, *weights)
    from_core_theirs = send(cross_theirs, CORE)
    from_core = send(cross, CORE)
    passed = call(add_kernel, row, "sum_theirs", 100_000, 1_000_000, (theirs, from_core_theirs))
    arrived = send(passed, Y_LO)

    part = pl.pallas_call(
        weight_kernel,
        in_specs=[pl.BlockSpec(memory_space=pltpu.VMEM)] * 6,
        out_shape=[piece] * 4 + [shape((half, cols))] * 2 + [piece] * 3,
        scratch_shapes=[pltpu.VMEM((4 * tokens, cols // TILES), BF)],
        compiler_params=PARAMS,
        name="weight_partial",
        cost_estimate=pl.CostEstimate(
            flops=1_600_000_000, bytes_accessed=6_000_000, transcendentals=0
        ),
    )(block, attended, neighbour, across, diagonal, passed)
    up, down = send(part[4], Z_UP), send(part[5], Z_DOWN)

    grad_attn, query_mine, query_cross = call(
        query_terms_kernel, (row, half_state, half_state), "query_terms", 40_000_000, 1_000_000,
        (log_decay, queries, kept, from_core, arrived),
    )
    up, down = call(
        first_adds_kernel, (piece, piece), "ring_sum_3", 400_000, 2_000_000,
        (part[3], up, part[6], down), (grad_attn,),
    )
    up, down = send(up, Z_UP), send(down, Z_DOWN)
    query_other = send(query_cross, CORE)
    query_merged = call(
        functools.partial(merge_kernel, 1), slices, "merge_queries", 1_000_000, 500_000,
        (key_mine, key_other, query_mine, query_other),
    )
    returned = exchange(query_merged)
    up, down = add_pieces(part[2], up), add_pieces(part[7], down)
    afters = call(
        functools.partial(recurrence_kernel, True), slices, "states_after", 1_000_000, 1_000_000,
        (gathered, returned), (up, down),
    )
    up, down = send(up, Z_UP), send(down, Z_DOWN)
    after = exchange(afters).reshape(HALF_ROWS, HEAD_DIM)
    up, down = add_pieces(part[1], up), add_pieces(part[8], down)
    grad_queries, inner_k, inner_v = call(
        inner_grads_kernel, (row, row32, row32), "inner_grads", 200_000_000, 3_000_000,
        (log_decay, queries, key_proj, value_proj, grad_attn, scores, states), (up, down),
    )
    after_own, after_cross = call(
        functools.partial(spread_kernel, 1), (half_state, half_state), "spread_after",
        25_000_000_000, 500_000, (key_mine, key_other, query_mine, query_other, after), (inner_k,),
    )
    after_other = send(after_cross, CORE)
    up, down = send(up, Z_UP), send(down, Z_DOWN)
    grad_keys, grad_values = call(
        outer_grads_kernel, (row, row), "outer_grads", 70_000_000, 3_000_000,
        (log_decay, key_proj, value_proj, inner_k, inner_v, after_own, after_other),
        scratch=[pltpu.VMEM((cols, HEAD_DIM), BF)],
    )
    grad_weight = call(last_add_kernel, piece, "ring_sum_0", 400_000, 2_000_000, (part[0], up, down))
    return grad_queries, grad_keys, grad_values, grad_weight


def solution(mesh):
    placed = P("seq", "head")
    return jax.shard_map(
        body,
        mesh=mesh,
        in_specs=(placed,) * 6,
        out_specs=(placed,) * 4,
        check_vma=False,
    )
```

```python
import functools

import jax
import jax.numpy as jnp
from jax import lax
from jax.experimental import pallas as pl
from jax.experimental.pallas import tpu as pltpu
from jax.sharding import PartitionSpec as P

HEAD_DIM = 128
BLOCK = 128
HEADS_LOCAL = 8
CHIPS = 16
HALF_ROWS = 512
ROWS = 32
NZ = 8
TILES = 4
BF = jnp.bfloat16
F32 = jnp.float32
AXES = ("seq", "head")
PARAMS = pltpu.CompilerParams(vmem_limit_bytes=16 * 1024 * 1024)


def pairs(move):
    out = []
    for yl in range(2):
        for z in range(8):
            for c in range(2):
                for yh in range(2):
                    for x in range(4):
                        a, b, d, e, f = move(yl, z, c, yh, x)
                        out.append(
                            (
                                (yl * 16 + z * 2 + c) * 8 + yh * 4 + x,
                                (a * 16 + (b % 8) * 2 + d) * 8 + e * 4 + f % 4,
                            )
                        )
    return out


Z_UP = pairs(lambda yl, z, c, yh, x: (yl, z + 1, c, yh, x))
Z_DOWN = pairs(lambda yl, z, c, yh, x: (yl, z + 7, c, yh, x))
X_UP = pairs(lambda yl, z, c, yh, x: (yl, z, c, yh, x + 1))
X_DOWN = pairs(lambda yl, z, c, yh, x: (yl, z, c, yh, x + 3))
CORE = pairs(lambda yl, z, c, yh, x: (yl, z, 1 - c, yh, x))
Y_LO = pairs(lambda yl, z, c, yh, x: (1 - yl, z, c, yh, x))


CHIP_GROUPS = [[2 * p + c for p in range(CHIPS)] for c in range(2)]


def send(array, table):
    return lax.ppermute(array, AXES, table)


def mm(a, b, ca, cb):
    return lax.dot_general(a, b, (((ca,), (cb,)), ((), ())), preferred_element_type=F32)


def coordinates():
    seq, head = lax.axis_index("seq"), lax.axis_index("head")
    y_lo = seq // 16
    rest = seq - 16 * y_lo
    z = rest // 2
    core = rest - 2 * z
    y_hi = head // 4
    return y_lo, z, core, y_hi, head - 4 * y_hi


def flip_bit():
    y_lo, _, _, y_hi, _ = coordinates()
    return y_lo + y_hi - 2 * y_lo * y_hi


def within_columns(decay):
    at = lax.broadcasted_iota(jnp.int32, (BLOCK, BLOCK), 0)
    of = lax.broadcasted_iota(jnp.int32, (BLOCK, BLOCK), 1)
    lower = (of <= at).astype(F32)
    return lax.dot_general(
        lower, decay, (((1,), (1,)), ((), ())),
        precision=lax.Precision.HIGHEST, preferred_element_type=F32,
    )


def causal_mask(within_col):
    gaps = within_col - jnp.transpose(within_col)
    at = lax.broadcasted_iota(jnp.int32, (BLOCK, BLOCK), 0)
    of = lax.broadcasted_iota(jnp.int32, (BLOCK, BLOCK), 1)
    return jnp.exp(jnp.where(at >= of, gaps, -jnp.inf))


def head_cols(h):
    return pl.ds(h * HEAD_DIM, HEAD_DIM)


def cotangent_kernel(cot_ref, *rest):
    same_ref, swap_ref = rest[-2:]
    _, _, core, _, _ = coordinates()
    turned = jnp.transpose(cot_ref[...])
    share = turned.shape[0] // 4
    for i in range(2):
        first = turned[(2 * i) * share : (2 * i + 1) * share]
        second = turned[(2 * i + 1) * share : (2 * i + 2) * share]
        rows = pl.ds(i * share, share)

        @pl.when(core == 0)
        def _():
            same_ref[rows, :] = first
            swap_ref[rows, :] = second

        @pl.when(core == 1)
        def _():
            same_ref[rows, :] = second
            swap_ref[rows, :] = first


def key_terms_kernel(decay_ref, key_hbm, value_hbm, mine_ref, cross_ref, key_ref, value_ref, sems):
    copies = (
        pltpu.make_async_copy(key_hbm, key_ref, sems.at[0]),
        pltpu.make_async_copy(value_hbm, value_ref, sems.at[1]),
    )
    for copy in copies:
        copy.start()
    within = within_columns(decay_ref[...])
    for copy in copies:
        copy.wait()
    _, _, core, _, _ = coordinates()
    row = lax.broadcasted_iota(jnp.int32, (16, HEAD_DIM), 0)
    for half in range(2):
        decays = jnp.zeros((16, HEAD_DIM), F32)
        for i in range(4):
            h = 4 * half + i
            col = within[:, h : h + 1]
            last = col[BLOCK - 1 : BLOCK]
            scaled = (jnp.exp(last - col) * key_ref[:, head_cols(h)].astype(F32)).astype(BF)
            terms = mm(scaled, value_ref[:, head_cols(h)], 0, 0).astype(BF)
            decays = put_parts(decays, row, 3 * i, last)
            store_half(core, half, i, terms, mine_ref, cross_ref)
        decays = decays.astype(BF)
        rows = pl.ds(HALF_ROWS, 16)

        @pl.when(core == half)
        def _():
            mine_ref[rows, :] = decays

        @pl.when(core != half)
        def _():
            cross_ref[rows, :] = decays


def put_parts(decays, row, at, value):
    high = value.astype(BF).astype(F32)
    middle = (value - high).astype(BF).astype(F32)
    low = value - high - middle
    decays = jnp.where(row == at, high, decays)
    decays = jnp.where(row == at + 1, middle, decays)
    return jnp.where(row == at + 2, low, decays)


def add_parts(decays, at):
    return decays[at : at + 1] + (decays[at + 1 : at + 2] + decays[at + 2 : at + 3])


def store_half(core, half, i, value, mine_ref, cross_ref):
    rows = pl.ds(i * HEAD_DIM, HEAD_DIM)

    @pl.when(core == half)
    def _():
        mine_ref[rows, :] = value

    @pl.when(core != half)
    def _():
        cross_ref[rows, :] = value


def merge_kernel(lead, mine_decay_ref, other_decay_ref, mine_ref, other_ref, *rest):
    out_ref = rest[-1]
    _, _, core, _, _ = coordinates()
    row = lax.broadcasted_iota(jnp.int32, (16, HEAD_DIM), 0)
    mine_decays = mine_decay_ref[HALF_ROWS : HALF_ROWS + 16, :].astype(F32)
    other_decays = other_decay_ref[HALF_ROWS : HALF_ROWS + 16, :].astype(F32)
    for j in range(4):
        rows = slice(j * HEAD_DIM, (j + 1) * HEAD_DIM)
        mine_decay, other_decay = add_parts(mine_decays, 3 * j), add_parts(other_decays, 3 * j)
        mine, other = mine_ref[rows, :].astype(F32), other_ref[rows, :].astype(F32)
        is_lead = core == lead
        mine = mine * jnp.where(is_lead, jnp.exp(other_decay), 1.0)
        other = other * jnp.where(is_lead, 1.0, jnp.exp(mine_decay))
        terms = (mine + other).astype(BF)
        for i in range(4):
            out_ref[4 * j + i, 0:ROWS, :] = terms[i * ROWS : (i + 1) * ROWS]
        if out_ref.shape[1] > ROWS:
            parts = put_parts(jnp.zeros((16, HEAD_DIM), F32), row, 0, mine_decay + other_decay)
            parts = parts.astype(BF)
            for i in range(4):
                out_ref[4 * j + i, ROWS : ROWS + 16, :] = parts


def spread_kernel(
    lead, mine_decay_ref, other_decay_ref, mine_ref, other_ref, state_ref, *rest
):
    own_out_ref, cross_out_ref = rest[-2:]
    _, _, core, _, _ = coordinates()
    mine_decays = mine_decay_ref[HALF_ROWS : HALF_ROWS + 16, :].astype(F32)
    other_decays = other_decay_ref[HALF_ROWS : HALF_ROWS + 16, :].astype(F32)
    for j in range(4):
        rows = slice(j * HEAD_DIM, (j + 1) * HEAD_DIM)
        state = state_ref[rows, :]
        wide = state.astype(F32)
        mine_moved = jnp.exp(add_parts(mine_decays, 3 * j)) * wide + mine_ref[rows, :].astype(F32)
        other_moved = jnp.exp(add_parts(other_decays, 3 * j)) * wide + other_ref[rows, :].astype(F32)

        @pl.when(core == lead)
        def _():
            own_out_ref[rows, :] = state
            cross_out_ref[rows, :] = mine_moved.astype(BF)

        @pl.when(core != lead)
        def _():
            own_out_ref[rows, :] = other_moved.astype(BF)
            cross_out_ref[rows, :] = state


def recurrence_kernel(reverse, decay_ref, terms_ref, *rest):
    out_ref = rest[-1]
    state = jnp.zeros((ROWS, HEAD_DIM), F32)
    for k in reversed(range(CHIPS)) if reverse else range(CHIPS):
        out_ref[k] = state.astype(BF)
        factor = jnp.exp(add_parts(decay_ref[k, ROWS : ROWS + 16, :].astype(F32), 0))
        state = factor * state + terms_ref[k, 0:ROWS, :].astype(F32)


def gather_halves(own_ref, other_ref, out_ref):
    _, _, core, _, _ = coordinates()
    out_ref[pl.ds(pl.multiple_of(core * HALF_ROWS, HALF_ROWS), HALF_ROWS), :] = own_ref[...]
    out_ref[pl.ds(pl.multiple_of((1 - core) * HALF_ROWS, HALF_ROWS), HALF_ROWS), :] = other_ref[...]


def attended_kernel(decay_ref, query_ref, key_ref, value_ref, own_ref, other_ref, *rest):
    att_ref, score_ref, state_ref = rest[-3:]
    gather_halves(own_ref, other_ref, state_ref)
    within = within_columns(decay_ref[...])
    for h in range(HEADS_LOCAL):
        cols = head_cols(h)
        col = within[:, h : h + 1]
        query = query_ref[:, cols]
        scores = (mm(query, key_ref[:, cols], 1, 1) * causal_mask(col)).astype(BF)
        score_ref[:, cols] = scores
        att = jnp.exp(col) * mm(query, state_ref[pl.ds(h * HEAD_DIM, HEAD_DIM), :], 1, 0)
        att_ref[:, cols] = (att + mm(scores, value_ref[:, cols], 1, 0)).astype(BF)


def query_terms_kernel(decay_ref, query_ref, own_ref, core_ref, other_ref, *rest):
    grad_ref, mine_ref, cross_ref = rest[-3:]
    _, _, core, _, _ = coordinates()
    within = within_columns(decay_ref[...])
    for h in range(HEADS_LOCAL):
        cols = head_cols(h)
        grad = own_ref[:, cols] + core_ref[:, cols].astype(F32) + other_ref[:, cols].astype(F32)
        grad = grad.astype(BF)
        grad_ref[:, cols] = grad
        scaled = (jnp.exp(within[:, h : h + 1]) * query_ref[:, cols].astype(F32)).astype(BF)
        terms = mm(scaled, grad, 0, 0).astype(BF)
        store_half(core, h // 4, h % 4, terms, mine_ref, cross_ref)


def inner_grads_kernel(
    decay_ref, query_ref, key_ref, value_ref, grad_ref, score_ref, state_ref, *rest
):
    gq_ref, gk_ref, gv_ref = rest[-3:]
    within = within_columns(decay_ref[...])
    for h in range(HEADS_LOCAL):
        cols = head_cols(h)
        col = within[:, h : h + 1]
        grad, key = grad_ref[:, cols], key_ref[:, cols]
        grad_scores = (mm(grad, value_ref[:, cols], 1, 1) * causal_mask(col)).astype(BF)
        state = state_ref[pl.ds(h * HEAD_DIM, HEAD_DIM), :]
        gq = jnp.exp(col) * mm(grad, state, 1, 1) + mm(grad_scores, key, 1, 0)
        gq_ref[:, cols] = gq.astype(BF)
        gk_ref[:, cols] = mm(grad_scores, query_ref[:, cols], 0, 0)
        gv_ref[:, cols] = mm(score_ref[:, cols], grad, 0, 0)


def outer_grads_kernel(
    decay_ref, key_ref, value_ref, inner_k_ref, inner_v_ref, own_ref, other_ref,
    gk_ref, gv_ref, after_ref,
):
    gather_halves(own_ref, other_ref, after_ref)
    within = within_columns(decay_ref[...])
    for h in range(HEADS_LOCAL):
        cols = head_cols(h)
        key_weight = jnp.exp(within[BLOCK - 1 : BLOCK, h : h + 1] - within[:, h : h + 1])
        after = after_ref[pl.ds(h * HEAD_DIM, HEAD_DIM), :]
        gk = key_weight * mm(value_ref[:, cols], after, 1, 1) + inner_k_ref[:, cols]
        gk_ref[:, cols] = gk.astype(BF)
        gv = key_weight * mm(key_ref[:, cols], after, 1, 0) + inner_v_ref[:, cols]
        gv_ref[:, cols] = gv.astype(BF)


def collect_kernel(a_ref, b_ref, c_ref, d_ref, *rest):
    out_ref = rest[-1]
    flip = flip_bit()
    for i, ref in ((flip, a_ref), (1 - flip, b_ref), (2 + flip, c_ref), (3 - flip, d_ref)):
        out_ref[:, pl.ds(pl.multiple_of(i * BLOCK, BLOCK), BLOCK)] = ref[...]


def assemble_kernel(share, own_ref, left_ref, right_ref, opposite_ref, out_ref, out_t_ref):
    _, z, _, _, x = coordinates()
    for off, ref, start, part in (
        (0, own_ref, 0, 0), (0, own_ref, share, 1),
        (1, right_ref, 0, 0), (1, right_ref, share, 1),
        (2, opposite_ref, 0, 0), (2, opposite_ref, share, 1),
        (3, left_ref, 0, 0), (3, left_ref, share, 1),
    ):
        k = (2 * ((x + off) % 4) + part - z + NZ) % NZ
        at = pl.multiple_of(k * share, 64)
        out_ref[pl.ds(at, share), :] = ref[start : start + share, :]
    for i in range(NZ * share // 256):
        rows = pl.ds(i * 256, 256)
        out_t_ref[:, rows] = jnp.transpose(out_ref[rows, :])


def project_kernel(block_ref, *refs):
    pieces, (kept_ref, theirs_ref, cross_ref, cross_theirs_ref), weight_ref = refs[:9], refs[-5:-1], refs[-1]
    width = weight_ref.shape[1]
    for tile in range(kept_ref.shape[1] // width):
        cols = slice(tile * width, (tile + 1) * width)
        at = 0
        for ref in pieces:
            weight_ref[at : at + ref.shape[0], :] = ref[:, cols]
            at += ref.shape[0]
        out = mm(block_ref[...], weight_ref[...], 1, 0)
        kept_ref[:, cols] = out[0:BLOCK]
        theirs_ref[:, cols] = out[BLOCK : 2 * BLOCK]
        cross_ref[:, cols] = out[2 * BLOCK : 3 * BLOCK].astype(BF)
        cross_theirs_ref[:, cols] = out[3 * BLOCK : 4 * BLOCK].astype(BF)


def weight_kernel(block_ref, own_ref, neighbour_ref, across_ref, diagonal_ref, *rest):
    outs, tokens_ref = rest[-10:-1], rest[-1]
    width = tokens_ref.shape[1]
    for tile in range(own_ref.shape[1] // width):
        cols = slice(tile * width, (tile + 1) * width)
        for i, ref in enumerate((own_ref, neighbour_ref, across_ref, diagonal_ref)):
            tokens_ref[i * BLOCK : (i + 1) * BLOCK, :] = ref[:, cols]
        at = 0
        for ref in outs:
            rows = slice(at, at + ref.shape[0])
            ref[:, cols] = mm(block_ref[rows, :], tokens_ref[...], 1, 0).astype(BF)
            at += ref.shape[0]


def add_kernel(a_ref, b_ref, out_ref):
    out_ref[...] = (a_ref[...].astype(F32) + b_ref[...].astype(F32)).astype(BF)


def first_adds_kernel(up_part_ref, up_ref, down_part_ref, down_ref, *rest):
    up_out_ref, down_out_ref = rest[-2:]
    half = up_ref.shape[0]
    up_out_ref[:half] = (up_part_ref[:half].astype(F32) + up_ref[...].astype(F32)).astype(BF)
    up_out_ref[half:] = up_part_ref[half:]
    down_out_ref[:half] = down_part_ref[:half]
    down_out_ref[half:] = (down_part_ref[half:].astype(F32) + down_ref[...].astype(F32)).astype(BF)


def adds_kernel(up_part_ref, up_ref, down_part_ref, down_ref, *rest):
    up_out_ref, down_out_ref = rest[-2:]
    up_out_ref[...] = (up_part_ref[...].astype(F32) + up_ref[...].astype(F32)).astype(BF)
    down_out_ref[...] = (down_part_ref[...].astype(F32) + down_ref[...].astype(F32)).astype(BF)


def last_add_kernel(part_ref, up_ref, down_ref, out_ref):
    out_ref[...] = (
        part_ref[...].astype(F32) + (up_ref[...].astype(F32) + down_ref[...].astype(F32))
    ).astype(BF)


def shape(dims, dtype=BF):
    return jax.ShapeDtypeStruct(dims, dtype)


def call(body, outs, name, flops, moved, args, after=(), scratch=()):
    return pl.pallas_call(
        body,
        in_specs=[pl.BlockSpec(a.shape, lambda n=a.ndim: (0,) * n) for a in args]
        + [pl.BlockSpec(memory_space=pltpu.VMEM)] * len(after),
        out_shape=outs,
        scratch_shapes=list(scratch),
        compiler_params=PARAMS,
        name=name,
        cost_estimate=pl.CostEstimate(flops=flops, bytes_accessed=moved, transcendentals=0),
    )(*args, *after)


def add_pieces(a, b):
    return (a.astype(F32) + b.astype(F32)).astype(BF)


def exchange(array):
    return lax.all_to_all(array, "seq", 0, 0, tiled=True, axis_index_groups=CHIP_GROUPS)


def body(cotangent, queries, key_proj, value_proj, log_decay, out_weight):
    tokens, cols = queries.shape
    share = out_weight.shape[0]
    half = share // 2
    features = NZ * share
    row = shape((tokens, cols))
    row32 = shape((tokens, cols), F32)
    piece = shape((share, cols))
    slices = shape((CHIPS, ROWS, HEAD_DIM))
    half_state = shape((HALF_ROWS, HEAD_DIM))
    tagged = shape((HALF_ROWS + 16, HEAD_DIM))

    below, above = [send(out_weight, Z_UP)], [send(out_weight, Z_DOWN)]

    log_decay = jnp.transpose(log_decay)
    key_mine, key_cross = pl.pallas_call(
        key_terms_kernel,
        in_specs=[pl.BlockSpec(memory_space=pltpu.VMEM)] + [pl.BlockSpec(memory_space=pltpu.HBM)] * 2,
        out_shape=(tagged, tagged),
        scratch_shapes=[pltpu.VMEM((tokens, cols), BF)] * 2 + [pltpu.SemaphoreType.DMA((2,))],
        compiler_params=PARAMS,
        name="key_terms",
        cost_estimate=pl.CostEstimate(flops=40_000_000, bytes_accessed=1_000_000, transcendentals=0),
    )(log_decay, key_proj, value_proj)
    key_other = send(key_cross, CORE)
    merged = call(
        functools.partial(merge_kernel, 0), shape((CHIPS, ROWS + 16, HEAD_DIM)), "merge_keys",
        1_000_000, 500_000, (key_mine, key_other, key_mine, key_other),
    )
    parts = call(
        cotangent_kernel, (shape((2 * share, tokens)),) * 2, "cotangent_parts", 40_000_000_000, 400_000,
        (cotangent,), (below[0], above[0], merged),
    )
    below.append(send(below[0], Z_UP))
    above.append(send(above[0], Z_DOWN))
    pieces = []
    for a in range(2):
        for b in range(2):
            table = pairs(lambda yl, z, c, yh, x, a=a, b=b: (yh, z, c ^ a, yl ^ b, x))
            pieces.append(send(parts[a], table))
    gathered = exchange(merged)

    befores = call(
        functools.partial(recurrence_kernel, False), slices, "states_before", 1_000_000, 1_000_000,
        (gathered, gathered),
    )
    own = call(collect_kernel, shape((2 * share, 4 * tokens)), "collect", 0, 800_000, pieces, (befores,))
    left, right = send(own, X_UP), send(own, X_DOWN)
    before = exchange(befores).reshape(HALF_ROWS, HEAD_DIM)
    before_own, before_cross = call(
        functools.partial(spread_kernel, 0), (half_state, half_state), "spread_before",
        20_000_000_000, 500_000, (key_mine, key_other, key_mine, key_other, before),
    )
    before_other = send(before_cross, CORE)
    attended, scores, states = call(
        attended_kernel, (row, row, shape((cols, HEAD_DIM))), "attended", 110_000_000, 2_000_000,
        (log_decay, queries, key_proj, value_proj, before_own, before_other), (below[1], above[1]),
    )
    below.append(send(below[-1], Z_UP))
    above.append(send(above[-1], Z_DOWN))
    across = send(attended, CORE)
    neighbour = send(attended, Y_LO)
    opposite = send(left, X_UP)
    block, block_t = call(
        functools.partial(assemble_kernel, share),
        (shape((features, 4 * tokens)), shape((4 * tokens, features))), "assemble",
        1_000_000, 5_000_000, (own, left, right, opposite),
    )
    diagonal = send(neighbour, CORE)
    far_low = send(below[2][:half], Z_UP)
    far_high = send(above[2][half:], Z_DOWN)

    weights = [out_weight] + above + [far_low, far_high] + below[::-1]
    kept, theirs, cross, cross_theirs = pl.pallas_call(
        project_kernel,
        out_shape=[row32, row32, row, row],
        scratch_shapes=[pltpu.VMEM((features, cols // TILES), BF)],
        compiler_params=PARAMS,
        name="project",
        cost_estimate=pl.CostEstimate(
            flops=1_600_000_000, bytes_accessed=6_000_000, transcendentals=0
        ),
    )(block_t, *weights)
    from_core_theirs = send(cross_theirs, CORE)
    from_core = send(cross, CORE)
    passed = call(add_kernel, row, "sum_theirs", 100_000, 1_000_000, (theirs, from_core_theirs))
    arrived = send(passed, Y_LO)

    part = pl.pallas_call(
        weight_kernel,
        in_specs=[pl.BlockSpec(memory_space=pltpu.VMEM)] * 6,
        out_shape=[piece] * 4 + [shape((half, cols))] * 2 + [piece] * 3,
        scratch_shapes=[pltpu.VMEM((4 * tokens, cols // TILES), BF)],
        compiler_params=PARAMS,
        name="weight_partial",
        cost_estimate=pl.CostEstimate(
            flops=1_600_000_000, bytes_accessed=6_000_000, transcendentals=0
        ),
    )(block, attended, neighbour, across, diagonal, passed)
    up, down = send(part[4], Z_UP), send(part[5], Z_DOWN)

    grad_attn, query_mine, query_cross = call(
        query_terms_kernel, (row, half_state, half_state), "query_terms", 40_000_000, 1_000_000,
        (log_decay, queries, kept, from_core, arrived),
    )
    up, down = call(
        first_adds_kernel, (piece, piece), "ring_sum_3", 400_000, 2_000_000,
        (part[3], up, part[6], down), (grad_attn,),
    )
    up, down = send(up, Z_UP), send(down, Z_DOWN)
    query_other = send(query_cross, CORE)
    query_merged = call(
        functools.partial(merge_kernel, 1), slices, "merge_queries", 1_000_000, 500_000,
        (key_mine, key_other, query_mine, query_other),
    )
    returned = exchange(query_merged)
    up, down = add_pieces(part[2], up), add_pieces(part[7], down)
    afters = call(
        functools.partial(recurrence_kernel, True), slices, "states_after", 1_000_000, 1_000_000,
        (gathered, returned), (up, down),
    )
    up, down = send(up, Z_UP), send(down, Z_DOWN)
    after = exchange(afters).reshape(HALF_ROWS, HEAD_DIM)
    up, down = add_pieces(part[1], up), add_pieces(part[8], down)
    grad_queries, inner_k, inner_v = call(
        inner_grads_kernel, (row, row32, row32), "inner_grads", 200_000_000, 3_000_000,
        (log_decay, queries, key_proj, value_proj, grad_attn, scores, states), (up, down),
    )
    after_own, after_cross = call(
        functools.partial(spread_kernel, 1), (half_state, half_state), "spread_after",
        25_000_000_000, 500_000, (key_mine, key_other, query_mine, query_other, after), (inner_k,),
    )
    after_other = send(after_cross, CORE)
    up, down = send(up, Z_UP), send(down, Z_DOWN)
    grad_keys, grad_values = call(
        outer_grads_kernel, (row, row), "outer_grads", 70_000_000, 3_000_000,
        (log_decay, key_proj, value_proj, inner_k, inner_v, after_own, after_other),
        scratch=[pltpu.VMEM((cols, HEAD_DIM), BF)],
    )
    grad_weight = (part[0].astype(F32) + (up.astype(F32) + down.astype(F32))).astype(BF)
    return grad_queries, grad_keys, grad_values, grad_weight


def solution(mesh):
    placed = P("seq", "head")
    return jax.shard_map(
        body,
        mesh=mesh,
        in_specs=(placed,) * 6,
        out_specs=(placed,) * 4,
        check_vma=False,
    )
```
